32 devices in a mesh: rep: 8 (over z, core), seq: 4 (over y, x).
Axes of the slice: x: 2, y: 2, z: 4, core: 2. Of those that a mesh axis runs over, the one named last changes fastest.
Arguments:
- tokens: bfloat16 [8, 2048, 1024], P('rep', 'seq'), may hold values from -6 to 6
- mixer_gain: bfloat16 [1024], P('seq'), may hold values from 0.5 to 1.5
- query_weight: bfloat16 [1024, 512], P('seq'), may hold values from -0.1875 to 0.1875
- key_weight: bfloat16 [1024, 512], P('seq'), may hold values from -0.1875 to 0.1875
- value_weight: bfloat16 [1024, 1024], P('seq'), may hold values from -0.1875 to 0.1875
- decay_down: bfloat16 [1024, 16], P('seq'), may hold values from -0.1875 to 0.1875
- decay_up: bfloat16 [16, 512], P(None, 'seq'), may hold values from -1.5 to 1.5
- decay_bias: bfloat16 [512], P('seq'), may hold values from 0 to 6
- outgate_weight: bfloat16 [1024, 1024], P('seq'), may hold values from -0.1875 to 0.1875
- head_gain: bfloat16 [256], P('seq'), may hold values from 0.5 to 1.5
- output_weight: bfloat16 [1024, 1024], P('seq'), may hold values from -0.25 to 0.25
- channel_gain: bfloat16 [1024], P('seq'), may hold values from 0.5 to 1.5
- gate_weight: bfloat16 [1024, 2816], P('seq'), may hold values from -0.1875 to 0.1875
- up_weight: bfloat16 [1024, 2816], P('seq'), may hold values from -0.1875 to 0.1875
- down_weight: bfloat16 [2816, 1024], P('seq'), may hold values from -0.21875 to 0.21875
- cotangent: bfloat16 [8, 2048, 1024], P('rep', 'seq'), may hold values from -6 to 6
Outputs:
- block_out: bfloat16 [8, 2048, 1024], P('rep', 'seq')
- tokens_grad: float32 [8, 2048, 1024], P('rep', 'seq')
- mixer_gain_grad: float32 [1024], P('seq')
- query_weight_grad: float32 [1024, 512], P('seq')
- key_weight_grad: float32 [1024, 512], P('seq')
- value_weight_grad: float32 [1024, 1024], P('seq')
- decay_down_grad: float32 [1024, 16], P('seq')
- decay_up_grad: float32 [16, 512], P(None, 'seq')
- decay_bias_grad: float32 [512], P('seq')
- outgate_weight_grad: float32 [1024, 1024], P('seq')
- head_gain_grad: float32 [256], P('seq')
- output_weight_grad: float32 [1024, 1024], P('seq')
- channel_gain_grad: float32 [1024], P('seq')
- gate_weight_grad: float32 [1024, 2816], P('seq')
- up_weight_grad: float32 [1024, 2816], P('seq')
- down_weight_grad: float32 [2816, 1024], P('seq')
The draws below stay inside these ranges and needn't reach their ends.
All inputs are finite; a program needn't handle non-finite values.
Results may differ from the reference program's by a relative error of at most 0.018.
Values may be sent and summed in bfloat16 or wider, within the bound.
No kernel may reach another device: no remote copies, remote signals or barrier semaphores. Data moves between devices by JAX's collectives and lax.ppermute only.
A program may use at most 320 MiB of HBM per device.

```python
import math
import jax
import jax.numpy as jnp
from jax import lax

D = 1024
HEADS = 4
DK = 128
DV = 256
FF = 2816
RANK = 16
SPAN = 64
SEQ_LEN = 2048
SEQUENCES = 8


def levels(stream_key, extent, cuts, smallest, high):
    level = 1.0
    for position, parts in cuts:
        steps = jax.random.uniform(jax.random.fold_in(jax.random.fold_in(stream_key, 6), position), (parts,), jnp.float32, smallest / len(cuts), high / len(cuts))
        level = level * jnp.repeat(jnp.exp(steps), extent[position] // parts).reshape((-1,) + (1,) * (len(extent) - 1 - position))
    return level


def scatter_about(own_key, dims, spread, limit, cuts=(), held_as=jnp.bfloat16):
    loudness = levels(own_key, dims, cuts, -0.22, 0.18) if cuts else 1.0
    values = jax.random.normal(own_key, dims, jnp.float32) * spread * loudness
    return jnp.minimum(jnp.maximum(values, -limit), limit).astype(held_as)


def setup_inputs(seed: int = 0) -> dict:
    arg_keys = jax.random.split(jax.random.key(seed), 17)
    tokens = scatter_about(arg_keys[0], (SEQUENCES, SEQ_LEN, D), 1.0, 6.0, ((0, 8), (1, 4)))
    mixer_gain = jnp.clip(1.0 + 0.1 * jax.random.normal(arg_keys[1], (D,), jnp.float32), 0.5, 1.5).astype(jnp.bfloat16)
    query_weight = scatter_about(arg_keys[2], (D, HEADS * DK), D ** -0.5, 0.1875, ((0, 4),))
    key_weight = scatter_about(arg_keys[3], (D, HEADS * DK), D ** -0.5, 0.1875, ((0, 4),))
    value_weight = scatter_about(arg_keys[4], (D, HEADS * DV), D ** -0.5, 0.1875, ((0, 4),))
    decay_down = scatter_about(arg_keys[5], (D, RANK), D ** -0.5, 0.1875, ((0, 4),))
    decay_up = scatter_about(arg_keys[6], (RANK, HEADS * DK), RANK ** -0.5, 1.5, ((1, 4),))
    decay_bias = jnp.clip(6.0 * jax.random.uniform(arg_keys[7], (HEADS * DK,), jnp.float32) ** levels(arg_keys[7], (HEADS * DK,), ((0, 4),), -0.2, 0.2), 0.0, 6.0).astype(jnp.bfloat16)
    outgate_weight = scatter_about(arg_keys[8], (D, HEADS * DV), D ** -0.5, 0.1875, ((0, 4),))
    head_gain = jnp.clip(1.0 + 0.1 * jax.random.normal(arg_keys[9], (DV,), jnp.float32), 0.5, 1.5).astype(jnp.bfloat16)
    output_weight = scatter_about(arg_keys[10], (HEADS * DV, D), (HEADS * DV // 2) ** -0.5, 0.25, ((0, 4),))
    channel_gain = jnp.clip(1.0 + 0.1 * jax.random.normal(arg_keys[11], (D,), jnp.float32), 0.5, 1.5).astype(jnp.bfloat16)
    gate_weight = scatter_about(arg_keys[12], (D, FF), D ** -0.5, 0.1875, ((0, 4),))
    up_weight = scatter_about(arg_keys[13], (D, FF), D ** -0.5, 0.1875, ((0, 4),))
    down_weight = scatter_about(arg_keys[14], (FF, D), (FF // 4) ** -0.5, 0.21875, ((0, 4),))
    cotangent = scatter_about(arg_keys[15], (SEQUENCES, SEQ_LEN, D), 1.0, 6.0, ((0, 8), (1, 4)))
    return {"tokens": tokens, "mixer_gain": mixer_gain, "query_weight": query_weight, "key_weight": key_weight, "value_weight": value_weight, "decay_down": decay_down, "decay_up": decay_up, "decay_bias": decay_bias, "outgate_weight": outgate_weight, "head_gain": head_gain, "output_weight": output_weight, "channel_gain": channel_gain, "gate_weight": gate_weight, "up_weight": up_weight, "down_weight": down_weight, "cotangent": cotangent}


epsilon = 1e-06
normalizer = 16.0
highest_precision = lax.Precision.HIGHEST

@jax.custom_vjp
def low(v):
    return lax.optimization_barrier(v.astype(jnp.bfloat16)).astype(jnp.float32)

@jax.custom_vjp
def low_back(v):
    return v

def low_keep(v):
    return (low(v), None)

def low_pass(kept, grad):
    return (grad,)

def back_keep(v):
    return (v, None)

def back_low(kept, grad):
    return (low(grad),)
low.defvjp(low_keep, low_pass)
low_back.defvjp(back_keep, back_low)

def normalize(values_in):
    return values_in * lax.rsqrt(lax.optimization_barrier(jnp.mean(values_in * values_in, axis=-1, keepdims=True)) + epsilon)

def span_math(carried, pieces):
    queries, keys_in, values_in, gates = pieces
    length = queries.shape[1]
    cumul = jnp.cumsum(gates, axis=1)
    finish = cumul[:, -1]
    inter = jnp.einsum('bchk,bhkv->bchv', queries * jnp.exp(cumul), carried, precision=highest_precision)
    lower = jnp.arange(length)[:, None] >= jnp.arange(length)[None, :]
    differ = cumul[:, :, None] - cumul[:, None, :]
    pairwise = jnp.exp(jnp.where(lower[None, :, :, None, None], differ, -1e+30))
    scores = jnp.einsum('bihk,bjhk,bijhk->bijh', queries, keys_in, pairwise, precision=highest_precision)
    intra = jnp.einsum('bijh,bjhv->bihv', scores, values_in, precision=highest_precision)
    update = carried * jnp.exp(finish)[..., None] + jnp.einsum('bjhk,bjhv->bhkv', keys_in * jnp.exp(finish[:, None] - cumul), values_in, precision=highest_precision)
    return (update, inter + intra)

def linear_attention(queries, keys_in, values_in, gates):
    number, length = (queries.shape[0], queries.shape[1])
    blocks = length // SPAN

    def split(array):
        return jnp.moveaxis(array.reshape((number, blocks, SPAN) + array.shape[2:]), 1, 0)
    start = jnp.zeros((number, HEADS, DK, DV), jnp.float32)
    final, outputs = lax.scan(jax.checkpoint(span_math), start, (split(queries), split(keys_in), split(values_in), split(gates)))
    return jnp.moveaxis(outputs, 0, 1).reshape(number, length, HEADS, DV)

def layer(params, inputs):
    mixer_gain, query_weight, key_weight, value_weight, decay_down, decay_up, decay_bias, outgate_weight, head_gain, output_weight, channel_gain, gate_weight, up_weight, down_weight = params
    number, length = (inputs.shape[0], inputs.shape[1])

    def project(left, right):
        return jnp.einsum('bld,df->blf', left, right, precision=highest_precision)

    def split_heads(array, size):
        return array.reshape(number, length, HEADS, size)
    normed_one = low(normalize(inputs) * mixer_gain)
    queries = low_back(project(normed_one, query_weight))
    keys_all = low_back(project(normed_one, key_weight))
    values_all = low_back(project(normed_one, value_weight))
    low_rank = low_back(project(normed_one, decay_down))
    outgate = low_back(project(normed_one, outgate_weight))
    gates = jax.nn.log_sigmoid(project(low_rank, decay_up) + decay_bias) / normalizer
    attention_result = linear_attention(split_heads(queries, DK) * DK ** (-0.5), split_heads(keys_all, DK), split_heads(values_all, DV), split_heads(gates, DK))
    mixed = low((normalize(attention_result) * head_gain).reshape(number, length, HEADS * DV) * jax.nn.silu(outgate))
    resid = inputs + low_back(project(mixed, output_weight))
    normed_two = low(normalize(resid) * channel_gain)
    hidden = low(jax.nn.silu(low_back(project(normed_two, gate_weight))) * low_back(project(normed_two, up_weight)))
    return resid + low_back(project(hidden, down_weight))

def reference(tokens, mixer_gain, query_weight, key_weight, value_weight, decay_down, decay_up, decay_bias, outgate_weight, head_gain, output_weight, channel_gain, gate_weight, up_weight, down_weight, cotangent):
    params = tuple((weight.astype(jnp.float32) for weight in (mixer_gain, query_weight, key_weight, value_weight, decay_down, decay_up, decay_bias, outgate_weight, head_gain, output_weight, channel_gain, gate_weight, up_weight, down_weight)))
    batch = math.gcd(SEQUENCES, max(1, 4096 // SEQ_LEN))
    inputs = tokens.astype(jnp.float32).reshape(SEQUENCES // batch, batch, SEQ_LEN, D)
    grads_in = cotangent.astype(jnp.float32).reshape(SEQUENCES // batch, batch, SEQ_LEN, D)

    def advance(totals, item):
        block_in, block_grad = item
        result, pullback = jax.vjp(layer, params, block_in)
        param_grads, input_grad = pullback(block_grad)
        summed = tuple((total + added for total, added in zip(totals, param_grads)))
        return (summed, (result.astype(jnp.bfloat16), input_grad))
    zeros = tuple((jnp.zeros_like(weight) for weight in params))
    totals, (outputs, input_grads) = lax.scan(advance, zeros, (inputs, grads_in))
    return (outputs.reshape(SEQUENCES, SEQ_LEN, D), input_grads.reshape(SEQUENCES, SEQ_LEN, D), totals[0], totals[1], totals[2], totals[3], totals[4], totals[5], totals[6], totals[7], totals[8], totals[9], totals[10], totals[11], totals[12], totals[13])
```

```python
import functools

import jax
import jax.numpy as jnp
from jax import lax
from jax.experimental import pallas as pl
from jax.experimental.pallas import tpu as pltpu
from jax.sharding import PartitionSpec as P

HEADS = 4
DK = 128
DV = 256
CHUNK = 128
SAFE = 60.0


epsilon = 1e-06
normalizer = 16.0
highest_precision = lax.Precision.HIGHEST


def normalize(values_in):
    return values_in * lax.rsqrt(jnp.mean(values_in * values_in, axis=-1, keepdims=True) + epsilon)


def dot_nn(left, right):
    return lax.dot_general(left, right, (((1,), (0,)), ((), ())), preferred_element_type=jnp.float32)


def dot_nt(left, right):
    return lax.dot_general(left, right, (((1,), (1,)), ((), ())), preferred_element_type=jnp.float32)


def dot_tn(left, right):
    return lax.dot_general(left, right, (((0,), (0,)), ((), ())), preferred_element_type=jnp.float32)


def low(array):
    return array.astype(jnp.bfloat16)


def exact_sum(selector, array):
    high = low(array)
    rest = low(array - high.astype(jnp.float32))
    return dot_nn(selector, high) + dot_nn(selector, rest)


def halves(array):
    high = low(array)
    return high, low(array - high.astype(jnp.float32))


def close_dot(dot, left, right):
    (left_high, left_rest), (right_high, right_rest) = halves(left), halves(right)
    return dot(left_high, right_high) + (dot(left_high, right_rest) + dot(left_rest, right_high))


def positions(chunk):
    row = lax.broadcasted_iota(jnp.int32, (chunk, chunk), 0)
    column = lax.broadcasted_iota(jnp.int32, (chunk, chunk), 1)
    return row, column


def as_selector(mask):
    return low(jnp.where(mask, 1.0, 0.0))


def halvings(chunk):
    sizes, half = [], chunk // 2
    while half >= 1:
        sizes.append(half)
        half //= 2
    return sizes


def halving_parts(chunk, half):
    row, column = positions(chunk)
    row_late = (row & half) != 0
    pairs = ((row & -(2 * half)) == (column & -(2 * half))) & row_late & ((column & half) == 0)
    middle = (row & -(2 * half)) + (half - 1)
    late = row_late & (column > middle) & (column <= row)
    early = jnp.logical_not(row_late) & (column > row) & (column <= middle)
    return pairs, as_selector(late | early)


def scan_forward_kernel(chunk, q_ref, k_ref, v_ref, g_ref, o_ref, qf_ref, a_ref, st_ref, cs_ref, sum_ref, state, start, table):
    step, steps = pl.program_id(1), pl.num_programs(1)

    @pl.when(step == 0)
    def _():
        state[...] = jnp.zeros_like(state)
        start[...] = jnp.zeros_like(start)

    row, column = positions(chunk)
    gates = g_ref[...]
    cumul = exact_sum(as_selector(row >= column), gates)
    left = exact_sum(as_selector(row < column), gates)
    finish = cumul[chunk - 1 : chunk, :]
    mild = jnp.min(finish) > -SAFE
    begin = start[...]
    cs_ref[0] = begin
    grown = jnp.exp(cumul)
    faded = jnp.exp(left)
    begun = jnp.exp(begin)
    kept = jnp.exp(finish)
    scale = DK ** (-0.5)

    @pl.when(mild)
    def _():
        for h in range(HEADS):
            ks = slice(h * DK, (h + 1) * DK)
            far = q_ref[:, ks] * scale * grown[:, ks]
            near = k_ref[:, ks] * jnp.exp(-cumul[:, ks])
            table[h] = jnp.where(row >= column, close_dot(dot_nt, far, near), 0.0)

    @pl.when(jnp.logical_not(mild))
    def _():
        def one_head(h, carry):
            ks = pl.ds(pl.multiple_of(h * DK, DK), DK)
            queries, keys, decay = q_ref[:, ks] * scale, k_ref[:, ks], g_ref[:, ks]
            total = jnp.where(row == column, close_dot(dot_nt, queries, keys), 0.0)
            for half in halvings(chunk):
                pairs, selector = halving_parts(chunk, half)
                factor = jnp.exp(exact_sum(selector, decay))
                total = jnp.where(pairs, close_dot(dot_nt, queries * factor, keys * factor), total)
            table[h] = total
            return carry

        lax.fori_loop(0, HEADS, one_head, 0)

    for h in range(HEADS):
        ks, vs = slice(h * DK, (h + 1) * DK), slice(h * DV, (h + 1) * DV)
        queries = q_ref[:, ks] * scale * grown[:, ks]
        values = low(v_ref[:, vs])
        held = state[h]
        st_ref[0, h] = held
        scores = table[h]
        a_ref[0, h] = low(scores)
        o_ref[:, vs] = close_dot(dot_nn, scores, v_ref[:, vs]) + dot_nt(low(queries), low(held))
        qf_ref[:, ks] = low(queries * begun[:, ks])
        state[h] = held * kept[:, ks] + dot_tn(values, low(k_ref[:, ks] * faded[:, ks]))
    start[...] = begin + finish

    @pl.when(step == steps - 1)
    def _():
        for h in range(HEADS):
            ks = slice(h * DK, (h + 1) * DK)
            sum_ref[0, h, :DV] = state[h]
            sum_ref[0, h, DV:] = jnp.broadcast_to(jnp.exp(begin[:, ks] + finish[:, ks]), (8, DK))


def scan_backward_kernel(
    chunk, q_ref, k_ref, v_ref, g_ref, a_ref, st_ref, cs_ref, in_ref, do_ref, later_ref,
    dq_ref, dk_ref, dv_ref, dg_ref, later, dqi, dki, dci,
):
    @pl.when(pl.program_id(1) == 0)
    def _():
        later[...] = later_ref[0]

    row, column = positions(chunk)
    lower = row >= column
    gates = g_ref[...]
    cumul = exact_sum(as_selector(lower), gates)
    left = exact_sum(as_selector(row < column), gates)
    finish = cumul[chunk - 1 : chunk, :]
    mild = jnp.min(finish) > -SAFE
    grown = jnp.exp(cumul)
    faded = jnp.exp(left)
    kept = jnp.exp(finish)
    begun = jnp.exp(cs_ref[0])
    scale = DK ** (-0.5)

    def overlap(h, vs):
        return close_dot(dot_nt, do_ref[:, vs], v_ref[:, vs])

    @pl.when(mild)
    def _():
        for h in range(HEADS):
            ks, vs = slice(h * DK, (h + 1) * DK), slice(h * DV, (h + 1) * DV)
            shrunk = jnp.exp(-cumul[:, ks])
            far = low(q_ref[:, ks] * scale * grown[:, ks])
            near = low(k_ref[:, ks] * shrunk)
            pairs = low(jnp.where(lower, overlap(h, vs), 0.0))
            for_q, for_k = dot_nn(pairs, near), dot_tn(pairs, far)
            dqi[:, ks] = grown[:, ks] * for_q
            dki[:, ks] = shrunk * for_k
            dci[:, ks] = far.astype(jnp.float32) * for_q - near.astype(jnp.float32) * for_k

    @pl.when(jnp.logical_not(mild))
    def _():
        def one_head(h, carry):
            ks = pl.ds(pl.multiple_of(h * DK, DK), DK)
            vs = pl.ds(pl.multiple_of(h * DV, DV), DV)
            queries, keys, decay = q_ref[:, ks] * scale, k_ref[:, ks], g_ref[:, ks]
            both = overlap(h, vs)
            pairs = low(jnp.where(row == column, both, 0.0))
            grad_q, grad_k = dot_nn(pairs, low(keys)), dot_tn(pairs, low(queries))
            grad_c = jnp.zeros_like(grad_q)
            for half in halvings(chunk):
                here, selector = halving_parts(chunk, half)
                factor = jnp.exp(exact_sum(selector, decay))
                far, near = low(queries * factor), low(keys * factor)
                pairs = low(jnp.where(here, both, 0.0))
                for_q, for_k = dot_nn(pairs, near), dot_tn(pairs, far)
                grad_q += factor * for_q
                grad_k += factor * for_k
                grad_c += far.astype(jnp.float32) * for_q - near.astype(jnp.float32) * for_k
            dqi[:, ks] = grad_q
            dki[:, ks] = grad_k
            dci[:, ks] = grad_c
            return carry

        lax.fori_loop(0, HEADS, one_head, 0)

    before = as_selector(row > column)
    after = as_selector(row <= column)
    for h in range(HEADS):
        ks, vs = slice(h * DK, (h + 1) * DK), slice(h * DV, (h + 1) * DV)
        values, grad_out = low(v_ref[:, vs]), low(do_ref[:, vs])
        held = st_ref[0, h] + in_ref[0, h] * begun[:, ks]
        ahead = later[h]
        ahead_low = low(ahead)
        queries = q_ref[:, ks] * scale * grown[:, ks]
        keys = k_ref[:, ks] * faded[:, ks]
        from_state = dot_nn(grad_out, low(held))
        from_later = dot_nn(values, ahead_low)
        dq_ref[:, ks] = low((dqi[:, ks] + grown[:, ks] * from_state) * scale)
        dk_ref[:, ks] = low(dki[:, ks] + faded[:, ks] * from_later)
        dv_ref[:, vs] = low(dot_tn(a_ref[0, h], grad_out) + dot_nt(low(keys), ahead_low))
        through = kept[:, ks] * jnp.sum(held * ahead, axis=0, keepdims=True)
        dg_ref[:, ks] = (
            exact_sum(after, dci[:, ks] + queries * from_state)
            + exact_sum(before, keys * from_later)
            + through
        )
        later[h] = ahead * kept[:, ks] + dot_tn(grad_out, low(queries))


def mix_forward_kernel(o_ref, qf_ref, in_ref, og_ref, gain_ref, att_ref, mixed_ref):
    gain = gain_ref[...]
    for h in range(HEADS):
        ks, vs = slice(h * DK, (h + 1) * DK), slice(h * DV, (h + 1) * DV)
        attended = o_ref[:, vs] + dot_nt(qf_ref[:, ks], low(in_ref[0, h]))
        att_ref[:, vs] = attended
        outgate = og_ref[:, vs]
        mixed_ref[:, vs] = low(normalize(attended) * gain * (outgate * jax.nn.sigmoid(outgate)))


def mix_backward_kernel(dm_ref, att_ref, og_ref, gain_ref, qf_ref, do_ref, dog_ref, grad_ref, dgain_ref):
    @pl.when(pl.program_id(1) == 0)
    def _():
        grad_ref[...] = jnp.zeros_like(grad_ref)
        dgain_ref[...] = jnp.zeros_like(dgain_ref)

    gain = gain_ref[...]
    for h in range(HEADS):
        ks, vs = slice(h * DK, (h + 1) * DK), slice(h * DV, (h + 1) * DV)
        attended, outgate, grad = att_ref[:, vs], og_ref[:, vs], dm_ref[:, vs]
        inverse = lax.rsqrt(jnp.mean(attended * attended, axis=-1, keepdims=True) + epsilon)
        normed = attended * inverse
        sigma = jax.nn.sigmoid(outgate)
        gated = grad * (outgate * sigma)
        dog_ref[:, vs] = low(grad * normed * gain * (sigma + outgate * sigma * (1.0 - sigma)))
        dgain_ref[0] += jnp.sum(gated * normed, axis=0, keepdims=True)
        inner = gated * gain
        result = inverse * (inner - normed * jnp.mean(inner * normed, axis=-1, keepdims=True))
        do_ref[:, vs] = result
        grad_ref[0, h] += dot_tn(low(result), qf_ref[:, ks])


def rows_spec(chunk, chunks, width, backward=False):
    if backward:
        return pl.BlockSpec((chunk, width), lambda s, c: (s * chunks + chunks - 1 - c, 0))
    return pl.BlockSpec((chunk, width), lambda s, c: (s * chunks + c, 0))


def item_spec(shape):
    return pl.BlockSpec((1,) + shape, lambda s, c: (s,) + (0,) * len(shape))


def chunk_spec(chunks, shape, backward=False):
    if backward:
        return pl.BlockSpec((1,) + shape, lambda s, c: (s * chunks + chunks - 1 - c,) + (0,) * len(shape))
    return pl.BlockSpec((1,) + shape, lambda s, c: (s * chunks + c,) + (0,) * len(shape))


def shaped(shape, kind=jnp.float32):
    return jax.ShapeDtypeStruct(shape, kind)


KEYS, VALUES = HEADS * DK, HEADS * DV
ROOM = pltpu.CompilerParams(vmem_limit_bytes=40 * 1024 * 1024)


def scan_forward(queries, keys, values, gates, seqs, chunk):
    rows = queries.shape[0]
    chunks = rows // seqs // chunk
    keyed, valued = rows_spec(chunk, chunks, KEYS), rows_spec(chunk, chunks, VALUES)
    return pl.pallas_call(
        functools.partial(scan_forward_kernel, chunk),
        grid=(seqs, chunks),
        in_specs=[keyed, keyed, valued, keyed],
        out_specs=[
            valued,
            keyed,
            chunk_spec(chunks, (HEADS, chunk, chunk)),
            chunk_spec(chunks, (HEADS, DV, DK)),
            chunk_spec(chunks, (1, KEYS)),
            item_spec((HEADS, DV + 8, DK)),
        ],
        out_shape=[
            shaped((rows, VALUES)),
            shaped((rows, KEYS), jnp.bfloat16),
            shaped((seqs * chunks, HEADS, chunk, chunk), jnp.bfloat16),
            shaped((seqs * chunks, HEADS, DV, DK)),
            shaped((seqs * chunks, 1, KEYS)),
            shaped((seqs, HEADS, DV + 8, DK)),
        ],
        scratch_shapes=[
            pltpu.VMEM((HEADS, DV, DK), jnp.float32),
            pltpu.VMEM((1, KEYS), jnp.float32),
            pltpu.VMEM((HEADS, chunk, chunk), jnp.float32),
        ],
        compiler_params=ROOM,
        name="scan_forward",
    )(queries, keys, values, gates)


def scan_backward(queries, keys, values, gates, scores, states, starts, incoming, grad_out, later, seqs, chunk):
    rows = queries.shape[0]
    chunks = rows // seqs // chunk
    keyed, valued = rows_spec(chunk, chunks, KEYS, True), rows_spec(chunk, chunks, VALUES, True)
    return pl.pallas_call(
        functools.partial(scan_backward_kernel, chunk),
        grid=(seqs, chunks),
        in_specs=[
            keyed, keyed, valued, keyed,
            chunk_spec(chunks, (HEADS, chunk, chunk), True),
            chunk_spec(chunks, (HEADS, DV, DK), True),
            chunk_spec(chunks, (1, KEYS), True),
            item_spec((HEADS, DV, DK)),
            valued,
            item_spec((HEADS, DV, DK)),
        ],
        out_specs=[keyed, keyed, valued, keyed],
        out_shape=[
            shaped((rows, KEYS), jnp.bfloat16),
            shaped((rows, KEYS), jnp.bfloat16),
            shaped((rows, VALUES), jnp.bfloat16),
            shaped((rows, KEYS)),
        ],
        scratch_shapes=[pltpu.VMEM((HEADS, DV, DK), jnp.float32)] + [pltpu.VMEM((chunk, KEYS), jnp.float32)] * 3,
        compiler_params=ROOM,
        name="scan_backward",
    )(queries, keys, values, gates, scores, states, starts, incoming, grad_out, later)


def mix_forward(local_out, forget, incoming, outgate, gain, seqs, chunk):
    rows = local_out.shape[0]
    chunks = rows // seqs // chunk
    keyed, valued = rows_spec(chunk, chunks, KEYS), rows_spec(chunk, chunks, VALUES)
    whole_gain = pl.BlockSpec((1, DV), lambda s, c: (0, 0))
    return pl.pallas_call(
        mix_forward_kernel,
        grid=(seqs, chunks),
        in_specs=[valued, keyed, item_spec((HEADS, DV, DK)), valued, whole_gain],
        out_specs=[valued, valued],
        out_shape=[shaped((rows, VALUES)), shaped((rows, VALUES), jnp.bfloat16)],
        compiler_params=ROOM,
        name="mix_forward",
    )(local_out, forget, incoming, outgate, gain)


def mix_backward(mixed_grad, attended, outgate, gain, forget, seqs, chunk):
    rows = attended.shape[0]
    chunks = rows // seqs // chunk
    keyed, valued = rows_spec(chunk, chunks, KEYS), rows_spec(chunk, chunks, VALUES)
    whole_gain = pl.BlockSpec((1, DV), lambda s, c: (0, 0))
    return pl.pallas_call(
        mix_backward_kernel,
        grid=(seqs, chunks),
        in_specs=[valued, valued, valued, whole_gain, keyed],
        out_specs=[valued, valued, item_spec((HEADS, DV, DK)), item_spec((1, DV))],
        out_shape=[
            shaped((rows, VALUES)),
            shaped((rows, VALUES), jnp.bfloat16),
            shaped((seqs, HEADS, DV, DK)),
            shaped((seqs, 1, DV)),
        ],
        compiler_params=ROOM,
        name="mix_backward",
    )(mixed_grad, attended, outgate, gain, forget)


def from_neighbours(summary, step):
    count = lax.axis_size("seq")
    total, factor = None, None
    for distance in range(1, count):
        shift = step * distance
        pairs = [(i, i + shift) for i in range(count) if 0 <= i + shift < count]
        came = lax.ppermute(summary, "seq", pairs)
        state, retain = came[:, :, :DV].astype(jnp.float32), came[:, :, DV : DV + 1].astype(jnp.float32)
        if total is None:
            total, factor = state, retain
        else:
            total, factor = total + factor * state, factor * retain
    return total


def product(left, right):
    return jnp.dot(left, right, preferred_element_type=jnp.float32)


def product_left(left, right):
    return lax.dot_general(
        left, right, (((0,), (0,)), ((), ())), preferred_element_type=jnp.float32
    )


def product_right(left, right):
    return lax.dot_general(
        left, right, (((1,), (1,)), ((), ())), preferred_element_type=jnp.float32
    )


def local(
    tokens,
    mixer_gain,
    query_weight,
    key_weight,
    value_weight,
    decay_down,
    decay_up,
    decay_bias,
    outgate_weight,
    head_gain,
    output_weight,
    channel_gain,
    gate_weight,
    up_weight,
    down_weight,
    cotangent,
):
    seqs_here, seg_len, width = tokens.shape
    rows_here = seqs_here * seg_len

    mixer_full = (
        lax.all_gather(mixer_gain, "seq", axis=0, tiled=True),
        lax.all_gather(query_weight, "seq", axis=0, tiled=True),
        lax.all_gather(key_weight, "seq", axis=0, tiled=True),
        lax.all_gather(value_weight, "seq", axis=0, tiled=True),
        lax.all_gather(decay_down, "seq", axis=0, tiled=True),
        lax.all_gather(decay_up, "seq", axis=1, tiled=True),
        lax.all_gather(decay_bias, "seq", axis=0, tiled=True),
        lax.all_gather(outgate_weight, "seq", axis=0, tiled=True),
        lax.all_gather(head_gain, "seq", axis=0, tiled=True),
        lax.all_gather(output_weight, "seq", axis=0, tiled=True),
    )
    gain_one = mixer_full[0].astype(jnp.float32)
    decay_up_f = mixer_full[5].astype(jnp.float32)
    decay_bias_f = mixer_full[6].astype(jnp.float32)
    head_gain_f = mixer_full[8].astype(jnp.float32)
    inputs = tokens.reshape(rows_here, width).astype(jnp.float32)

    def first_norm(inputs_in, gain_in):
        return normalize(inputs_in) * gain_in

    normed_one = first_norm(inputs, gain_one).astype(jnp.bfloat16)
    queries = product(normed_one, mixer_full[1])
    keys_all = product(normed_one, mixer_full[2])
    values_all = product(normed_one, mixer_full[3])
    low_rank = product(normed_one, mixer_full[4])
    outgate = product(normed_one, mixer_full[7])

    def gate_fn(rank_in, up_in, bias_in):
        return (
            jax.nn.log_sigmoid(jnp.dot(rank_in, up_in, precision=highest_precision) + bias_in)
            / normalizer
        )

    gates = gate_fn(low_rank, decay_up_f, decay_bias_f)
    chunk = min(CHUNK, seg_len)
    local_out, forget, scores, states, starts, summary = scan_forward(
        queries, keys_all, values_all, gates, seqs_here, chunk
    )
    incoming_state = from_neighbours(summary, 1)
    attended, mixed = mix_forward(
        local_out, forget, incoming_state, outgate, head_gain_f[None, :], seqs_here, chunk
    )
    resid = inputs + product(mixed, mixer_full[9])
    ffn_full = (
        lax.all_gather(channel_gain, "seq", axis=0, tiled=True),
        lax.all_gather(gate_weight, "seq", axis=0, tiled=True),
        lax.all_gather(up_weight, "seq", axis=0, tiled=True),
        lax.all_gather(down_weight, "seq", axis=0, tiled=True),
    )
    gain_two = ffn_full[0].astype(jnp.float32)
    normed_two = first_norm(resid, gain_two).astype(jnp.bfloat16)
    gate_pre = product(normed_two, ffn_full[1])
    up_pre = product(normed_two, ffn_full[2])

    def swiglu(gate_in, up_in):
        return jax.nn.silu(gate_in) * up_in

    hidden = swiglu(gate_pre, up_pre).astype(jnp.bfloat16)
    result = resid + product(hidden, ffn_full[3])
    block_out = result.astype(jnp.bfloat16).reshape(tokens.shape)
    mixer_back = (
        lax.all_gather(mixer_gain, "seq", axis=0, tiled=True),
        lax.all_gather(query_weight, "seq", axis=0, tiled=True),
        lax.all_gather(key_weight, "seq", axis=0, tiled=True),
        lax.all_gather(value_weight, "seq", axis=0, tiled=True),
        lax.all_gather(decay_down, "seq", axis=0, tiled=True),
        lax.all_gather(decay_up, "seq", axis=1, tiled=True),
        lax.all_gather(decay_bias, "seq", axis=0, tiled=True),
        lax.all_gather(outgate_weight, "seq", axis=0, tiled=True),
        lax.all_gather(head_gain, "seq", axis=0, tiled=True),
        lax.all_gather(output_weight, "seq", axis=0, tiled=True),
    )
    ffn_back = (
        lax.all_gather(channel_gain, "seq", axis=0, tiled=True),
        lax.all_gather(gate_weight, "seq", axis=0, tiled=True),
        lax.all_gather(up_weight, "seq", axis=0, tiled=True),
        lax.all_gather(down_weight, "seq", axis=0, tiled=True),
    )
    grad_out = cotangent.reshape(rows_here, width).astype(jnp.float32)
    grad_low = grad_out.astype(jnp.bfloat16)
    down_weight_grad = product_left(hidden, grad_low)
    hidden_grad = product_right(grad_low, ffn_back[3])
    swiglu_pulled = jax.vjp(swiglu, gate_pre, up_pre)[1](hidden_grad)
    gate_grad = swiglu_pulled[0].astype(jnp.bfloat16)
    up_grad = swiglu_pulled[1].astype(jnp.bfloat16)
    gate_weight_grad = product_left(normed_two, gate_grad)
    up_weight_grad = product_left(normed_two, up_grad)
    normed_two_grad = product_right(gate_grad, ffn_back[1]) + product_right(up_grad, ffn_back[2])
    norm_pulled = jax.vjp(first_norm, resid, gain_two)[1](normed_two_grad)
    resid_grad = grad_out + norm_pulled[0]
    channel_gain_grad = norm_pulled[1]
    branch_grad = resid_grad.astype(jnp.bfloat16)
    output_weight_grad = product_left(mixed, branch_grad)
    mixed_grad = product_right(branch_grad, mixer_back[9])
    attended_grad, outgate_grad, state_grad, head_gain_grad = mix_backward(
        mixed_grad, attended, outgate, head_gain_f[None, :], forget, seqs_here, chunk
    )
    head_gain_grad = head_gain_grad.sum((0, 1))
    later_grad = from_neighbours(
        jnp.concatenate([state_grad, summary[:, :, DV:]], axis=2).astype(jnp.bfloat16), -1
    )
    query_grad, key_grad, value_grad, gates_grad = scan_backward(
        queries, keys_all, values_all, gates, scores, states, starts, incoming_state,
        attended_grad, later_grad, seqs_here, chunk,
    )
    gate_pulled = jax.vjp(gate_fn, low_rank, decay_up_f, decay_bias_f)[1](gates_grad)
    low_rank_grad = gate_pulled[0].astype(jnp.bfloat16)
    decay_up_grad = gate_pulled[1]
    decay_bias_grad = gate_pulled[2]
    query_weight_grad = product_left(normed_one, query_grad)
    key_weight_grad = product_left(normed_one, key_grad)
    value_weight_grad = product_left(normed_one, value_grad)
    decay_down_grad = product_left(normed_one, low_rank_grad)
    outgate_weight_grad = product_left(normed_one, outgate_grad)
    normed_one_grad = (
        product_right(query_grad, mixer_back[1])
        + product_right(key_grad, mixer_back[2])
        + product_right(value_grad, mixer_back[3])
        + product_right(low_rank_grad, mixer_back[4])
        + product_right(outgate_grad, mixer_back[7])
    )
    first_pulled = jax.vjp(first_norm, inputs, gain_one)[1](normed_one_grad)
    tokens_grad = (resid_grad + first_pulled[0]).reshape(tokens.shape)
    mixer_gain_grad = first_pulled[1]
    shares = (
        lax.psum_scatter(
            mixer_gain_grad.astype(jnp.bfloat16), "seq", scatter_dimension=0, tiled=True
        ).astype(jnp.float32),
        lax.psum_scatter(
            query_weight_grad.astype(jnp.bfloat16), "seq", scatter_dimension=0, tiled=True
        ).astype(jnp.float32),
        lax.psum_scatter(
            key_weight_grad.astype(jnp.bfloat16), "seq", scatter_dimension=0, tiled=True
        ).astype(jnp.float32),
        lax.psum_scatter(
            value_weight_grad.astype(jnp.bfloat16), "seq", scatter_dimension=0, tiled=True
        ).astype(jnp.float32),
        lax.psum_scatter(
            decay_down_grad.astype(jnp.bfloat16), "seq", scatter_dimension=0, tiled=True
        ).astype(jnp.float32),
        lax.psum_scatter(
            decay_up_grad.astype(jnp.bfloat16), "seq", scatter_dimension=1, tiled=True
        ).astype(jnp.float32),
        lax.psum_scatter(
            decay_bias_grad.astype(jnp.bfloat16), "seq", scatter_dimension=0, tiled=True
        ).astype(jnp.float32),
        lax.psum_scatter(
            outgate_weight_grad.astype(jnp.bfloat16), "seq", scatter_dimension=0, tiled=True
        ).astype(jnp.float32),
        lax.psum_scatter(
            head_gain_grad.astype(jnp.bfloat16), "seq", scatter_dimension=0, tiled=True
        ).astype(jnp.float32),
        lax.psum_scatter(
            output_weight_grad.astype(jnp.bfloat16), "seq", scatter_dimension=0, tiled=True
        ).astype(jnp.float32),
        lax.psum_scatter(
            channel_gain_grad.astype(jnp.bfloat16), "seq", scatter_dimension=0, tiled=True
        ).astype(jnp.float32),
        lax.psum_scatter(
            gate_weight_grad.astype(jnp.bfloat16), "seq", scatter_dimension=0, tiled=True
        ).astype(jnp.float32),
        lax.psum_scatter(
            up_weight_grad.astype(jnp.bfloat16), "seq", scatter_dimension=0, tiled=True
        ).astype(jnp.float32),
        lax.psum_scatter(
            down_weight_grad.astype(jnp.bfloat16), "seq", scatter_dimension=0, tiled=True
        ).astype(jnp.float32),
    )
    totals = (
        lax.psum(shares[0].astype(jnp.bfloat16), "rep").astype(jnp.float32),
        lax.psum(shares[1].astype(jnp.bfloat16), "rep").astype(jnp.float32),
        lax.psum(shares[2].astype(jnp.bfloat16), "rep").astype(jnp.float32),
        lax.psum(shares[3].astype(jnp.bfloat16), "rep").astype(jnp.float32),
        lax.psum(shares[4].astype(jnp.bfloat16), "rep").astype(jnp.float32),
        lax.psum(shares[5].astype(jnp.bfloat16), "rep").astype(jnp.float32),
        lax.psum(shares[6].astype(jnp.bfloat16), "rep").astype(jnp.float32),
        lax.psum(shares[7].astype(jnp.bfloat16), "rep").astype(jnp.float32),
        lax.psum(shares[8].astype(jnp.bfloat16), "rep").astype(jnp.float32),
        lax.psum(shares[9].astype(jnp.bfloat16), "rep").astype(jnp.float32),
        lax.psum(shares[10].astype(jnp.bfloat16), "rep").astype(jnp.float32),
        lax.psum(shares[11].astype(jnp.bfloat16), "rep").astype(jnp.float32),
        lax.psum(shares[12].astype(jnp.bfloat16), "rep").astype(jnp.float32),
        lax.psum(shares[13].astype(jnp.bfloat16), "rep").astype(jnp.float32),
    )
    return (
        block_out,
        tokens_grad,
        totals[0],
        totals[1],
        totals[2],
        totals[3],
        totals[4],
        totals[5],
        totals[6],
        totals[7],
        totals[8],
        totals[9],
        totals[10],
        totals[11],
        totals[12],
        totals[13],
    )


def solution(mesh):
    in_specs = (
        P("rep", "seq", None),
        P("seq"),
        P("seq", None),
        P("seq", None),
        P("seq", None),
        P("seq", None),
        P(None, "seq"),
        P("seq"),
        P("seq", None),
        P("seq"),
        P("seq", None),
        P("seq"),
        P("seq", None),
        P("seq", None),
        P("seq", None),
        P("rep", "seq", None),
    )
    out_specs = (
        P("rep", "seq", None),
        P("rep", "seq", None),
        P("seq"),
        P("seq", None),
        P("seq", None),
        P("seq", None),
        P("seq", None),
        P(None, "seq"),
        P("seq"),
        P("seq", None),
        P("seq"),
        P("seq", None),
        P("seq"),
        P("seq", None),
        P("seq", None),
        P("seq", None),
    )
    return jax.shard_map(local, mesh=mesh, in_specs=in_specs, out_specs=out_specs, check_vma=False)
```

```python
import functools

import jax
import jax.numpy as jnp
from jax import lax
from jax.experimental import pallas as pl
from jax.experimental.pallas import tpu as pltpu
from jax.sharding import Mesh, PartitionSpec as P

HEADS = 4
DK = 128
DV = 256
CHUNK = 128
SAFE = 60.0


epsilon = 1e-06
normalizer = 16.0
highest_precision = lax.Precision.HIGHEST


def normalize(values_in):
    return values_in * lax.rsqrt(jnp.mean(values_in * values_in, axis=-1, keepdims=True) + epsilon)


def dot_nn(left, right):
    return lax.dot_general(left, right, (((1,), (0,)), ((), ())), preferred_element_type=jnp.float32)


def dot_nt(left, right):
    return lax.dot_general(left, right, (((1,), (1,)), ((), ())), preferred_element_type=jnp.float32)


def dot_tn(left, right):
    return lax.dot_general(left, right, (((0,), (0,)), ((), ())), preferred_element_type=jnp.float32)


def low(array):
    return array.astype(jnp.bfloat16)


def exact_sum(selector, array):
    high = low(array)
    rest = low(array - high.astype(jnp.float32))
    return dot_nn(selector, high) + dot_nn(selector, rest)


def halves(array):
    high = low(array)
    return high, low(array - high.astype(jnp.float32))


def close_dot(dot, left, right):
    (left_high, left_rest), (right_high, right_rest) = halves(left), halves(right)
    return dot(left_high, right_high) + (dot(left_high, right_rest) + dot(left_rest, right_high))


def positions(chunk):
    row = lax.broadcasted_iota(jnp.int32, (chunk, chunk), 0)
    column = lax.broadcasted_iota(jnp.int32, (chunk, chunk), 1)
    return row, column


def as_selector(mask):
    return low(jnp.where(mask, 1.0, 0.0))


def halvings(chunk):
    sizes, half = [], chunk // 2
    while half >= 1:
        sizes.append(half)
        half //= 2
    return sizes


def halving_parts(chunk, half):
    row, column = positions(chunk)
    row_late = (row & half) != 0
    pairs = ((row & -(2 * half)) == (column & -(2 * half))) & row_late & ((column & half) == 0)
    middle = (row & -(2 * half)) + (half - 1)
    late = row_late & (column > middle) & (column <= row)
    early = jnp.logical_not(row_late) & (column > row) & (column <= middle)
    return pairs, as_selector(late | early)


def scan_forward_kernel(chunk, q_ref, k_ref, v_ref, g_ref, o_ref, qf_ref, a_ref, st_ref, cs_ref, sum_ref, state, start, table):
    step, steps = pl.program_id(1), pl.num_programs(1)

    @pl.when(step == 0)
    def _():
        state[...] = jnp.zeros_like(state)
        start[...] = jnp.zeros_like(start)

    row, column = positions(chunk)
    gates = g_ref[...]
    cumul = exact_sum(as_selector(row >= column), gates)
    left = exact_sum(as_selector(row < column), gates)
    finish = cumul[chunk - 1 : chunk, :]
    mild = jnp.min(finish) > -SAFE
    begin = start[...]
    cs_ref[0] = begin
    grown = jnp.exp(cumul)
    faded = jnp.exp(left)
    begun = jnp.exp(begin)
    kept = jnp.exp(finish)
    scale = DK ** (-0.5)

    @pl.when(mild)
    def _():
        for h in range(HEADS):
            ks = slice(h * DK, (h + 1) * DK)
            far = q_ref[:, ks] * scale * grown[:, ks]
            near = k_ref[:, ks] * jnp.exp(-cumul[:, ks])
            table[h] = jnp.where(row >= column, close_dot(dot_nt, far, near), 0.0)

    @pl.when(jnp.logical_not(mild))
    def _():
        def one_head(h, carry):
            ks = pl.ds(pl.multiple_of(h * DK, DK), DK)
            queries, keys, decay = q_ref[:, ks] * scale, k_ref[:, ks], g_ref[:, ks]
            total = jnp.where(row == column, close_dot(dot_nt, queries, keys), 0.0)
            for half in halvings(chunk):
                pairs, selector = halving_parts(chunk, half)
                factor = jnp.exp(exact_sum(selector, decay))
                total = jnp.where(pairs, close_dot(dot_nt, queries * factor, keys * factor), total)
            table[h] = total
            return carry

        lax.fori_loop(0, HEADS, one_head, 0)

    for h in range(HEADS):
        ks, vs = slice(h * DK, (h + 1) * DK), slice(h * DV, (h + 1) * DV)
        queries = q_ref[:, ks] * scale * grown[:, ks]
        values = low(v_ref[:, vs])
        held = state[h]
        st_ref[0, h] = held
        scores = table[h]
        a_ref[0, h] = low(scores)
        o_ref[:, vs] = close_dot(dot_nn, scores, v_ref[:, vs]) + dot_nt(low(queries), low(held))
        qf_ref[:, ks] = low(queries * begun[:, ks])
        state[h] = held * kept[:, ks] + dot_tn(values, low(k_ref[:, ks] * faded[:, ks]))
    start[...] = begin + finish

    @pl.when(step == steps - 1)
    def _():
        for h in range(HEADS):
            ks = slice(h * DK, (h + 1) * DK)
            sum_ref[0, h, :DV] = state[h]
            sum_ref[0, h, DV:] = jnp.broadcast_to(jnp.exp(begin[:, ks] + finish[:, ks]), (8, DK))


def scan_backward_kernel(
    chunk, q_ref, k_ref, v_ref, g_ref, a_ref, st_ref, cs_ref, in_ref, do_ref, later_ref, dog_ref,
    out_ref, dg_ref, later, dqi, dki, dci,
):
    @pl.when(pl.program_id(1) == 0)
    def _():
        later[...] = later_ref[0]

    row, column = positions(chunk)
    lower = row >= column
    gates = g_ref[...]
    cumul = exact_sum(as_selector(lower), gates)
    left = exact_sum(as_selector(row < column), gates)
    finish = cumul[chunk - 1 : chunk, :]
    mild = jnp.min(finish) > -SAFE
    grown = jnp.exp(cumul)
    faded = jnp.exp(left)
    kept = jnp.exp(finish)
    begun = jnp.exp(cs_ref[0])
    scale = DK ** (-0.5)

    def overlap(h, vs):
        return close_dot(dot_nt, do_ref[:, vs], v_ref[:, vs])

    @pl.when(mild)
    def _():
        for h in range(HEADS):
            ks, vs = slice(h * DK, (h + 1) * DK), slice(h * DV, (h + 1) * DV)
            shrunk = jnp.exp(-cumul[:, ks])
            far = low(q_ref[:, ks] * scale * grown[:, ks])
            near = low(k_ref[:, ks] * shrunk)
            pairs = low(jnp.where(lower, overlap(h, vs), 0.0))
            for_q, for_k = dot_nn(pairs, near), dot_tn(pairs, far)
            dqi[:, ks] = grown[:, ks] * for_q
            dki[:, ks] = shrunk * for_k
            dci[:, ks] = far.astype(jnp.float32) * for_q - near.astype(jnp.float32) * for_k

    @pl.when(jnp.logical_not(mild))
    def _():
        def one_head(h, carry):
            ks = pl.ds(pl.multiple_of(h * DK, DK), DK)
            vs = pl.ds(pl.multiple_of(h * DV, DV), DV)
            queries, keys, decay = q_ref[:, ks] * scale, k_ref[:, ks], g_ref[:, ks]
            both = overlap(h, vs)
            pairs = low(jnp.where(row == column, both, 0.0))
            grad_q, grad_k = dot_nn(pairs, low(keys)), dot_tn(pairs, low(queries))
            grad_c = jnp.zeros_like(grad_q)
            for half in halvings(chunk):
                here, selector = halving_parts(chunk, half)
                factor = jnp.exp(exact_sum(selector, decay))
                far, near = low(queries * factor), low(keys * factor)
                pairs = low(jnp.where(here, both, 0.0))
                for_q, for_k = dot_nn(pairs, near), dot_tn(pairs, far)
                grad_q += factor * for_q
                grad_k += factor * for_k
                grad_c += far.astype(jnp.float32) * for_q - near.astype(jnp.float32) * for_k
            dqi[:, ks] = grad_q
            dki[:, ks] = grad_k
            dci[:, ks] = grad_c
            return carry

        lax.fori_loop(0, HEADS, one_head, 0)

    before = as_selector(row > column)
    after = as_selector(row <= column)
    for h in range(HEADS):
        ks, vs = slice(h * DK, (h + 1) * DK), slice(h * DV, (h + 1) * DV)
        values, grad_out = low(v_ref[:, vs]), low(do_ref[:, vs])
        held = st_ref[0, h] + in_ref[0, h] * begun[:, ks]
        ahead = later[h]
        ahead_low = low(ahead)
        queries = q_ref[:, ks] * scale * grown[:, ks]
        keys = k_ref[:, ks] * faded[:, ks]
        from_state = dot_nn(grad_out, low(held))
        from_later = dot_nn(values, ahead_low)
        out_ref[:, ks] = low((dqi[:, ks] + grown[:, ks] * from_state) * scale)
        out_ref[:, KEYS + h * DK : KEYS + (h + 1) * DK] = low(dki[:, ks] + faded[:, ks] * from_later)
        out_ref[:, 2 * KEYS + h * DV : 2 * KEYS + (h + 1) * DV] = low(
            dot_tn(a_ref[0, h], grad_out) + dot_nt(low(keys), ahead_low)
        )
        through = kept[:, ks] * jnp.sum(held * ahead, axis=0, keepdims=True)
        dg_ref[:, ks] = (
            exact_sum(after, dci[:, ks] + queries * from_state)
            + exact_sum(before, keys * from_later)
            + through
        )
        later[h] = ahead * kept[:, ks] + dot_tn(grad_out, low(queries))
    out_ref[:, 2 * KEYS + VALUES :] = dog_ref[...]


def mix_forward_kernel(o_ref, qf_ref, in_ref, og_ref, gain_ref, att_ref, mixed_ref):
    gain = gain_ref[...]
    for h in range(HEADS):
        ks, vs = slice(h * DK, (h + 1) * DK), slice(h * DV, (h + 1) * DV)
        attended = o_ref[:, vs] + dot_nt(qf_ref[:, ks], low(in_ref[0, h]))
        att_ref[:, vs] = attended
        outgate = og_ref[:, vs]
        mixed_ref[:, vs] = low(normalize(attended) * gain * (outgate * jax.nn.sigmoid(outgate)))


def mix_backward_kernel(dm_ref, att_ref, og_ref, gain_ref, qf_ref, do_ref, dog_ref, grad_ref, dgain_ref):
    @pl.when(pl.program_id(1) == 0)
    def _():
        grad_ref[...] = jnp.zeros_like(grad_ref)
        dgain_ref[...] = jnp.zeros_like(dgain_ref)

    gain = gain_ref[...]
    for h in range(HEADS):
        ks, vs = slice(h * DK, (h + 1) * DK), slice(h * DV, (h + 1) * DV)
        attended, outgate, grad = att_ref[:, vs], og_ref[:, vs], dm_ref[:, vs]
        inverse = lax.rsqrt(jnp.mean(attended * attended, axis=-1, keepdims=True) + epsilon)
        normed = attended * inverse
        sigma = jax.nn.sigmoid(outgate)
        gated = grad * (outgate * sigma)
        dog_ref[:, vs] = low(grad * normed * gain * (sigma + outgate * sigma * (1.0 - sigma)))
        dgain_ref[0] += jnp.sum(gated * normed, axis=0, keepdims=True)
        inner = gated * gain
        result = inverse * (inner - normed * jnp.mean(inner * normed, axis=-1, keepdims=True))
        do_ref[:, vs] = result
        grad_ref[0, h] += dot_tn(low(result), qf_ref[:, ks])


def rows_spec(chunk, chunks, width, backward=False):
    if backward:
        return pl.BlockSpec((chunk, width), lambda s, c: (s * chunks + chunks - 1 - c, 0))
    return pl.BlockSpec((chunk, width), lambda s, c: (s * chunks + c, 0))


def item_spec(shape):
    return pl.BlockSpec((1,) + shape, lambda s, c: (s,) + (0,) * len(shape))


def chunk_spec(chunks, shape, backward=False):
    if backward:
        return pl.BlockSpec((1,) + shape, lambda s, c: (s * chunks + chunks - 1 - c,) + (0,) * len(shape))
    return pl.BlockSpec((1,) + shape, lambda s, c: (s * chunks + c,) + (0,) * len(shape))


def shaped(shape, kind=jnp.float32):
    return jax.ShapeDtypeStruct(shape, kind)


def packed_specs(chunk, chunks, backward=False):
    def at(width, place):
        whole = rows_spec(chunk, chunks, width, backward)
        return pl.BlockSpec(whole.block_shape, lambda s, c: (whole.index_map(s, c)[0], place))

    return [at(KEYS, 0), at(KEYS, 1), at(VALUES, 1), at(VALUES, 2)]


KEYS, VALUES = HEADS * DK, HEADS * DV
PACKED = 2 * KEYS + 2 * VALUES
ROOM = pltpu.CompilerParams(vmem_limit_bytes=40 * 1024 * 1024)


def scan_forward(projected, gates, seqs, chunk):
    rows = projected.shape[0]
    chunks = rows // seqs // chunk
    keyed, valued = rows_spec(chunk, chunks, KEYS), rows_spec(chunk, chunks, VALUES)
    return pl.pallas_call(
        functools.partial(scan_forward_kernel, chunk),
        grid=(seqs, chunks),
        in_specs=packed_specs(chunk, chunks)[:3] + [keyed],
        out_specs=[
            valued,
            keyed,
            chunk_spec(chunks, (HEADS, chunk, chunk)),
            chunk_spec(chunks, (HEADS, DV, DK)),
            chunk_spec(chunks, (1, KEYS)),
            item_spec((HEADS, DV + 8, DK)),
        ],
        out_shape=[
            shaped((rows, VALUES)),
            shaped((rows, KEYS), jnp.bfloat16),
            shaped((seqs * chunks, HEADS, chunk, chunk), jnp.bfloat16),
            shaped((seqs * chunks, HEADS, DV, DK)),
            shaped((seqs * chunks, 1, KEYS)),
            shaped((seqs, HEADS, DV + 8, DK)),
        ],
        scratch_shapes=[
            pltpu.VMEM((HEADS, DV, DK), jnp.float32),
            pltpu.VMEM((1, KEYS), jnp.float32),
            pltpu.VMEM((HEADS, chunk, chunk), jnp.float32),
        ],
        compiler_params=ROOM,
        name="scan_forward",
    )(projected, projected, projected, gates)


def scan_backward(
    projected, gates, scores, states, starts, incoming, grad_out, later, outgate_grad, seqs, chunk
):
    rows = projected.shape[0]
    chunks = rows // seqs // chunk
    keyed, valued = rows_spec(chunk, chunks, KEYS, True), rows_spec(chunk, chunks, VALUES, True)
    return pl.pallas_call(
        functools.partial(scan_backward_kernel, chunk),
        grid=(seqs, chunks),
        in_specs=[
            *packed_specs(chunk, chunks, True)[:3],
            keyed,
            chunk_spec(chunks, (HEADS, chunk, chunk), True),
            chunk_spec(chunks, (HEADS, DV, DK), True),
            chunk_spec(chunks, (1, KEYS), True),
            item_spec((HEADS, DV, DK)),
            valued,
            item_spec((HEADS, DV, DK)),
            valued,
        ],
        out_specs=[rows_spec(chunk, chunks, PACKED, True), keyed],
        out_shape=[shaped((rows, PACKED), jnp.bfloat16), shaped((rows, KEYS))],
        scratch_shapes=[pltpu.VMEM((HEADS, DV, DK), jnp.float32)] + [pltpu.VMEM((chunk, KEYS), jnp.float32)] * 3,
        compiler_params=ROOM,
        name="scan_backward",
    )(
        projected, projected, projected, gates, scores, states, starts, incoming, grad_out, later, outgate_grad
    )


def mix_forward(local_out, forget, incoming, projected, gain, seqs, chunk):
    rows = local_out.shape[0]
    chunks = rows // seqs // chunk
    keyed, valued = rows_spec(chunk, chunks, KEYS), rows_spec(chunk, chunks, VALUES)
    whole_gain = pl.BlockSpec((1, DV), lambda s, c: (0, 0))
    return pl.pallas_call(
        mix_forward_kernel,
        grid=(seqs, chunks),
        in_specs=[valued, keyed, item_spec((HEADS, DV, DK)), packed_specs(chunk, chunks)[3], whole_gain],
        out_specs=[valued, valued],
        out_shape=[shaped((rows, VALUES)), shaped((rows, VALUES), jnp.bfloat16)],
        compiler_params=ROOM,
        name="mix_forward",
    )(local_out, forget, incoming, projected, gain)


def mix_backward(mixed_grad, attended, projected, gain, forget, seqs, chunk):
    rows = attended.shape[0]
    chunks = rows // seqs // chunk
    keyed, valued = rows_spec(chunk, chunks, KEYS), rows_spec(chunk, chunks, VALUES)
    whole_gain = pl.BlockSpec((1, DV), lambda s, c: (0, 0))
    return pl.pallas_call(
        mix_backward_kernel,
        grid=(seqs, chunks),
        in_specs=[valued, valued, packed_specs(chunk, chunks)[3], whole_gain, keyed],
        out_specs=[valued, valued, item_spec((HEADS, DV, DK)), item_spec((1, DV))],
        out_shape=[
            shaped((rows, VALUES)),
            shaped((rows, VALUES), jnp.bfloat16),
            shaped((seqs, HEADS, DV, DK)),
            shaped((seqs, 1, DV)),
        ],
        compiler_params=ROOM,
        name="mix_backward",
    )(mixed_grad, attended, projected, gain, forget)


def from_neighbours(summary, step):
    count = lax.axis_size("seq")
    total, factor = None, None
    for distance in range(1, count):
        shift = step * distance
        pairs = [(i, i + shift) for i in range(count) if 0 <= i + shift < count]
        came = lax.ppermute(summary, "seq", pairs)
        state, retain = came[:, :, :DV].astype(jnp.float32), came[:, :, DV : DV + 1].astype(jnp.float32)
        if total is None:
            total, factor = state, retain
        else:
            total, factor = total + factor * state, factor * retain
    return total


def product(left, right):
    return jnp.dot(left, right, preferred_element_type=jnp.float32)


def product_left(left, right):
    return lax.dot_general(
        left, right, (((0,), (0,)), ((), ())), preferred_element_type=jnp.float32
    )


def product_right(left, right):
    return lax.dot_general(
        left, right, (((1,), (1,)), ((), ())), preferred_element_type=jnp.float32
    )


EVERYWHERE = ("z", "core", "seq")


def swapped(array):
    return lax.ppermute(array, "core", [(0, 1), (1, 0)])


def own_half(array, dim, other=False):
    core = lax.axis_index("core")
    size = array.shape[dim] // 2
    return lax.dynamic_slice_in_dim(array, ((1 - core) if other else core) * size, size, dim)


def joined(mine, theirs, dim):
    first = lax.axis_index("core") == 0
    return jnp.where(
        first, jnp.concatenate([mine, theirs], dim), jnp.concatenate([theirs, mine], dim)
    )


def core_columns(array, other=False):
    count = lax.axis_size("seq")
    rows, width = array.shape
    split = array.reshape(rows, count, width // count)
    return own_half(split, 2, other).reshape(rows, width // 2)


def pair_sum(left_theirs, left_mine, right_theirs, right_mine):
    theirs = swapped(low(product_left(left_theirs, right_theirs)))
    return low(product_left(left_mine, right_mine) + theirs.astype(jnp.float32))


def scattered(array):
    return lax.psum_scatter(array, "seq", scatter_dimension=0, tiled=True)


def local(
    tokens,
    mixer_gain,
    query_weight,
    key_weight,
    value_weight,
    decay_down,
    decay_up,
    decay_bias,
    outgate_weight,
    head_gain,
    output_weight,
    channel_gain,
    gate_weight,
    up_weight,
    down_weight,
    cotangent,
):
    seqs_here, seg_len, width = tokens.shape
    rows_here = seqs_here * seg_len
    count, place = lax.axis_size("seq"), lax.axis_index("seq")
    ff = gate_weight.shape[1]

    half_rows = query_weight.shape[0] // 2
    smalls = [mixer_gain, decay_down, decay_up, decay_bias, head_gain, channel_gain]
    flat = jnp.concatenate([small.reshape(-1) for small in smalls])
    extra = -(-flat.size // (half_rows * 128)) * 128
    flat = jnp.pad(flat, (0, half_rows * extra - flat.size)).reshape(half_rows, extra)
    mixer_packed = jnp.concatenate(
        [
            own_half(weight, 0)
            for weight in (query_weight, key_weight, value_weight, outgate_weight, output_weight)
        ]
        + [flat],
        axis=1,
    )
    mixer_mine = lax.all_gather(mixer_packed, "seq")
    mixer_theirs = swapped(mixer_mine)
    wide = PACKED + width
    mixer_full = joined(mixer_mine[:, :, :wide], mixer_theirs[:, :, :wide], 1).reshape(width, wide)
    projections, output_full = mixer_full[:, :PACKED], mixer_full[:, PACKED:]
    small_all = mixer_mine[:, :, wide:].reshape(count, -1)
    pieces, begin = [], 0
    for small in smalls:
        pieces.append(small_all[:, begin : begin + small.size].reshape((count,) + small.shape))
        begin += small.size
    gain_one = pieces[0].reshape(-1).astype(jnp.float32)
    decay_down_all = pieces[1].reshape(width, -1)
    decay_up_f = pieces[2].transpose(1, 0, 2).reshape(decay_up.shape[0], -1).astype(jnp.float32)
    decay_bias_f = pieces[3].reshape(-1).astype(jnp.float32)
    head_gain_f = pieces[4].reshape(-1).astype(jnp.float32)
    gain_two = pieces[5].reshape(-1).astype(jnp.float32)

    ffn_packed = jnp.concatenate([own_half(gate_weight, 0), own_half(up_weight, 0)], axis=1)
    ffn_mine = lax.all_gather(ffn_packed, "seq")
    ffn_full = joined(ffn_mine, swapped(ffn_mine), 1).reshape(width, 2 * ff)
    down_mine = lax.all_gather(own_half(down_weight, 1), "seq", tiled=True)
    down_full = joined(down_mine, swapped(down_mine), 1)

    inputs = tokens.reshape(rows_here, width).astype(jnp.float32)

    def first_norm(inputs_in, gain_in):
        return normalize(inputs_in) * gain_in

    normed_one = first_norm(inputs, gain_one).astype(jnp.bfloat16)
    projected = product(normed_one, projections)
    low_rank = product(normed_one, decay_down_all)

    def gate_fn(rank_in, up_in, bias_in):
        return (
            jax.nn.log_sigmoid(jnp.dot(rank_in, up_in, precision=highest_precision) + bias_in)
            / normalizer
        )

    gates = gate_fn(low_rank, decay_up_f, decay_bias_f)
    chunk = min(CHUNK, seg_len)
    local_out, forget, scores, states, starts, summary = scan_forward(projected, gates, seqs_here, chunk)
    incoming_state = from_neighbours(summary, 1)
    attended, mixed = mix_forward(
        local_out, forget, incoming_state, projected, head_gain_f[None, :], seqs_here, chunk
    )
    resid = inputs + product(mixed, output_full)
    normed_two = first_norm(resid, gain_two).astype(jnp.bfloat16)
    both_pre = product(normed_two, ffn_full)

    def swiglu(both):
        return jax.nn.silu(both[:, :ff]) * both[:, ff:]

    hidden = swiglu(both_pre).astype(jnp.bfloat16)
    result = resid + product(hidden, down_full)
    block_out = result.astype(jnp.bfloat16).reshape(tokens.shape)

    grad_low = cotangent.reshape(rows_here, width)
    grad_out = grad_low.astype(jnp.float32)
    down_share = scattered(pair_sum(hidden, hidden, own_half(grad_low, 1, True), own_half(grad_low, 1)))
    hidden_grad = product_right(grad_low, down_full)
    gate_pre, up_pre = both_pre[:, :ff], both_pre[:, ff:]
    sigma = jax.nn.sigmoid(gate_pre)
    both_grad = jnp.concatenate(
        [
            low(hidden_grad * up_pre * (sigma + gate_pre * sigma * (1.0 - sigma))),
            low(hidden_grad * (gate_pre * sigma)),
        ],
        axis=1,
    )
    ffn_share = scattered(
        pair_sum(core_columns(normed_two, True), core_columns(normed_two), both_grad, both_grad)
    )
    normed_two_grad = product_right(both_grad, ffn_full)
    norm_pulled = jax.vjp(first_norm, resid, gain_two)[1](normed_two_grad)
    resid_grad = grad_out + norm_pulled[0]
    channel_gain_grad = norm_pulled[1]
    branch_grad = resid_grad.astype(jnp.bfloat16)
    mixed_grad = product_right(branch_grad, output_full)
    attended_grad, outgate_grad, state_grad, head_gain_grad = mix_backward(
        mixed_grad, attended, projected, head_gain_f[None, :], forget, seqs_here, chunk
    )
    head_gain_grad = head_gain_grad.sum((0, 1))
    later_grad = from_neighbours(
        jnp.concatenate([state_grad, summary[:, :, DV:]], axis=2).astype(jnp.bfloat16), -1
    )
    packed_grad, gates_grad = scan_backward(
        projected, gates, scores, states, starts, incoming_state,
        attended_grad, later_grad, outgate_grad, seqs_here, chunk,
    )
    gate_pulled = jax.vjp(gate_fn, low_rank, decay_up_f, decay_bias_f)[1](gates_grad)
    low_rank_grad = gate_pulled[0].astype(jnp.bfloat16)
    decay_down_grad = product_left(normed_one, low_rank_grad)
    normed_one_grad = product_right(packed_grad, projections) + product_right(low_rank_grad, decay_down_all)
    first_pulled = jax.vjp(first_norm, inputs, gain_one)[1](normed_one_grad)
    tokens_grad = (resid_grad + first_pulled[0]).reshape(tokens.shape)

    packed_theirs = swapped(
        jnp.concatenate(
            [
                low(product_left(core_columns(normed_one, True), packed_grad)),
                low(product_left(core_columns(mixed, True), branch_grad)),
            ],
            axis=1,
        )
    ).astype(jnp.float32)
    mixer_share = scattered(
        jnp.concatenate(
            [
                low(product_left(core_columns(normed_one), packed_grad) + packed_theirs[:, :PACKED]),
                low(product_left(core_columns(mixed), branch_grad) + packed_theirs[:, PACKED:]),
            ],
            axis=1,
        )
    )

    def whole(share, dim):
        total = lax.psum(share, "z")
        return joined(total, swapped(total), dim).astype(jnp.float32)

    down_weight_grad = whole(down_share, 1)
    ffn_total = whole(ffn_share, 0)
    mixer_total = whole(mixer_share, 0)

    small_grads = [
        first_pulled[1], decay_down_grad, gate_pulled[1], gate_pulled[2], head_gain_grad, channel_gain_grad,
    ]
    summed = lax.psum(jnp.concatenate([grad.reshape(-1) for grad in small_grads]), EVERYWHERE)
    shares, begin = [], 0
    for grad in small_grads:
        shares.append(summed[begin : begin + grad.size].reshape(grad.shape))
        begin += grad.size

    def own_share(array, dim=0):
        size = array.shape[dim] // count
        return lax.dynamic_slice_in_dim(array, place * size, size, dim)

    columns = (0, KEYS, 2 * KEYS, 2 * KEYS + VALUES, PACKED, wide)
    query_g, key_g, value_g, outgate_g, output_g = (
        mixer_total[:, a:b] for a, b in zip(columns[:-1], columns[1:])
    )
    return (
        block_out,
        tokens_grad,
        own_share(shares[0]),
        query_g,
        key_g,
        value_g,
        own_share(shares[1]),
        own_share(shares[2], 1),
        own_share(shares[3]),
        outgate_g,
        own_share(shares[4]),
        output_g,
        own_share(shares[5]),
        ffn_total[:, :ff],
        ffn_total[:, ff:],
        down_weight_grad,
    )


def solution(mesh):
    rep, seq = mesh.shape["rep"], mesh.shape["seq"]
    cores = Mesh(mesh.devices.reshape(rep // 2, 2, seq), EVERYWHERE)
    sequences, weights = P(("z", "core"), "seq", None), P("seq", None)
    in_specs = (
        sequences,
        P("seq"),
        weights,
        weights,
        weights,
        weights,
        P(None, "seq"),
        P("seq"),
        weights,
        P("seq"),
        weights,
        P("seq"),
        weights,
        weights,
        weights,
        sequences,
    )
    out_specs = (sequences, *in_specs[:15])
    return jax.shard_map(local, mesh=cores, in_specs=in_specs, out_specs=out_specs, check_vma=False)
```

```python
import functools

import jax
import jax.numpy as jnp
from jax import lax
from jax.experimental import pallas as pl
from jax.experimental.pallas import tpu as pltpu
from jax.sharding import Mesh, PartitionSpec as P

HEADS = 4
DK = 128
DV = 256
PAIR = HEADS // 2
CHUNK = 128
SAFE = 60.0


epsilon = 1e-06
normalizer = 16.0
highest_precision = lax.Precision.HIGHEST


def normalize(values_in):
    return values_in * lax.rsqrt(jnp.mean(values_in * values_in, axis=-1, keepdims=True) + epsilon)


def dot_nn(left, right):
    return lax.dot_general(left, right, (((1,), (0,)), ((), ())), preferred_element_type=jnp.float32)


def dot_nt(left, right):
    return lax.dot_general(left, right, (((1,), (1,)), ((), ())), preferred_element_type=jnp.float32)


def dot_tn(left, right):
    return lax.dot_general(left, right, (((0,), (0,)), ((), ())), preferred_element_type=jnp.float32)


def low(array):
    return array.astype(jnp.bfloat16)


def exact_sum(selector, array):
    high = low(array)
    rest = low(array - high.astype(jnp.float32))
    return dot_nn(selector, high) + dot_nn(selector, rest)


def halves(array):
    high = low(array)
    return high, low(array - high.astype(jnp.float32))


def close_dot(dot, left, right):
    (left_high, left_rest), (right_high, right_rest) = halves(left), halves(right)
    return dot(left_high, right_high) + (dot(left_high, right_rest) + dot(left_rest, right_high))


def at_head(refs, head, size):
    place = head % PAIR
    return refs[head // PAIR][:, place * size : (place + 1) * size]


def positions(chunk):
    row = lax.broadcasted_iota(jnp.int32, (chunk, chunk), 0)
    column = lax.broadcasted_iota(jnp.int32, (chunk, chunk), 1)
    return row, column


def as_selector(mask):
    return low(jnp.where(mask, 1.0, 0.0))


def halvings(chunk):
    sizes, half = [], chunk // 2
    while half >= 1:
        sizes.append(half)
        half //= 2
    return sizes


def halving_parts(chunk, half):
    row, column = positions(chunk)
    row_late = (row & half) != 0
    pairs = ((row & -(2 * half)) == (column & -(2 * half))) & row_late & ((column & half) == 0)
    middle = (row & -(2 * half)) + (half - 1)
    late = row_late & (column > middle) & (column <= row)
    early = jnp.logical_not(row_late) & (column > row) & (column <= middle)
    return pairs, as_selector(late | early)


def scan_forward_kernel(chunk, q0, k0, v0, q1, k1, v1, g_ref, o_ref, qf_ref, a_ref, st_ref, cs_ref, sum_ref, state, start, table):
    step, steps = pl.program_id(1), pl.num_programs(1)
    q_refs, k_refs, v_refs = (q0, q1), (k0, k1), (v0, v1)

    @pl.when(step == 0)
    def _():
        state[...] = jnp.zeros_like(state)
        start[...] = jnp.zeros_like(start)

    row, column = positions(chunk)
    gates = g_ref[...]
    cumul = exact_sum(as_selector(row >= column), gates)
    left = exact_sum(as_selector(row < column), gates)
    finish = cumul[chunk - 1 : chunk, :]
    mild = jnp.min(finish) > -SAFE
    begin = start[...]
    cs_ref[0] = begin
    grown = jnp.exp(cumul)
    faded = jnp.exp(left)
    begun = jnp.exp(begin)
    kept = jnp.exp(finish)
    scale = DK ** (-0.5)

    @pl.when(mild)
    def _():
        for h in range(HEADS):
            ks = slice(h * DK, (h + 1) * DK)
            far = at_head(q_refs, h, DK) * scale * grown[:, ks]
            near = at_head(k_refs, h, DK) * jnp.exp(-cumul[:, ks])
            table[h] = jnp.where(row >= column, close_dot(dot_nt, far, near), 0.0)

    @pl.when(jnp.logical_not(mild))
    def _():
        for h in range(HEADS):
            ks = slice(h * DK, (h + 1) * DK)
            queries, keys, decay = at_head(q_refs, h, DK) * scale, at_head(k_refs, h, DK), g_ref[:, ks]
            total = jnp.where(row == column, close_dot(dot_nt, queries, keys), 0.0)
            for half in halvings(chunk):
                pairs, selector = halving_parts(chunk, half)
                factor = jnp.exp(exact_sum(selector, decay))
                total = jnp.where(pairs, close_dot(dot_nt, queries * factor, keys * factor), total)
            table[h] = total

    for h in range(HEADS):
        ks, vs = slice(h * DK, (h + 1) * DK), slice(h * DV, (h + 1) * DV)
        queries = at_head(q_refs, h, DK) * scale * grown[:, ks]
        own_values = at_head(v_refs, h, DV)
        values = low(own_values)
        held = state[h]
        st_ref[0, h] = held
        scores = table[h]
        a_ref[0, h] = low(scores)
        o_ref[:, vs] = close_dot(dot_nn, scores, own_values) + dot_nt(low(queries), low(held))
        qf_ref[:, ks] = low(queries * begun[:, ks])
        state[h] = held * kept[:, ks] + dot_tn(values, low(at_head(k_refs, h, DK) * faded[:, ks]))
    start[...] = begin + finish

    @pl.when(step == steps - 1)
    def _():
        for h in range(HEADS):
            ks = slice(h * DK, (h + 1) * DK)
            sum_ref[0, h, :DV] = state[h]
            sum_ref[0, h, DV:] = jnp.broadcast_to(jnp.exp(begin[:, ks] + finish[:, ks]), (8, DK))


def scan_backward_kernel(
    chunk, q0, k0, v0, q1, k1, v1, g_ref, a_ref, st_ref, cs_ref, in_ref, do_ref, later_ref, dog0, dog1,
    out0, out1, dg_ref, later, dqi, dki, dci,
):
    q_refs, k_refs, v_refs = (q0, q1), (k0, k1), (v0, v1)

    @pl.when(pl.program_id(1) == 0)
    def _():
        later[...] = later_ref[0]

    row, column = positions(chunk)
    lower = row >= column
    gates = g_ref[...]
    cumul = exact_sum(as_selector(lower), gates)
    left = exact_sum(as_selector(row < column), gates)
    finish = cumul[chunk - 1 : chunk, :]
    mild = jnp.min(finish) > -SAFE
    grown = jnp.exp(cumul)
    faded = jnp.exp(left)
    kept = jnp.exp(finish)
    begun = jnp.exp(cs_ref[0])
    scale = DK ** (-0.5)

    def overlap(h, vs):
        return close_dot(dot_nt, do_ref[:, vs], at_head(v_refs, h, DV))

    @pl.when(mild)
    def _():
        for h in range(HEADS):
            ks, vs = slice(h * DK, (h + 1) * DK), slice(h * DV, (h + 1) * DV)
            shrunk = jnp.exp(-cumul[:, ks])
            far = low(at_head(q_refs, h, DK) * scale * grown[:, ks])
            near = low(at_head(k_refs, h, DK) * shrunk)
            pairs = low(jnp.where(lower, overlap(h, vs), 0.0))
            for_q, for_k = dot_nn(pairs, near), dot_tn(pairs, far)
            dqi[:, ks] = grown[:, ks] * for_q
            dki[:, ks] = shrunk * for_k
            dci[:, ks] = far.astype(jnp.float32) * for_q - near.astype(jnp.float32) * for_k

    @pl.when(jnp.logical_not(mild))
    def _():
        for h in range(HEADS):
            ks, vs = slice(h * DK, (h + 1) * DK), slice(h * DV, (h + 1) * DV)
            queries, keys, decay = at_head(q_refs, h, DK) * scale, at_head(k_refs, h, DK), g_ref[:, ks]
            both = overlap(h, vs)
            pairs = low(jnp.where(row == column, both, 0.0))
            grad_q, grad_k = dot_nn(pairs, low(keys)), dot_tn(pairs, low(queries))
            grad_c = jnp.zeros_like(grad_q)
            for half in halvings(chunk):
                here, selector = halving_parts(chunk, half)
                factor = jnp.exp(exact_sum(selector, decay))
                far, near = low(queries * factor), low(keys * factor)
                pairs = low(jnp.where(here, both, 0.0))
                for_q, for_k = dot_nn(pairs, near), dot_tn(pairs, far)
                grad_q += factor * for_q
                grad_k += factor * for_k
                grad_c += far.astype(jnp.float32) * for_q - near.astype(jnp.float32) * for_k
            dqi[:, ks] = grad_q
            dki[:, ks] = grad_k
            dci[:, ks] = grad_c

    before = as_selector(row > column)
    after = as_selector(row <= column)
    for h in range(HEADS):
        ks, vs = slice(h * DK, (h + 1) * DK), slice(h * DV, (h + 1) * DV)
        values, grad_out = low(at_head(v_refs, h, DV)), low(do_ref[:, vs])
        held = st_ref[0, h] + in_ref[0, h] * begun[:, ks]
        ahead = later[h]
        ahead_low = low(ahead)
        queries = at_head(q_refs, h, DK) * scale * grown[:, ks]
        keys = at_head(k_refs, h, DK) * faded[:, ks]
        out_ref, place = (out0, out1)[h // PAIR], h % PAIR
        from_state = dot_nn(grad_out, low(held))
        from_later = dot_nn(values, ahead_low)
        out_ref[:, place * DK : (place + 1) * DK] = low((dqi[:, ks] + grown[:, ks] * from_state) * scale)
        out_ref[:, KEYS // 2 + place * DK : KEYS // 2 + (place + 1) * DK] = low(dki[:, ks] + faded[:, ks] * from_later)
        out_ref[:, KEYS + place * DV : KEYS + (place + 1) * DV] = low(
            dot_tn(a_ref[0, h], grad_out) + dot_nt(low(keys), ahead_low)
        )
        through = kept[:, ks] * jnp.sum(held * ahead, axis=0, keepdims=True)
        dg_ref[:, ks] = (
            exact_sum(after, dci[:, ks] + queries * from_state)
            + exact_sum(before, keys * from_later)
            + through
        )
        later[h] = ahead * kept[:, ks] + dot_tn(grad_out, low(queries))
    out0[:, KEYS + VALUES // 2 :] = dog0[...]
    out1[:, KEYS + VALUES // 2 :] = dog1[...]


def mix_forward_kernel(o_ref, qf_ref, in_ref, og0, og1, gain_ref, att_ref, mixed_ref):
    gain = gain_ref[...]
    for h in range(HEADS):
        ks, vs = slice(h * DK, (h + 1) * DK), slice(h * DV, (h + 1) * DV)
        attended = o_ref[:, vs] + dot_nt(qf_ref[:, ks], low(in_ref[0, h]))
        att_ref[:, vs] = attended
        outgate = at_head((og0, og1), h, DV)
        mixed_ref[:, vs] = low(normalize(attended) * gain * (outgate * jax.nn.sigmoid(outgate)))


def mix_backward_kernel(dm_ref, att_ref, og0, og1, gain_ref, qf_ref, do_ref, dog0, dog1, grad_ref, dgain_ref):
    @pl.when(pl.program_id(1) == 0)
    def _():
        grad_ref[...] = jnp.zeros_like(grad_ref)
        dgain_ref[...] = jnp.zeros_like(dgain_ref)

    gain = gain_ref[...]
    for h in range(HEADS):
        ks, vs = slice(h * DK, (h + 1) * DK), slice(h * DV, (h + 1) * DV)
        attended, outgate, grad = att_ref[:, vs], at_head((og0, og1), h, DV), dm_ref[:, vs]
        dog_ref, place = (dog0, dog1)[h // PAIR], h % PAIR
        inverse = lax.rsqrt(jnp.mean(attended * attended, axis=-1, keepdims=True) + epsilon)
        normed = attended * inverse
        sigma = jax.nn.sigmoid(outgate)
        gated = grad * (outgate * sigma)
        dog_ref[:, place * DV : (place + 1) * DV] = low(grad * normed * gain * (sigma + outgate * sigma * (1.0 - sigma)))
        dgain_ref[0] += jnp.sum(gated * normed, axis=0, keepdims=True)
        inner = gated * gain
        result = inverse * (inner - normed * jnp.mean(inner * normed, axis=-1, keepdims=True))
        do_ref[:, vs] = result
        grad_ref[0, h] += dot_tn(low(result), qf_ref[:, ks])


def rows_spec(chunk, chunks, width, backward=False):
    if backward:
        return pl.BlockSpec((chunk, width), lambda s, c: (s * chunks + chunks - 1 - c, 0))
    return pl.BlockSpec((chunk, width), lambda s, c: (s * chunks + c, 0))


def item_spec(shape):
    return pl.BlockSpec((1,) + shape, lambda s, c: (s,) + (0,) * len(shape))


def chunk_spec(chunks, shape, backward=False):
    if backward:
        return pl.BlockSpec((1,) + shape, lambda s, c: (s * chunks + chunks - 1 - c,) + (0,) * len(shape))
    return pl.BlockSpec((1,) + shape, lambda s, c: (s * chunks + c,) + (0,) * len(shape))


def shaped(shape, kind=jnp.float32):
    return jax.ShapeDtypeStruct(shape, kind)


def packed_specs(chunk, chunks, backward=False):
    def at(width, place):
        whole = rows_spec(chunk, chunks, width, backward)
        return pl.BlockSpec(whole.block_shape, lambda s, c: (whole.index_map(s, c)[0], place))

    return [at(KEYS // 2, 0), at(KEYS // 2, 1), at(VALUES // 2, 1), at(VALUES // 2, 2)]


KEYS, VALUES = HEADS * DK, HEADS * DV
PACKED = KEYS + VALUES
ROOM = pltpu.CompilerParams(vmem_limit_bytes=40 * 1024 * 1024)


def scan_forward(mine, theirs, gates, seqs, chunk):
    rows = gates.shape[0]
    chunks = rows // seqs // chunk
    keyed, valued = rows_spec(chunk, chunks, KEYS), rows_spec(chunk, chunks, VALUES)
    return pl.pallas_call(
        functools.partial(scan_forward_kernel, chunk),
        grid=(seqs, chunks),
        in_specs=packed_specs(chunk, chunks)[:3] * 2 + [keyed],
        out_specs=[
            valued,
            keyed,
            chunk_spec(chunks, (HEADS, chunk, chunk)),
            chunk_spec(chunks, (HEADS, DV, DK)),
            chunk_spec(chunks, (1, KEYS)),
            item_spec((HEADS, DV + 8, DK)),
        ],
        out_shape=[
            shaped((rows, VALUES)),
            shaped((rows, KEYS), jnp.bfloat16),
            shaped((seqs * chunks, HEADS, chunk, chunk), jnp.bfloat16),
            shaped((seqs * chunks, HEADS, DV, DK)),
            shaped((seqs * chunks, 1, KEYS)),
            shaped((seqs, HEADS, DV + 8, DK)),
        ],
        scratch_shapes=[
            pltpu.VMEM((HEADS, DV, DK), jnp.float32),
            pltpu.VMEM((1, KEYS), jnp.float32),
            pltpu.VMEM((HEADS, chunk, chunk), jnp.float32),
        ],
        compiler_params=ROOM,
        name="scan_forward",
    )(mine, mine, mine, theirs, theirs, theirs, gates)


def scan_backward(
    mine, theirs, gates, scores, states, starts, incoming, grad_out, later, outgate_grads, seqs, chunk
):
    rows = gates.shape[0]
    chunks = rows // seqs // chunk
    keyed, valued = rows_spec(chunk, chunks, KEYS, True), rows_spec(chunk, chunks, VALUES, True)
    return pl.pallas_call(
        functools.partial(scan_backward_kernel, chunk),
        grid=(seqs, chunks),
        in_specs=[
            *packed_specs(chunk, chunks, True)[:3] * 2,
            keyed,
            chunk_spec(chunks, (HEADS, chunk, chunk), True),
            chunk_spec(chunks, (HEADS, DV, DK), True),
            chunk_spec(chunks, (1, KEYS), True),
            item_spec((HEADS, DV, DK)),
            valued,
            item_spec((HEADS, DV, DK)),
            *[rows_spec(chunk, chunks, VALUES // 2, True)] * 2,
        ],
        out_specs=[*[rows_spec(chunk, chunks, PACKED, True)] * 2, keyed],
        out_shape=[*[shaped((rows, PACKED), jnp.bfloat16)] * 2, shaped((rows, KEYS))],
        scratch_shapes=[pltpu.VMEM((HEADS, DV, DK), jnp.float32)] + [pltpu.VMEM((chunk, KEYS), jnp.float32)] * 3,
        compiler_params=ROOM,
        name="scan_backward",
    )(
        mine, mine, mine, theirs, theirs, theirs,
        gates, scores, states, starts, incoming, grad_out, later, *outgate_grads,
    )


def mix_forward(local_out, forget, incoming, mine, theirs, gain, seqs, chunk):
    rows = local_out.shape[0]
    chunks = rows // seqs // chunk
    keyed, valued = rows_spec(chunk, chunks, KEYS), rows_spec(chunk, chunks, VALUES)
    whole_gain = pl.BlockSpec((1, DV), lambda s, c: (0, 0))
    return pl.pallas_call(
        mix_forward_kernel,
        grid=(seqs, chunks),
        in_specs=[valued, keyed, item_spec((HEADS, DV, DK)), *packed_specs(chunk, chunks)[3:] * 2, whole_gain],
        out_specs=[valued, valued],
        out_shape=[shaped((rows, VALUES)), shaped((rows, VALUES), jnp.bfloat16)],
        compiler_params=ROOM,
        name="mix_forward",
    )(local_out, forget, incoming, mine, theirs, gain)


def mix_backward(mixed_grad, attended, mine, theirs, gain, forget, seqs, chunk):
    rows = attended.shape[0]
    chunks = rows // seqs // chunk
    keyed, valued = rows_spec(chunk, chunks, KEYS), rows_spec(chunk, chunks, VALUES)
    whole_gain = pl.BlockSpec((1, DV), lambda s, c: (0, 0))
    return pl.pallas_call(
        mix_backward_kernel,
        grid=(seqs, chunks),
        in_specs=[valued, valued, *packed_specs(chunk, chunks)[3:] * 2, whole_gain, keyed],
        out_specs=[
            valued,
            *[rows_spec(chunk, chunks, VALUES // 2)] * 2,
            item_spec((HEADS, DV, DK)),
            item_spec((1, DV)),
        ],
        out_shape=[
            shaped((rows, VALUES)),
            *[shaped((rows, VALUES // 2), jnp.bfloat16)] * 2,
            shaped((seqs, HEADS, DV, DK)),
            shaped((seqs, 1, DV)),
        ],
        compiler_params=ROOM,
        name="mix_backward",
    )(mixed_grad, attended, mine, theirs, gain, forget)


def from_neighbours(summary, step):
    count = lax.axis_size("seq")
    total, factor = None, None
    for distance in range(1, count):
        shift = step * distance
        pairs = [(i, i + shift) for i in range(count) if 0 <= i + shift < count]
        came = lax.ppermute(summary, "seq", pairs)
        state, retain = came[:, :, :DV].astype(jnp.float32), came[:, :, DV : DV + 1].astype(jnp.float32)
        if total is None:
            total, factor = state, retain
        else:
            total, factor = total + factor * state, factor * retain
    return total


def product(left, right):
    return jnp.dot(left, right, preferred_element_type=jnp.float32)


def product_left(left, right):
    return lax.dot_general(
        left, right, (((0,), (0,)), ((), ())), preferred_element_type=jnp.float32
    )


def product_right(left, right):
    return lax.dot_general(
        left, right, (((1,), (1,)), ((), ())), preferred_element_type=jnp.float32
    )


EVERYWHERE = ("z", "core", "seq")


def swapped(array):
    return lax.ppermute(array, "core", [(0, 1), (1, 0)])


def after(array, other):
    def nothing(array_ref, other_ref, out_ref):
        pass

    anywhere = pl.BlockSpec(memory_space=pl.ANY)
    return pl.pallas_call(
        nothing,
        in_specs=[anywhere, anywhere],
        out_specs=anywhere,
        out_shape=shaped(array.shape, array.dtype),
        input_output_aliases={0: 0},
        name="after",
    )(array, other)


def first_core():
    return lax.axis_index("core") == 0


def own_half(array, dim, other=False):
    core = lax.axis_index("core")
    size = array.shape[dim] // 2
    return lax.dynamic_slice_in_dim(array, ((1 - core) if other else core) * size, size, dim)


def joined(mine, theirs, dim):
    return jnp.where(
        first_core(), jnp.concatenate([mine, theirs], dim), jnp.concatenate([theirs, mine], dim)
    )


def halves_of(array):
    half = array.shape[1] // 2
    first = first_core()
    return (
        jnp.where(first, array[:, :half], array[:, half:]),
        jnp.where(first, array[:, half:], array[:, :half]),
    )


def scattered(array):
    return lax.psum_scatter(array, "seq", scatter_dimension=0, tiled=True)


def line_sum(array):
    count, me = lax.axis_size("z"), lax.axis_index("z")
    if count % 2:
        return (lax.psum(array, "z"),) * 2
    middle = count // 2
    total = array

    def send(pairs):
        return lax.ppermute(total, "z", pairs)

    for step in range(middle - 1):
        came = send([(step, step + 1), (count - 1 - step, count - 2 - step)])
        total = low(total.astype(jnp.float32) + came.astype(jnp.float32))
    came = send([(middle - 1, middle), (middle, middle - 1)])
    total = low(total.astype(jnp.float32) + came.astype(jnp.float32))
    at_middle = total
    for step in reversed(range(middle - 1)):
        came = send([(step + 1, step), (count - 2 - step, count - 1 - step)])
        total = jnp.where((me == step) | (me == count - 1 - step), came, total)
    return total, at_middle


def local(
    tokens,
    mixer_gain,
    query_weight,
    key_weight,
    value_weight,
    decay_down,
    decay_up,
    decay_bias,
    outgate_weight,
    head_gain,
    output_weight,
    channel_gain,
    gate_weight,
    up_weight,
    down_weight,
    cotangent,
):
    seqs_here, seg_len, width = tokens.shape
    rows_here = seqs_here * seg_len
    count = lax.axis_size("seq")
    ff = gate_weight.shape[1]

    shard_rows = query_weight.shape[0]
    smalls = [mixer_gain, decay_down, decay_up, decay_bias, head_gain, channel_gain]
    flat = jnp.concatenate([small.reshape(-1) for small in smalls])
    flat_size = flat.size
    extra = -(-flat_size // (shard_rows * 128)) * 128
    flat = jnp.pad(flat, (0, shard_rows * extra - flat_size)).reshape(shard_rows, extra)
    mixer_packed = jnp.concatenate(
        [
            own_half(weight, 1)
            for weight in (query_weight, key_weight, value_weight, outgate_weight, output_weight)
        ]
        + [flat],
        axis=1,
    )
    ffn_packed = jnp.concatenate([own_half(gate_weight, 1), own_half(up_weight, 1)], axis=1)
    down_packed = own_half(down_weight, 1)
    wide = PACKED + width // 2
    mixer_mine = lax.all_gather(mixer_packed, "seq", tiled=True)
    ffn_mine = lax.all_gather(ffn_packed, "seq", tiled=True)
    down_mine = lax.all_gather(down_packed, "seq", tiled=True)
    mixer_theirs = swapped(mixer_mine)
    projection_mine, projection_theirs = mixer_mine[:, :PACKED], mixer_theirs[:, :PACKED]
    output_mine, output_theirs = mixer_mine[:, PACKED:wide], mixer_theirs[:, PACKED:wide]
    small_all = mixer_mine[:, wide:].reshape(count, -1)
    pieces, begin = [], 0
    for small in smalls:
        pieces.append(small_all[:, begin : begin + small.size].reshape((count,) + small.shape))
        begin += small.size
    gain_one = pieces[0].reshape(-1).astype(jnp.float32)
    decay_down_all = pieces[1].reshape(width, -1)
    decay_up_f = pieces[2].transpose(1, 0, 2).reshape(decay_up.shape[0], -1).astype(jnp.float32)
    decay_bias_f = pieces[3].reshape(1, -1).astype(jnp.float32)
    head_gain_f = pieces[4].reshape(-1).astype(jnp.float32)
    gain_two = pieces[5].reshape(-1).astype(jnp.float32)
    decay_up_f = jnp.concatenate(halves_of(decay_up_f), 1)
    decay_bias_f = jnp.concatenate(halves_of(decay_bias_f), 1)

    inputs = tokens.reshape(rows_here, width).astype(jnp.float32)

    def first_norm(inputs_in, gain_in):
        return normalize(inputs_in) * gain_in

    normed_one = first_norm(inputs, gain_one).astype(jnp.bfloat16)
    low_rank = product(normed_one, decay_down_all)

    def gate_fn(rank_in, up_in, bias_in):
        return (
            jax.nn.log_sigmoid(jnp.dot(rank_in, up_in, precision=highest_precision) + bias_in)
            / normalizer
        )

    gates = gate_fn(low_rank, decay_up_f, decay_bias_f)
    mine = product(normed_one, projection_mine)
    theirs = product(normed_one, projection_theirs)
    chunk = min(CHUNK, seg_len)
    local_out, forget, scores, states, starts, summary = scan_forward(mine, theirs, gates, seqs_here, chunk)
    incoming_state = from_neighbours(summary, 1)
    attended, mixed = mix_forward(
        local_out, forget, incoming_state, mine, theirs, head_gain_f[None, :], seqs_here, chunk
    )
    ffn_mine = after(ffn_mine, mixed)
    mixed = jnp.concatenate(halves_of(mixed), 1)
    resid = inputs + joined(product(mixed, output_mine), product(mixed, output_theirs), 1)
    normed_two = first_norm(resid, gain_two).astype(jnp.bfloat16)
    ffn_theirs = swapped(ffn_mine)

    def swiglu(both):
        gate_pre, up_pre = both[:, : ff // 2], both[:, ff // 2 :]
        return low(gate_pre * jax.nn.sigmoid(gate_pre) * up_pre)

    both_mine, both_theirs = product(normed_two, ffn_mine), product(normed_two, ffn_theirs)
    hidden = joined(swiglu(both_mine), swiglu(both_theirs), 1)
    down_mine = after(down_mine, normed_two)
    down_theirs = swapped(down_mine)
    result = resid + joined(product(hidden, down_mine), product(hidden, down_theirs), 1)
    block_out = result.astype(jnp.bfloat16).reshape(tokens.shape)

    grad_low = cotangent.reshape(rows_here, width)
    grad_out = grad_low.astype(jnp.float32)
    low_mine, low_theirs = halves_of(grad_low)
    down_came = swapped(low(product_left(hidden, low_theirs)))
    hidden_grad = product_right(low_mine, down_mine) + product_right(low_theirs, down_theirs)

    def swiglu_back(both, grad):
        gate_pre, up_pre = both[:, : ff // 2], both[:, ff // 2 :]
        sigma = jax.nn.sigmoid(gate_pre)
        return jnp.concatenate(
            [
                low(grad * up_pre * (sigma + gate_pre * sigma * (1.0 - sigma))),
                low(grad * (gate_pre * sigma)),
            ],
            axis=1,
        )

    grad_mine, grad_theirs = halves_of(hidden_grad)
    back_mine, back_theirs = swiglu_back(both_mine, grad_mine), swiglu_back(both_theirs, grad_theirs)
    down_pair = low(product_left(hidden, low_mine) + down_came.astype(jnp.float32))
    down_share = scattered(down_pair)

    ffn_came = swapped(low(product_left(normed_two, back_theirs)))
    normed_two_grad = product_right(back_mine, ffn_mine) + product_right(back_theirs, ffn_theirs)
    norm_pulled = jax.vjp(first_norm, resid, gain_two)[1](normed_two_grad)
    resid_grad = grad_out + norm_pulled[0]
    channel_gain_grad = norm_pulled[1]
    branch_grad = resid_grad.astype(jnp.bfloat16)
    branch_mine, branch_theirs = halves_of(branch_grad)
    mixed_grad = product_right(branch_mine, output_mine) + product_right(branch_theirs, output_theirs)
    mixed_grad = jnp.concatenate(halves_of(mixed_grad), 1)
    ffn_pair = low(product_left(normed_two, back_mine) + ffn_came.astype(jnp.float32))
    ffn_share = scattered(ffn_pair)
    mixed_grad = after(mixed_grad, ffn_pair)

    attended_grad, *outgate_grads, state_grad, head_gain_grad = mix_backward(
        mixed_grad, attended, mine, theirs, head_gain_f[None, :], forget, seqs_here, chunk
    )
    head_gain_grad = head_gain_grad.sum((0, 1))
    later_grad = from_neighbours(
        jnp.concatenate([state_grad, summary[:, :, DV:]], axis=2).astype(jnp.bfloat16), -1
    )
    packed_mine, packed_theirs, gates_grad = scan_backward(
        mine, theirs, gates, scores, states, starts, incoming_state,
        attended_grad, later_grad, outgate_grads, seqs_here, chunk,
    )
    output_theirs_grad = low(product_left(mixed, branch_theirs))
    packed_came = swapped(
        jnp.concatenate([low(product_left(normed_one, packed_theirs)), output_theirs_grad], axis=1)
    ).astype(jnp.float32)
    gate_pulled = jax.vjp(gate_fn, low_rank, decay_up_f, decay_bias_f)[1](gates_grad)
    low_rank_grad = gate_pulled[0].astype(jnp.bfloat16)
    decay_up_grad = jnp.concatenate(halves_of(gate_pulled[1]), 1)
    decay_bias_grad = jnp.concatenate(halves_of(gate_pulled[2]), 1)[0]
    decay_down_grad = product_left(normed_one, low_rank_grad)
    normed_one_grad = (
        product_right(packed_mine, projection_mine)
        + product_right(packed_theirs, projection_theirs)
        + product_right(low_rank_grad, decay_down_all)
    )
    first_pulled = jax.vjp(first_norm, inputs, gain_one)[1](normed_one_grad)
    tokens_grad = (resid_grad + first_pulled[0]).reshape(tokens.shape)

    def by_shard(grad, dim=0):
        shape = grad.shape[:dim] + (count, grad.shape[dim] // count) + grad.shape[dim + 1 :]
        return jnp.moveaxis(grad.reshape(shape), dim, 0).reshape(count, -1)

    small_grads = jnp.concatenate(
        [
            by_shard(first_pulled[1]),
            by_shard(decay_down_grad),
            by_shard(decay_up_grad, 1),
            by_shard(decay_bias_grad),
            by_shard(head_gain_grad),
            by_shard(channel_gain_grad),
        ],
        axis=1,
    )
    small_grads = jnp.pad(low(small_grads), ((0, 0), (0, shard_rows * extra - flat_size)))
    mixer_pair = jnp.concatenate(
        [
            low(product_left(normed_one, packed_mine) + packed_came[:, :PACKED]),
            low(product_left(mixed, branch_mine) + packed_came[:, PACKED:]),
            small_grads.reshape(count * shard_rows, extra),
        ],
        axis=1,
    )
    mixer_share = scattered(mixer_pair)

    down_total, down_middle = line_sum(down_share)
    down_weight_grad = joined(down_total, swapped(down_total), 1).astype(jnp.float32)
    ffn_total, ffn_middle = line_sum(after(ffn_share, down_middle))
    ffn_other = swapped(ffn_total)
    mixer_total, _ = line_sum(after(mixer_share, ffn_middle))
    mixer_other = swapped(mixer_total)

    def both_cores(total, other, begin, end):
        return joined(total[:, begin:end], other[:, begin:end], 1).astype(jnp.float32)

    summed = mixer_total[:, wide:].astype(jnp.float32) + mixer_other[:, wide:].astype(jnp.float32)
    summed, shares, begin = summed.reshape(-1), [], 0
    for small in smalls:
        shares.append(summed[begin : begin + small.size].reshape(small.shape))
        begin += small.size

    columns = (0, KEYS // 2, KEYS, KEYS + VALUES // 2, PACKED, wide)
    query_g, key_g, value_g, outgate_g, output_g = (
        both_cores(mixer_total, mixer_other, a, b) for a, b in zip(columns[:-1], columns[1:])
    )
    return (
        block_out,
        tokens_grad,
        shares[0],
        query_g,
        key_g,
        value_g,
        shares[1],
        shares[2],
        shares[3],
        outgate_g,
        shares[4],
        output_g,
        shares[5],
        both_cores(ffn_total, ffn_other, 0, ff // 2),
        both_cores(ffn_total, ffn_other, ff // 2, ff),
        down_weight_grad,
    )


def solution(mesh):
    rep, seq = mesh.shape["rep"], mesh.shape["seq"]
    cores = Mesh(mesh.devices.reshape(rep // 2, 2, seq), EVERYWHERE)
    sequences, weights = P(("z", "core"), "seq", None), P("seq", None)
    in_specs = (
        sequences,
        P("seq"),
        weights,
        weights,
        weights,
        weights,
        P(None, "seq"),
        P("seq"),
        weights,
        P("seq"),
        weights,
        P("seq"),
        weights,
        weights,
        weights,
        sequences,
    )
    out_specs = (sequences, *in_specs[:15])
    return jax.shard_map(local, mesh=cores, in_specs=in_specs, out_specs=out_specs, check_vma=False)
```

```python
import functools

import jax
import jax.numpy as jnp
from jax import lax
from jax.experimental import pallas as pl
from jax.experimental.pallas import tpu as pltpu
from jax.sharding import Mesh, PartitionSpec as P

HEADS = 4
DK = 128
DV = 256
PAIR = HEADS // 2
CHUNK = 128
SAFE = 60.0


epsilon = 1e-06
normalizer = 16.0
highest_precision = lax.Precision.HIGHEST


def normalize(values_in):
    return values_in * lax.rsqrt(jnp.mean(values_in * values_in, axis=-1, keepdims=True) + epsilon)


def dot_nn(left, right):
    return lax.dot_general(left, right, (((1,), (0,)), ((), ())), preferred_element_type=jnp.float32)


def dot_nt(left, right):
    return lax.dot_general(left, right, (((1,), (1,)), ((), ())), preferred_element_type=jnp.float32)


def dot_tn(left, right):
    return lax.dot_general(left, right, (((0,), (0,)), ((), ())), preferred_element_type=jnp.float32)


def low(array):
    return array.astype(jnp.bfloat16)


def exact_sum(selector, array):
    high = low(array)
    rest = low(array - high.astype(jnp.float32))
    return dot_nn(selector, high) + dot_nn(selector, rest)


def halves(array):
    high = low(array)
    return high, low(array - high.astype(jnp.float32))


def close_dot(dot, left, right):
    (left_high, left_rest), (right_high, right_rest) = halves(left), halves(right)
    return dot(left_high, right_high) + (dot(left_high, right_rest) + dot(left_rest, right_high))


def at_head(refs, head, size):
    place = head % PAIR
    return refs[head // PAIR][:, place * size : (place + 1) * size]


def positions(chunk):
    row = lax.broadcasted_iota(jnp.int32, (chunk, chunk), 0)
    column = lax.broadcasted_iota(jnp.int32, (chunk, chunk), 1)
    return row, column


def as_selector(mask):
    return low(jnp.where(mask, 1.0, 0.0))


def halvings(chunk):
    sizes, half = [], chunk // 2
    while half >= 1:
        sizes.append(half)
        half //= 2
    return sizes


def halving_parts(chunk, half):
    row, column = positions(chunk)
    row_late = (row & half) != 0
    pairs = ((row & -(2 * half)) == (column & -(2 * half))) & row_late & ((column & half) == 0)
    middle = (row & -(2 * half)) + (half - 1)
    late = row_late & (column > middle) & (column <= row)
    early = jnp.logical_not(row_late) & (column > row) & (column <= middle)
    return pairs, as_selector(late | early)


def scan_forward_kernel(chunk, q0, k0, v0, q1, k1, v1, g_ref, o_ref, qf_ref, a_ref, st_ref, cs_ref, sum_ref, state, start, table):
    step, steps = pl.program_id(1), pl.num_programs(1)
    q_refs, k_refs, v_refs = (q0, q1), (k0, k1), (v0, v1)

    @pl.when(step == 0)
    def _():
        state[...] = jnp.zeros_like(state)
        start[...] = jnp.zeros_like(start)

    row, column = positions(chunk)
    gates = g_ref[...]
    cumul = exact_sum(as_selector(row >= column), gates)
    left = exact_sum(as_selector(row < column), gates)
    finish = cumul[chunk - 1 : chunk, :]
    mild = jnp.min(finish) > -SAFE
    begin = start[...]
    cs_ref[0] = begin
    grown = jnp.exp(cumul)
    faded = jnp.exp(left)
    begun = jnp.exp(begin)
    kept = jnp.exp(finish)
    scale = DK ** (-0.5)

    @pl.when(mild)
    def _():
        for h in range(HEADS):
            ks = slice(h * DK, (h + 1) * DK)
            far = at_head(q_refs, h, DK) * scale * grown[:, ks]
            near = at_head(k_refs, h, DK) * jnp.exp(-cumul[:, ks])
            table[h] = jnp.where(row >= column, close_dot(dot_nt, far, near), 0.0)

    @pl.when(jnp.logical_not(mild))
    def _():
        for h in range(HEADS):
            ks = slice(h * DK, (h + 1) * DK)
            queries, keys, decay = at_head(q_refs, h, DK) * scale, at_head(k_refs, h, DK), g_ref[:, ks]
            total = jnp.where(row == column, close_dot(dot_nt, queries, keys), 0.0)
            for half in halvings(chunk):
                pairs, selector = halving_parts(chunk, half)
                factor = jnp.exp(exact_sum(selector, decay))
                total = jnp.where(pairs, close_dot(dot_nt, queries * factor, keys * factor), total)
            table[h] = total

    for h in range(HEADS):
        ks, vs = slice(h * DK, (h + 1) * DK), slice(h * DV, (h + 1) * DV)
        queries = at_head(q_refs, h, DK) * scale * grown[:, ks]
        own_values = at_head(v_refs, h, DV)
        values = low(own_values)
        held = state[h]
        st_ref[0, h] = held
        scores = table[h]
        a_ref[0, h] = low(scores)
        o_ref[:, vs] = close_dot(dot_nn, scores, own_values) + dot_nt(low(queries), low(held))
        qf_ref[:, ks] = low(queries * begun[:, ks])
        state[h] = held * kept[:, ks] + dot_tn(values, low(at_head(k_refs, h, DK) * faded[:, ks]))
    start[...] = begin + finish

    @pl.when(step == steps - 1)
    def _():
        for h in range(HEADS):
            ks = slice(h * DK, (h + 1) * DK)
            sum_ref[0, h, :DV] = state[h]
            sum_ref[0, h, DV:] = jnp.broadcast_to(jnp.exp(begin[:, ks] + finish[:, ks]), (8, DK))


def scan_backward_kernel(
    chunk, q0, k0, v0, q1, k1, v1, g_ref, a_ref, st_ref, cs_ref, in_ref, do_ref, later_ref, dog0, dog1,
    out0, out1, dg_ref, later, dqi, dki, dci,
):
    q_refs, k_refs, v_refs = (q0, q1), (k0, k1), (v0, v1)

    @pl.when(pl.program_id(1) == 0)
    def _():
        later[...] = later_ref[0]

    row, column = positions(chunk)
    lower = row >= column
    gates = g_ref[...]
    cumul = exact_sum(as_selector(lower), gates)
    left = exact_sum(as_selector(row < column), gates)
    finish = cumul[chunk - 1 : chunk, :]
    mild = jnp.min(finish) > -SAFE
    grown = jnp.exp(cumul)
    faded = jnp.exp(left)
    kept = jnp.exp(finish)
    begun = jnp.exp(cs_ref[0])
    scale = DK ** (-0.5)

    def overlap(h, vs):
        return close_dot(dot_nt, do_ref[:, vs], at_head(v_refs, h, DV))

    @pl.when(mild)
    def _():
        for h in range(HEADS):
            ks, vs = slice(h * DK, (h + 1) * DK), slice(h * DV, (h + 1) * DV)
            shrunk = jnp.exp(-cumul[:, ks])
            far = low(at_head(q_refs, h, DK) * scale * grown[:, ks])
            near = low(at_head(k_refs, h, DK) * shrunk)
            pairs = low(jnp.where(lower, overlap(h, vs), 0.0))
            for_q, for_k = dot_nn(pairs, near), dot_tn(pairs, far)
            dqi[:, ks] = grown[:, ks] * for_q
            dki[:, ks] = shrunk * for_k
            dci[:, ks] = far.astype(jnp.float32) * for_q - near.astype(jnp.float32) * for_k

    @pl.when(jnp.logical_not(mild))
    def _():
        for h in range(HEADS):
            ks, vs = slice(h * DK, (h + 1) * DK), slice(h * DV, (h + 1) * DV)
            queries, keys, decay = at_head(q_refs, h, DK) * scale, at_head(k_refs, h, DK), g_ref[:, ks]
            both = overlap(h, vs)
            pairs = low(jnp.where(row == column, both, 0.0))
            grad_q, grad_k = dot_nn(pairs, low(keys)), dot_tn(pairs, low(queries))
            grad_c = jnp.zeros_like(grad_q)
            for half in halvings(chunk):
                here, selector = halving_parts(chunk, half)
                factor = jnp.exp(exact_sum(selector, decay))
                far, near = low(queries * factor), low(keys * factor)
                pairs = low(jnp.where(here, both, 0.0))
                for_q, for_k = dot_nn(pairs, near), dot_tn(pairs, far)
                grad_q += factor * for_q
                grad_k += factor * for_k
                grad_c += far.astype(jnp.float32) * for_q - near.astype(jnp.float32) * for_k
            dqi[:, ks] = grad_q
            dki[:, ks] = grad_k
            dci[:, ks] = grad_c

    before = as_selector(row > column)
    after = as_selector(row <= column)
    for h in range(HEADS):
        ks, vs = slice(h * DK, (h + 1) * DK), slice(h * DV, (h + 1) * DV)
        values, grad_out = low(at_head(v_refs, h, DV)), low(do_ref[:, vs])
        held = st_ref[0, h] + in_ref[0, h] * begun[:, ks]
        ahead = later[h]
        ahead_low = low(ahead)
        queries = at_head(q_refs, h, DK) * scale * grown[:, ks]
        keys = at_head(k_refs, h, DK) * faded[:, ks]
        out_ref, place = (out0, out1)[h // PAIR], h % PAIR
        from_state = dot_nn(grad_out, low(held))
        from_later = dot_nn(values, ahead_low)
        out_ref[:, place * DK : (place + 1) * DK] = low((dqi[:, ks] + grown[:, ks] * from_state) * scale)
        out_ref[:, KEYS // 2 + place * DK : KEYS // 2 + (place + 1) * DK] = low(dki[:, ks] + faded[:, ks] * from_later)
        out_ref[:, KEYS + place * DV : KEYS + (place + 1) * DV] = low(
            dot_tn(a_ref[0, h], grad_out) + dot_nt(low(keys), ahead_low)
        )
        through = kept[:, ks] * jnp.sum(held * ahead, axis=0, keepdims=True)
        dg_ref[:, ks] = (
            exact_sum(after, dci[:, ks] + queries * from_state)
            + exact_sum(before, keys * from_later)
            + through
        )
        later[h] = ahead * kept[:, ks] + dot_tn(grad_out, low(queries))
    out0[:, KEYS + VALUES // 2 :] = dog0[...]
    out1[:, KEYS + VALUES // 2 :] = dog1[...]


def mix_forward_kernel(o_ref, qf_ref, in_ref, og0, og1, gain_ref, att_ref, mixed_ref):
    gain = gain_ref[...]
    for h in range(HEADS):
        ks, vs = slice(h * DK, (h + 1) * DK), slice(h * DV, (h + 1) * DV)
        attended = o_ref[:, vs] + dot_nt(qf_ref[:, ks], low(in_ref[0, h]))
        att_ref[:, vs] = attended
        outgate = at_head((og0, og1), h, DV)
        mixed_ref[:, vs] = low(normalize(attended) * gain * (outgate * jax.nn.sigmoid(outgate)))


def mix_backward_kernel(dm_ref, att_ref, og0, og1, gain_ref, qf_ref, do_ref, dog0, dog1, grad_ref, dgain_ref):
    @pl.when(pl.program_id(1) == 0)
    def _():
        grad_ref[...] = jnp.zeros_like(grad_ref)
        dgain_ref[...] = jnp.zeros_like(dgain_ref)

    gain = gain_ref[...]
    for h in range(HEADS):
        ks, vs = slice(h * DK, (h + 1) * DK), slice(h * DV, (h + 1) * DV)
        attended, outgate, grad = att_ref[:, vs], at_head((og0, og1), h, DV), dm_ref[:, vs]
        dog_ref, place = (dog0, dog1)[h // PAIR], h % PAIR
        inverse = lax.rsqrt(jnp.mean(attended * attended, axis=-1, keepdims=True) + epsilon)
        normed = attended * inverse
        sigma = jax.nn.sigmoid(outgate)
        gated = grad * (outgate * sigma)
        dog_ref[:, place * DV : (place + 1) * DV] = low(grad * normed * gain * (sigma + outgate * sigma * (1.0 - sigma)))
        dgain_ref[0] += jnp.sum(gated * normed, axis=0, keepdims=True)
        inner = gated * gain
        result = inverse * (inner - normed * jnp.mean(inner * normed, axis=-1, keepdims=True))
        do_ref[:, vs] = result
        grad_ref[0, h] += dot_tn(low(result), qf_ref[:, ks])


def rows_spec(chunk, chunks, width, backward=False):
    if backward:
        return pl.BlockSpec((chunk, width), lambda s, c: (s * chunks + chunks - 1 - c, 0))
    return pl.BlockSpec((chunk, width), lambda s, c: (s * chunks + c, 0))


def item_spec(shape):
    return pl.BlockSpec((1,) + shape, lambda s, c: (s,) + (0,) * len(shape))


def chunk_spec(chunks, shape, backward=False):
    if backward:
        return pl.BlockSpec((1,) + shape, lambda s, c: (s * chunks + chunks - 1 - c,) + (0,) * len(shape))
    return pl.BlockSpec((1,) + shape, lambda s, c: (s * chunks + c,) + (0,) * len(shape))


def shaped(shape, kind=jnp.float32):
    return jax.ShapeDtypeStruct(shape, kind)


def packed_specs(chunk, chunks, backward=False):
    def at(width, place):
        whole = rows_spec(chunk, chunks, width, backward)
        return pl.BlockSpec(whole.block_shape, lambda s, c: (whole.index_map(s, c)[0], place))

    return [at(KEYS // 2, 0), at(KEYS // 2, 1), at(VALUES // 2, 1), at(VALUES // 2, 2)]


KEYS, VALUES = HEADS * DK, HEADS * DV
PACKED = KEYS + VALUES
ROOM = pltpu.CompilerParams(vmem_limit_bytes=40 * 1024 * 1024)


def scan_forward(mine, theirs, gates, seqs, chunk):
    rows = gates.shape[0]
    chunks = rows // seqs // chunk
    keyed, valued = rows_spec(chunk, chunks, KEYS), rows_spec(chunk, chunks, VALUES)
    return pl.pallas_call(
        functools.partial(scan_forward_kernel, chunk),
        grid=(seqs, chunks),
        in_specs=packed_specs(chunk, chunks)[:3] * 2 + [keyed],
        out_specs=[
            valued,
            keyed,
            chunk_spec(chunks, (HEADS, chunk, chunk)),
            chunk_spec(chunks, (HEADS, DV, DK)),
            chunk_spec(chunks, (1, KEYS)),
            item_spec((HEADS, DV + 8, DK)),
        ],
        out_shape=[
            shaped((rows, VALUES)),
            shaped((rows, KEYS), jnp.bfloat16),
            shaped((seqs * chunks, HEADS, chunk, chunk), jnp.bfloat16),
            shaped((seqs * chunks, HEADS, DV, DK)),
            shaped((seqs * chunks, 1, KEYS)),
            shaped((seqs, HEADS, DV + 8, DK)),
        ],
        scratch_shapes=[
            pltpu.VMEM((HEADS, DV, DK), jnp.float32),
            pltpu.VMEM((1, KEYS), jnp.float32),
            pltpu.VMEM((HEADS, chunk, chunk), jnp.float32),
        ],
        compiler_params=ROOM,
        name="scan_forward",
    )(mine, mine, mine, theirs, theirs, theirs, gates)


def scan_backward(
    mine, theirs, gates, scores, states, starts, incoming, grad_out, later, outgate_grads, seqs, chunk
):
    rows = gates.shape[0]
    chunks = rows // seqs // chunk
    keyed, valued = rows_spec(chunk, chunks, KEYS, True), rows_spec(chunk, chunks, VALUES, True)
    return pl.pallas_call(
        functools.partial(scan_backward_kernel, chunk),
        grid=(seqs, chunks),
        in_specs=[
            *packed_specs(chunk, chunks, True)[:3] * 2,
            keyed,
            chunk_spec(chunks, (HEADS, chunk, chunk), True),
            chunk_spec(chunks, (HEADS, DV, DK), True),
            chunk_spec(chunks, (1, KEYS), True),
            item_spec((HEADS, DV, DK)),
            valued,
            item_spec((HEADS, DV, DK)),
            *[rows_spec(chunk, chunks, VALUES // 2, True)] * 2,
        ],
        out_specs=[*[rows_spec(chunk, chunks, PACKED, True)] * 2, keyed],
        out_shape=[*[shaped((rows, PACKED), jnp.bfloat16)] * 2, shaped((rows, KEYS))],
        scratch_shapes=[pltpu.VMEM((HEADS, DV, DK), jnp.float32)] + [pltpu.VMEM((chunk, KEYS), jnp.float32)] * 3,
        compiler_params=ROOM,
        name="scan_backward",
    )(
        mine, mine, mine, theirs, theirs, theirs,
        gates, scores, states, starts, incoming, grad_out, later, *outgate_grads,
    )


def mix_forward(local_out, forget, incoming, mine, theirs, gain, seqs, chunk):
    rows = local_out.shape[0]
    chunks = rows // seqs // chunk
    keyed, valued = rows_spec(chunk, chunks, KEYS), rows_spec(chunk, chunks, VALUES)
    whole_gain = pl.BlockSpec((1, DV), lambda s, c: (0, 0))
    return pl.pallas_call(
        mix_forward_kernel,
        grid=(seqs, chunks),
        in_specs=[valued, keyed, item_spec((HEADS, DV, DK)), *packed_specs(chunk, chunks)[3:] * 2, whole_gain],
        out_specs=[valued, valued],
        out_shape=[shaped((rows, VALUES)), shaped((rows, VALUES), jnp.bfloat16)],
        compiler_params=ROOM,
        name="mix_forward",
    )(local_out, forget, incoming, mine, theirs, gain)


def mix_backward(mixed_grad, attended, mine, theirs, gain, forget, seqs, chunk):
    rows = attended.shape[0]
    chunks = rows // seqs // chunk
    keyed, valued = rows_spec(chunk, chunks, KEYS), rows_spec(chunk, chunks, VALUES)
    whole_gain = pl.BlockSpec((1, DV), lambda s, c: (0, 0))
    return pl.pallas_call(
        mix_backward_kernel,
        grid=(seqs, chunks),
        in_specs=[valued, valued, *packed_specs(chunk, chunks)[3:] * 2, whole_gain, keyed],
        out_specs=[
            valued,
            *[rows_spec(chunk, chunks, VALUES // 2)] * 2,
            item_spec((HEADS, DV, DK)),
            item_spec((1, DV)),
        ],
        out_shape=[
            shaped((rows, VALUES)),
            *[shaped((rows, VALUES // 2), jnp.bfloat16)] * 2,
            shaped((seqs, HEADS, DV, DK)),
            shaped((seqs, 1, DV)),
        ],
        compiler_params=ROOM,
        name="mix_backward",
    )(mixed_grad, attended, mine, theirs, gain, forget)


def from_neighbours(summary, step):
    count = lax.axis_size("seq")
    total, factor = None, None
    for distance in range(1, count):
        shift = step * distance
        pairs = [(i, i + shift) for i in range(count) if 0 <= i + shift < count]
        came = lax.ppermute(summary, "seq", pairs)
        state, retain = came[:, :, :DV].astype(jnp.float32), came[:, :, DV : DV + 1].astype(jnp.float32)
        if total is None:
            total, factor = state, retain
        else:
            total, factor = total + factor * state, factor * retain
    return total


def product(left, right):
    return jnp.dot(left, right, preferred_element_type=jnp.float32)


def product_left(left, right):
    return lax.dot_general(
        left, right, (((0,), (0,)), ((), ())), preferred_element_type=jnp.float32
    )


def product_right(left, right):
    return lax.dot_general(
        left, right, (((1,), (1,)), ((), ())), preferred_element_type=jnp.float32
    )


EVERYWHERE = ("z", "core", "seq")


def swapped(array):
    return lax.ppermute(array, "core", [(0, 1), (1, 0)])


def after(array, other):
    def nothing(array_ref, other_ref, out_ref):
        pass

    anywhere = pl.BlockSpec(memory_space=pl.ANY)
    return pl.pallas_call(
        nothing,
        in_specs=[anywhere, anywhere],
        out_specs=anywhere,
        out_shape=shaped(array.shape, array.dtype),
        input_output_aliases={0: 0},
        name="after",
    )(array, other)


def first_core():
    return lax.axis_index("core") == 0


def own_half(array, dim, other=False):
    core = lax.axis_index("core")
    size = array.shape[dim] // 2
    return lax.dynamic_slice_in_dim(array, ((1 - core) if other else core) * size, size, dim)


def joined(mine, theirs, dim):
    return jnp.where(
        first_core(), jnp.concatenate([mine, theirs], dim), jnp.concatenate([theirs, mine], dim)
    )


def halves_of(array):
    half = array.shape[1] // 2
    first = first_core()
    return (
        jnp.where(first, array[:, :half], array[:, half:]),
        jnp.where(first, array[:, half:], array[:, :half]),
    )


def scattered(array):
    return lax.psum_scatter(array, "seq", scatter_dimension=0, tiled=True)


def direct(count):
    return count in (2, 4)


def spread(array):
    count, me = lax.axis_size("seq"), lax.axis_index("seq")
    if not direct(count):
        return lax.all_gather(array, "seq", tiled=True)
    rows = array.shape[0]
    whole = jnp.zeros((count * rows, array.shape[1]), array.dtype)
    whole = lax.dynamic_update_slice_in_dim(whole, array, me * rows, 0)
    for distance in range(1, count):
        came = lax.ppermute(array, "seq", [(i, i ^ distance) for i in range(count)])
        whole = lax.dynamic_update_slice_in_dim(whole, came, (me ^ distance) * rows, 0)
    return whole


def gathered_sum(array, late):
    count, me = lax.axis_size("seq"), lax.axis_index("seq")
    if not direct(count):
        return scattered(array)
    rows = array.shape[0] // count
    total = lax.dynamic_slice_in_dim(array, me * rows, rows, 0).astype(jnp.float32)
    for distance in range(1, count):
        piece = lax.dynamic_slice_in_dim(array, (me ^ distance) * rows, rows, 0)
        came = lax.ppermute(piece, "seq", [(i, i ^ distance) for i in range(count)])
        total = total + after(came, late).astype(jnp.float32)
    return low(total)


def line_sum(array, parts, earlier=None):
    count, me = lax.axis_size("z"), lax.axis_index("z")
    if count % 2:
        return (lax.psum(array, "z"),) * 2
    middle = count // 2
    rows = array.shape[0] // parts
    totals = [array[i * rows : (i + 1) * rows] for i in range(parts)]

    def send(pairs):
        return [lax.ppermute(total, "z", pairs) for total in totals]

    def add(came):
        return [
            low(total.astype(jnp.float32) + other.astype(jnp.float32)) for total, other in zip(totals, came)
        ]

    for step in range(middle - 1):
        totals = add(send([(step, step + 1), (count - 1 - step, count - 2 - step)]))
    if earlier is not None:
        totals[0] = after(totals[0], earlier)
    totals = add(send([(middle - 1, middle), (middle, middle - 1)]))
    at_middle = totals[-1]
    for step in reversed(range(middle - 1)):
        came = send([(step + 1, step), (count - 2 - step, count - 1 - step)])
        end = (me == step) | (me == count - 1 - step)
        totals = [jnp.where(end, other, total) for total, other in zip(totals, came)]
    return jnp.concatenate(totals, 0), at_middle


def local(
    tokens,
    mixer_gain,
    query_weight,
    key_weight,
    value_weight,
    decay_down,
    decay_up,
    decay_bias,
    outgate_weight,
    head_gain,
    output_weight,
    channel_gain,
    gate_weight,
    up_weight,
    down_weight,
    cotangent,
):
    seqs_here, seg_len, width = tokens.shape
    rows_here = seqs_here * seg_len
    count = lax.axis_size("seq")
    ff = gate_weight.shape[1]

    shard_rows = query_weight.shape[0]
    smalls = [mixer_gain, decay_down, decay_up, decay_bias, head_gain, channel_gain]
    flat = jnp.concatenate([small.reshape(-1) for small in smalls])
    flat_size = flat.size
    extra = -(-flat_size // (shard_rows * 128)) * 128
    flat = jnp.pad(flat, (0, shard_rows * extra - flat_size)).reshape(shard_rows, extra)
    mixer_packed = jnp.concatenate(
        [
            own_half(weight, 1)
            for weight in (query_weight, key_weight, value_weight, outgate_weight)
        ]
        + [flat],
        axis=1,
    )
    ffn_packed = jnp.concatenate([own_half(gate_weight, 1), own_half(up_weight, 1)], axis=1)
    mixer_mine = lax.all_gather(mixer_packed, "seq", tiled=True)
    ffn_mine = lax.all_gather(ffn_packed, "seq", tiled=True)
    output_mine = spread(own_half(output_weight, 1))
    mixer_mine = after(after(mixer_mine, output_mine), ffn_packed)
    down_mine = spread(after(own_half(down_weight, 1), mixer_mine))
    mixer_theirs, output_theirs = swapped(mixer_mine), swapped(output_mine)
    projection_mine, projection_theirs = mixer_mine[:, :PACKED], mixer_theirs[:, :PACKED]
    small_all = mixer_mine[:, PACKED:].reshape(count, -1)
    pieces, begin = [], 0
    for small in smalls:
        pieces.append(small_all[:, begin : begin + small.size].reshape((count,) + small.shape))
        begin += small.size
    gain_one = pieces[0].reshape(-1).astype(jnp.float32)
    decay_down_all = pieces[1].reshape(width, -1)
    decay_up_f = pieces[2].transpose(1, 0, 2).reshape(decay_up.shape[0], -1).astype(jnp.float32)
    decay_bias_f = pieces[3].reshape(1, -1).astype(jnp.float32)
    head_gain_f = pieces[4].reshape(-1).astype(jnp.float32)
    gain_two = pieces[5].reshape(-1).astype(jnp.float32)
    decay_up_f = jnp.concatenate(halves_of(decay_up_f), 1)
    decay_bias_f = jnp.concatenate(halves_of(decay_bias_f), 1)

    inputs = tokens.reshape(rows_here, width).astype(jnp.float32)

    def first_norm(inputs_in, gain_in):
        return normalize(inputs_in) * gain_in

    normed_one = first_norm(inputs, gain_one).astype(jnp.bfloat16)
    low_rank = product(normed_one, decay_down_all)

    def gate_fn(rank_in, up_in, bias_in):
        return (
            jax.nn.log_sigmoid(jnp.dot(rank_in, up_in, precision=highest_precision) + bias_in)
            / normalizer
        )

    gates = gate_fn(low_rank, decay_up_f, decay_bias_f)
    mine = product(normed_one, projection_mine)
    theirs = product(normed_one, projection_theirs)
    chunk = min(CHUNK, seg_len)
    local_out, forget, scores, states, starts, summary = scan_forward(mine, theirs, gates, seqs_here, chunk)
    incoming_state = after(from_neighbours(low(summary), 1), down_mine)
    attended, mixed = mix_forward(
        local_out, forget, incoming_state, mine, theirs, head_gain_f[None, :], seqs_here, chunk
    )
    ffn_mine = after(ffn_mine, mixed)
    mixed = jnp.concatenate(halves_of(mixed), 1)
    resid = inputs + joined(product(mixed, output_mine), product(mixed, output_theirs), 1)
    normed_two = first_norm(resid, gain_two).astype(jnp.bfloat16)
    ffn_theirs = swapped(ffn_mine)

    def swiglu(both):
        gate_pre, up_pre = both[:, : ff // 2], both[:, ff // 2 :]
        return low(gate_pre * jax.nn.sigmoid(gate_pre) * up_pre)

    both_mine, both_theirs = product(normed_two, ffn_mine), product(normed_two, ffn_theirs)
    hidden = joined(swiglu(both_mine), swiglu(both_theirs), 1)
    down_theirs = swapped(after(down_mine, mixed))
    result = resid + joined(product(hidden, down_mine), product(hidden, down_theirs), 1)
    block_out = result.astype(jnp.bfloat16).reshape(tokens.shape)

    grad_low = cotangent.reshape(rows_here, width)
    grad_out = grad_low.astype(jnp.float32)
    low_mine, low_theirs = halves_of(grad_low)
    down_came = swapped(low(product_left(hidden, low_theirs)))
    hidden_grad = product_right(low_mine, down_mine) + product_right(low_theirs, down_theirs)

    def swiglu_back(both, grad):
        gate_pre, up_pre = both[:, : ff // 2], both[:, ff // 2 :]
        sigma = jax.nn.sigmoid(gate_pre)
        return jnp.concatenate(
            [
                low(grad * up_pre * (sigma + gate_pre * sigma * (1.0 - sigma))),
                low(grad * (gate_pre * sigma)),
            ],
            axis=1,
        )

    grad_mine, grad_theirs = halves_of(hidden_grad)
    back_mine, back_theirs = swiglu_back(both_mine, grad_mine), swiglu_back(both_theirs, grad_theirs)
    down_pair = low(product_left(hidden, low_mine) + down_came.astype(jnp.float32))

    ffn_came = swapped(low(product_left(normed_two, back_theirs)))
    normed_two_grad = product_right(back_mine, ffn_mine) + product_right(back_theirs, ffn_theirs)
    norm_pulled = jax.vjp(first_norm, resid, gain_two)[1](normed_two_grad)
    resid_grad = grad_out + norm_pulled[0]
    channel_gain_grad = norm_pulled[1]
    branch_grad = resid_grad.astype(jnp.bfloat16)
    branch_mine, branch_theirs = halves_of(branch_grad)
    mixed_grad = product_right(branch_mine, output_mine) + product_right(branch_theirs, output_theirs)
    mixed_grad = jnp.concatenate(halves_of(mixed_grad), 1)
    ffn_pair = low(product_left(normed_two, back_mine) + ffn_came.astype(jnp.float32))
    ffn_share = scattered(ffn_pair)
    mixed_grad = after(mixed_grad, ffn_pair)
    mixed_later = after(mixed, mixed_grad)
    output_came = swapped(low(product_left(mixed_later, branch_theirs)))
    output_pair = low(product_left(mixed_later, branch_mine) + output_came.astype(jnp.float32))

    attended_grad, *outgate_grads, state_grad, head_gain_grad = mix_backward(
        mixed_grad, attended, mine, theirs, head_gain_f[None, :], forget, seqs_here, chunk
    )
    head_gain_grad = head_gain_grad.sum((0, 1))
    later_grad = from_neighbours(
        jnp.concatenate([state_grad, summary[:, :, DV:]], axis=2).astype(jnp.bfloat16), -1
    )
    packed_mine, packed_theirs, gates_grad = scan_backward(
        mine, theirs, gates, scores, states, starts, incoming_state,
        attended_grad, later_grad, outgate_grads, seqs_here, chunk,
    )
    packed_came = swapped(low(product_left(normed_one, packed_theirs)))
    down_share = gathered_sum(down_pair, gates_grad)
    output_share = gathered_sum(output_pair, gates_grad)
    gate_pulled = jax.vjp(gate_fn, low_rank, decay_up_f, decay_bias_f)[1](gates_grad)
    low_rank_grad = gate_pulled[0].astype(jnp.bfloat16)
    decay_up_grad = jnp.concatenate(halves_of(gate_pulled[1]), 1)
    decay_bias_grad = jnp.concatenate(halves_of(gate_pulled[2]), 1)[0]
    decay_down_grad = product_left(normed_one, low_rank_grad)
    normed_one_grad = (
        product_right(packed_mine, projection_mine)
        + product_right(packed_theirs, projection_theirs)
        + product_right(low_rank_grad, decay_down_all)
    )
    first_pulled = jax.vjp(first_norm, inputs, gain_one)[1](normed_one_grad)
    tokens_grad = (resid_grad + first_pulled[0]).reshape(tokens.shape)

    def by_shard(grad, dim=0):
        shape = grad.shape[:dim] + (count, grad.shape[dim] // count) + grad.shape[dim + 1 :]
        return jnp.moveaxis(grad.reshape(shape), dim, 0).reshape(count, -1)

    small_grads = jnp.concatenate(
        [
            by_shard(first_pulled[1]),
            by_shard(decay_down_grad),
            by_shard(decay_up_grad, 1),
            by_shard(decay_bias_grad),
            by_shard(head_gain_grad),
            by_shard(channel_gain_grad),
        ],
        axis=1,
    )
    small_grads = jnp.pad(low(small_grads), ((0, 0), (0, shard_rows * extra - flat_size)))
    mixer_pair = jnp.concatenate(
        [
            low(product_left(normed_one, packed_mine) + packed_came.astype(jnp.float32)),
            small_grads.reshape(count * shard_rows, extra),
        ],
        axis=1,
    )
    mixer_share = scattered(mixer_pair)

    others = after(jnp.concatenate([down_share, output_share], 0), mixer_pair)
    others_total, others_middle = line_sum(others, 1)
    others_other = swapped(others_total)
    ffn_total, ffn_middle = line_sum(after(ffn_share, others_middle), 2, others_total)
    ffn_other = swapped(ffn_total)
    mixer_total, _ = line_sum(after(mixer_share, ffn_middle), 2, ffn_total)
    mixer_other = swapped(mixer_total)
    down_rows = down_weight.shape[0]

    def both_cores(total, other, begin, end):
        return joined(total[:, begin:end], other[:, begin:end], 1).astype(jnp.float32)

    summed = mixer_total[:, PACKED:].astype(jnp.float32) + mixer_other[:, PACKED:].astype(jnp.float32)
    summed, shares, begin = summed.reshape(-1), [], 0
    for small in smalls:
        shares.append(summed[begin : begin + small.size].reshape(small.shape))
        begin += small.size

    columns = (0, KEYS // 2, KEYS, KEYS + VALUES // 2, PACKED)
    query_g, key_g, value_g, outgate_g = (
        both_cores(mixer_total, mixer_other, a, b) for a, b in zip(columns[:-1], columns[1:])
    )
    return (
        block_out,
        tokens_grad,
        shares[0],
        query_g,
        key_g,
        value_g,
        shares[1],
        shares[2],
        shares[3],
        outgate_g,
        shares[4],
        joined(others_total[down_rows:], others_other[down_rows:], 1).astype(jnp.float32),
        shares[5],
        both_cores(ffn_total, ffn_other, 0, ff // 2),
        both_cores(ffn_total, ffn_other, ff // 2, ff),
        joined(others_total[:down_rows], others_other[:down_rows], 1).astype(jnp.float32),
    )


def solution(mesh):
    rep, seq = mesh.shape["rep"], mesh.shape["seq"]
    cores = Mesh(mesh.devices.reshape(rep // 2, 2, seq), EVERYWHERE)
    sequences, weights = P(("z", "core"), "seq", None), P("seq", None)
    in_specs = (
        sequences,
        P("seq"),
        weights,
        weights,
        weights,
        weights,
        P(None, "seq"),
        P("seq"),
        weights,
        P("seq"),
        weights,
        P("seq"),
        weights,
        weights,
        weights,
        sequences,
    )
    out_specs = (sequences, *in_specs[:15])
    return jax.shard_map(local, mesh=cores, in_specs=in_specs, out_specs=out_specs, check_vma=False)
```

```python
import functools

import jax
import jax.numpy as jnp
from jax import lax
from jax.experimental import pallas as pl
from jax.experimental.pallas import tpu as pltpu
from jax.sharding import Mesh, PartitionSpec as P

HEADS = 4
DK = 128
DV = 256
PAIR = HEADS // 2
CHUNK = 128
SAFE = 60.0


epsilon = 1e-06
normalizer = 16.0
highest_precision = lax.Precision.HIGHEST


def normalize(values_in):
    return values_in * lax.rsqrt(jnp.mean(values_in * values_in, axis=-1, keepdims=True) + epsilon)


def dot_nn(left, right):
    return lax.dot_general(left, right, (((1,), (0,)), ((), ())), preferred_element_type=jnp.float32)


def dot_nt(left, right):
    return lax.dot_general(left, right, (((1,), (1,)), ((), ())), preferred_element_type=jnp.float32)


def dot_tn(left, right):
    return lax.dot_general(left, right, (((0,), (0,)), ((), ())), preferred_element_type=jnp.float32)


def low(array):
    return array.astype(jnp.bfloat16)


def exact_sum(selector, array):
    high = low(array)
    rest = low(array - high.astype(jnp.float32))
    return dot_nn(selector, high) + dot_nn(selector, rest)


def halves(array):
    high = low(array)
    return high, low(array - high.astype(jnp.float32))


def close_dot(dot, left, right):
    (left_high, left_rest), (right_high, right_rest) = halves(left), halves(right)
    return dot(left_high, right_high) + (dot(left_high, right_rest) + dot(left_rest, right_high))


def at_head(refs, head, size):
    place = head % PAIR
    return refs[head // PAIR][:, place * size : (place + 1) * size]


def positions(chunk):
    row = lax.broadcasted_iota(jnp.int32, (chunk, chunk), 0)
    column = lax.broadcasted_iota(jnp.int32, (chunk, chunk), 1)
    return row, column


def as_selector(mask):
    return low(jnp.where(mask, 1.0, 0.0))


def halvings(chunk):
    sizes, half = [], chunk // 2
    while half >= 1:
        sizes.append(half)
        half //= 2
    return sizes


def halving_parts(chunk, half):
    row, column = positions(chunk)
    row_late = (row & half) != 0
    pairs = ((row & -(2 * half)) == (column & -(2 * half))) & row_late & ((column & half) == 0)
    middle = (row & -(2 * half)) + (half - 1)
    late = row_late & (column > middle) & (column <= row)
    early = jnp.logical_not(row_late) & (column > row) & (column <= middle)
    return pairs, as_selector(late | early)


def scan_forward_kernel(chunk, q0, k0, v0, q1, k1, v1, g_ref, o_ref, qf_ref, a_ref, st_ref, cs_ref, sum_ref, state, start, table):
    step, steps = pl.program_id(1), pl.num_programs(1)
    q_refs, k_refs, v_refs = (q0, q1), (k0, k1), (v0, v1)

    @pl.when(step == 0)
    def _():
        state[...] = jnp.zeros_like(state)
        start[...] = jnp.zeros_like(start)

    row, column = positions(chunk)
    gates = g_ref[...]
    cumul = exact_sum(as_selector(row >= column), gates)
    left = exact_sum(as_selector(row < column), gates)
    finish = cumul[chunk - 1 : chunk, :]
    mild = jnp.min(finish) > -SAFE
    begin = start[...]
    cs_ref[0] = begin
    grown = jnp.exp(cumul)
    faded = jnp.exp(left)
    begun = jnp.exp(begin)
    kept = jnp.exp(finish)
    scale = DK ** (-0.5)

    @pl.when(mild)
    def _():
        for h in range(HEADS):
            ks = slice(h * DK, (h + 1) * DK)
            far = at_head(q_refs, h, DK) * scale * grown[:, ks]
            near = at_head(k_refs, h, DK) * jnp.exp(-cumul[:, ks])
            table[h] = jnp.where(row >= column, close_dot(dot_nt, far, near), 0.0)

    @pl.when(jnp.logical_not(mild))
    def _():
        for h in range(HEADS):
            ks = slice(h * DK, (h + 1) * DK)
            queries, keys, decay = at_head(q_refs, h, DK) * scale, at_head(k_refs, h, DK), g_ref[:, ks]
            total = jnp.where(row == column, close_dot(dot_nt, queries, keys), 0.0)
            for half in halvings(chunk):
                pairs, selector = halving_parts(chunk, half)
                factor = jnp.exp(exact_sum(selector, decay))
                total = jnp.where(pairs, close_dot(dot_nt, queries * factor, keys * factor), total)
            table[h] = total

    for h in range(HEADS):
        ks, vs = slice(h * DK, (h + 1) * DK), slice(h * DV, (h + 1) * DV)
        queries = at_head(q_refs, h, DK) * scale * grown[:, ks]
        own_values = at_head(v_refs, h, DV)
        values = low(own_values)
        held = state[h]
        st_ref[0, h] = held
        scores = table[h]
        a_ref[0, h] = low(scores)
        o_ref[:, vs] = close_dot(dot_nn, scores, own_values) + dot_nt(low(queries), low(held))
        qf_ref[:, ks] = low(queries * begun[:, ks])
        state[h] = held * kept[:, ks] + dot_tn(values, low(at_head(k_refs, h, DK) * faded[:, ks]))
    start[...] = begin + finish

    @pl.when(step == steps - 1)
    def _():
        for h in range(HEADS):
            ks = slice(h * DK, (h + 1) * DK)
            sum_ref[0, h, :DV] = state[h]
            sum_ref[0, h, DV:] = jnp.broadcast_to(jnp.exp(begin[:, ks] + finish[:, ks]), (8, DK))


def scan_backward_kernel(
    chunk, q0, k0, v0, q1, k1, v1, g_ref, a_ref, st_ref, cs_ref, in_ref, do_ref, later_ref, dog0, dog1,
    out0, out1, dg_ref, later, dqi, dki, dci,
):
    q_refs, k_refs, v_refs = (q0, q1), (k0, k1), (v0, v1)

    @pl.when(pl.program_id(1) == 0)
    def _():
        later[...] = later_ref[0]

    row, column = positions(chunk)
    lower = row >= column
    gates = g_ref[...]
    cumul = exact_sum(as_selector(lower), gates)
    left = exact_sum(as_selector(row < column), gates)
    finish = cumul[chunk - 1 : chunk, :]
    mild = jnp.min(finish) > -SAFE
    grown = jnp.exp(cumul)
    faded = jnp.exp(left)
    kept = jnp.exp(finish)
    begun = jnp.exp(cs_ref[0])
    scale = DK ** (-0.5)

    def overlap(h, vs):
        return close_dot(dot_nt, do_ref[:, vs], at_head(v_refs, h, DV))

    @pl.when(mild)
    def _():
        for h in range(HEADS):
            ks, vs = slice(h * DK, (h + 1) * DK), slice(h * DV, (h + 1) * DV)
            shrunk = jnp.exp(-cumul[:, ks])
            far = low(at_head(q_refs, h, DK) * scale * grown[:, ks])
            near = low(at_head(k_refs, h, DK) * shrunk)
            pairs = low(jnp.where(lower, overlap(h, vs), 0.0))
            for_q, for_k = dot_nn(pairs, near), dot_tn(pairs, far)
            dqi[:, ks] = grown[:, ks] * for_q
            dki[:, ks] = shrunk * for_k
            dci[:, ks] = far.astype(jnp.float32) * for_q - near.astype(jnp.float32) * for_k

    @pl.when(jnp.logical_not(mild))
    def _():
        for h in range(HEADS):
            ks, vs = slice(h * DK, (h + 1) * DK), slice(h * DV, (h + 1) * DV)
            queries, keys, decay = at_head(q_refs, h, DK) * scale, at_head(k_refs, h, DK), g_ref[:, ks]
            both = overlap(h, vs)
            pairs = low(jnp.where(row == column, both, 0.0))
            grad_q, grad_k = dot_nn(pairs, low(keys)), dot_tn(pairs, low(queries))
            grad_c = jnp.zeros_like(grad_q)
            for half in halvings(chunk):
                here, selector = halving_parts(chunk, half)
                factor = jnp.exp(exact_sum(selector, decay))
                far, near = low(queries * factor), low(keys * factor)
                pairs = low(jnp.where(here, both, 0.0))
                for_q, for_k = dot_nn(pairs, near), dot_tn(pairs, far)
                grad_q += factor * for_q
                grad_k += factor * for_k
                grad_c += far.astype(jnp.float32) * for_q - near.astype(jnp.float32) * for_k
            dqi[:, ks] = grad_q
            dki[:, ks] = grad_k
            dci[:, ks] = grad_c

    before = as_selector(row > column)
    after = as_selector(row <= column)
    for h in range(HEADS):
        ks, vs = slice(h * DK, (h + 1) * DK), slice(h * DV, (h + 1) * DV)
        values, grad_out = low(at_head(v_refs, h, DV)), low(do_ref[:, vs])
        held = st_ref[0, h] + in_ref[0, h] * begun[:, ks]
        ahead = later[h]
        ahead_low = low(ahead)
        queries = at_head(q_refs, h, DK) * scale * grown[:, ks]
        keys = at_head(k_refs, h, DK) * faded[:, ks]
        out_ref, place = (out0, out1)[h // PAIR], h % PAIR
        from_state = dot_nn(grad_out, low(held))
        from_later = dot_nn(values, ahead_low)
        out_ref[:, place * DK : (place + 1) * DK] = low((dqi[:, ks] + grown[:, ks] * from_state) * scale)
        out_ref[:, KEYS // 2 + place * DK : KEYS // 2 + (place + 1) * DK] = low(dki[:, ks] + faded[:, ks] * from_later)
        out_ref[:, KEYS + place * DV : KEYS + (place + 1) * DV] = low(
            dot_tn(a_ref[0, h], grad_out) + dot_nt(low(keys), ahead_low)
        )
        through = kept[:, ks] * jnp.sum(held * ahead, axis=0, keepdims=True)
        dg_ref[:, ks] = (
            exact_sum(after, dci[:, ks] + queries * from_state)
            + exact_sum(before, keys * from_later)
            + through
        )
        later[h] = ahead * kept[:, ks] + dot_tn(grad_out, low(queries))
    out0[:, KEYS + VALUES // 2 :] = dog0[...]
    out1[:, KEYS + VALUES // 2 :] = dog1[...]


def mix_forward_kernel(o_ref, qf_ref, in_ref, og0, og1, gain_ref, att_ref, mixed_ref):
    gain = gain_ref[...]
    for h in range(HEADS):
        ks, vs = slice(h * DK, (h + 1) * DK), slice(h * DV, (h + 1) * DV)
        attended = o_ref[:, vs] + dot_nt(qf_ref[:, ks], low(in_ref[0, h]))
        att_ref[:, vs] = attended
        outgate = at_head((og0, og1), h, DV)
        mixed_ref[:, vs] = low(normalize(attended) * gain * (outgate * jax.nn.sigmoid(outgate)))


def mix_backward_kernel(dm_ref, att_ref, og0, og1, gain_ref, qf_ref, do_ref, dog0, dog1, grad_ref, dgain_ref):
    @pl.when(pl.program_id(1) == 0)
    def _():
        grad_ref[...] = jnp.zeros_like(grad_ref)
        dgain_ref[...] = jnp.zeros_like(dgain_ref)

    gain = gain_ref[...]
    for h in range(HEADS):
        ks, vs = slice(h * DK, (h + 1) * DK), slice(h * DV, (h + 1) * DV)
        attended, outgate, grad = att_ref[:, vs], at_head((og0, og1), h, DV), dm_ref[:, vs]
        dog_ref, place = (dog0, dog1)[h // PAIR], h % PAIR
        inverse = lax.rsqrt(jnp.mean(attended * attended, axis=-1, keepdims=True) + epsilon)
        normed = attended * inverse
        sigma = jax.nn.sigmoid(outgate)
        gated = grad * (outgate * sigma)
        dog_ref[:, place * DV : (place + 1) * DV] = low(grad * normed * gain * (sigma + outgate * sigma * (1.0 - sigma)))
        dgain_ref[0] += jnp.sum(gated * normed, axis=0, keepdims=True)
        inner = gated * gain
        result = inverse * (inner - normed * jnp.mean(inner * normed, axis=-1, keepdims=True))
        do_ref[:, vs] = result
        grad_ref[0, h] += dot_tn(low(result), qf_ref[:, ks])


def rows_spec(chunk, chunks, width, backward=False):
    if backward:
        return pl.BlockSpec((chunk, width), lambda s, c: (s * chunks + chunks - 1 - c, 0))
    return pl.BlockSpec((chunk, width), lambda s, c: (s * chunks + c, 0))


def item_spec(shape):
    return pl.BlockSpec((1,) + shape, lambda s, c: (s,) + (0,) * len(shape))


def chunk_spec(chunks, shape, backward=False):
    if backward:
        return pl.BlockSpec((1,) + shape, lambda s, c: (s * chunks + chunks - 1 - c,) + (0,) * len(shape))
    return pl.BlockSpec((1,) + shape, lambda s, c: (s * chunks + c,) + (0,) * len(shape))


def shaped(shape, kind=jnp.float32):
    return jax.ShapeDtypeStruct(shape, kind)


def packed_specs(chunk, chunks, backward=False):
    def at(width, place):
        whole = rows_spec(chunk, chunks, width, backward)
        return pl.BlockSpec(whole.block_shape, lambda s, c: (whole.index_map(s, c)[0], place))

    return [at(KEYS // 2, 0), at(KEYS // 2, 1), at(VALUES // 2, 1), at(VALUES // 2, 2)]


KEYS, VALUES = HEADS * DK, HEADS * DV
PACKED = KEYS + VALUES
ROOM = pltpu.CompilerParams(vmem_limit_bytes=40 * 1024 * 1024)


def scan_forward(mine, theirs, gates, seqs, chunk):
    rows = gates.shape[0]
    chunks = rows // seqs // chunk
    keyed, valued = rows_spec(chunk, chunks, KEYS), rows_spec(chunk, chunks, VALUES)
    return pl.pallas_call(
        functools.partial(scan_forward_kernel, chunk),
        grid=(seqs, chunks),
        in_specs=packed_specs(chunk, chunks)[:3] * 2 + [keyed],
        out_specs=[
            valued,
            keyed,
            chunk_spec(chunks, (HEADS, chunk, chunk)),
            chunk_spec(chunks, (HEADS, DV, DK)),
            chunk_spec(chunks, (1, KEYS)),
            item_spec((HEADS, DV + 8, DK)),
        ],
        out_shape=[
            shaped((rows, VALUES)),
            shaped((rows, KEYS), jnp.bfloat16),
            shaped((seqs * chunks, HEADS, chunk, chunk), jnp.bfloat16),
            shaped((seqs * chunks, HEADS, DV, DK)),
            shaped((seqs * chunks, 1, KEYS)),
            shaped((seqs, HEADS, DV + 8, DK)),
        ],
        scratch_shapes=[
            pltpu.VMEM((HEADS, DV, DK), jnp.float32),
            pltpu.VMEM((1, KEYS), jnp.float32),
            pltpu.VMEM((HEADS, chunk, chunk), jnp.float32),
        ],
        compiler_params=ROOM,
        name="scan_forward",
    )(mine, mine, mine, theirs, theirs, theirs, gates)


def scan_backward(
    mine, theirs, gates, scores, states, starts, incoming, grad_out, later, outgate_grads, seqs, chunk
):
    rows = gates.shape[0]
    chunks = rows // seqs // chunk
    keyed, valued = rows_spec(chunk, chunks, KEYS, True), rows_spec(chunk, chunks, VALUES, True)
    return pl.pallas_call(
        functools.partial(scan_backward_kernel, chunk),
        grid=(seqs, chunks),
        in_specs=[
            *packed_specs(chunk, chunks, True)[:3] * 2,
            keyed,
            chunk_spec(chunks, (HEADS, chunk, chunk), True),
            chunk_spec(chunks, (HEADS, DV, DK), True),
            chunk_spec(chunks, (1, KEYS), True),
            item_spec((HEADS, DV, DK)),
            valued,
            item_spec((HEADS, DV, DK)),
            *[rows_spec(chunk, chunks, VALUES // 2, True)] * 2,
        ],
        out_specs=[*[rows_spec(chunk, chunks, PACKED, True)] * 2, keyed],
        out_shape=[*[shaped((rows, PACKED), jnp.bfloat16)] * 2, shaped((rows, KEYS))],
        scratch_shapes=[pltpu.VMEM((HEADS, DV, DK), jnp.float32)] + [pltpu.VMEM((chunk, KEYS), jnp.float32)] * 3,
        compiler_params=ROOM,
        name="scan_backward",
    )(
        mine, mine, mine, theirs, theirs, theirs,
        gates, scores, states, starts, incoming, grad_out, later, *outgate_grads,
    )


def mix_forward(local_out, forget, incoming, mine, theirs, gain, seqs, chunk):
    rows = local_out.shape[0]
    chunks = rows // seqs // chunk
    keyed, valued = rows_spec(chunk, chunks, KEYS), rows_spec(chunk, chunks, VALUES)
    whole_gain = pl.BlockSpec((1, DV), lambda s, c: (0, 0))
    return pl.pallas_call(
        mix_forward_kernel,
        grid=(seqs, chunks),
        in_specs=[valued, keyed, item_spec((HEADS, DV, DK)), *packed_specs(chunk, chunks)[3:] * 2, whole_gain],
        out_specs=[valued, valued],
        out_shape=[shaped((rows, VALUES)), shaped((rows, VALUES), jnp.bfloat16)],
        compiler_params=ROOM,
        name="mix_forward",
    )(local_out, forget, incoming, mine, theirs, gain)


def mix_backward(mixed_grad, attended, mine, theirs, gain, forget, seqs, chunk):
    rows = attended.shape[0]
    chunks = rows // seqs // chunk
    keyed, valued = rows_spec(chunk, chunks, KEYS), rows_spec(chunk, chunks, VALUES)
    whole_gain = pl.BlockSpec((1, DV), lambda s, c: (0, 0))
    return pl.pallas_call(
        mix_backward_kernel,
        grid=(seqs, chunks),
        in_specs=[valued, valued, *packed_specs(chunk, chunks)[3:] * 2, whole_gain, keyed],
        out_specs=[
            valued,
            *[rows_spec(chunk, chunks, VALUES // 2)] * 2,
            item_spec((HEADS, DV, DK)),
            item_spec((1, DV)),
        ],
        out_shape=[
            shaped((rows, VALUES)),
            *[shaped((rows, VALUES // 2), jnp.bfloat16)] * 2,
            shaped((seqs, HEADS, DV, DK)),
            shaped((seqs, 1, DV)),
        ],
        compiler_params=ROOM,
        name="mix_backward",
    )(mixed_grad, attended, mine, theirs, gain, forget)


def from_neighbours(summary, step):
    count = lax.axis_size("seq")
    total, factor = None, None
    for distance in range(1, count):
        shift = step * distance
        pairs = [(i, i + shift) for i in range(count) if 0 <= i + shift < count]
        came = lax.ppermute(summary, "seq", pairs)
        state, retain = came[:, :, :DV].astype(jnp.float32), came[:, :, DV : DV + 1].astype(jnp.float32)
        if total is None:
            total, factor = state, retain
        else:
            total, factor = total + factor * state, factor * retain
    return total


def product(left, right):
    return jnp.dot(left, right, preferred_element_type=jnp.float32)


def product_left(left, right):
    return lax.dot_general(
        left, right, (((0,), (0,)), ((), ())), preferred_element_type=jnp.float32
    )


def product_right(left, right):
    return lax.dot_general(
        left, right, (((1,), (1,)), ((), ())), preferred_element_type=jnp.float32
    )


EVERYWHERE = ("z", "core", "seq")


def swapped(array):
    return lax.ppermute(array, "core", [(0, 1), (1, 0)])


def after(array, other):
    def nothing(array_ref, other_ref, out_ref):
        pass

    anywhere = pl.BlockSpec(memory_space=pl.ANY)
    return pl.pallas_call(
        nothing,
        in_specs=[anywhere, anywhere],
        out_specs=anywhere,
        out_shape=shaped(array.shape, array.dtype),
        input_output_aliases={0: 0},
        name="after",
    )(array, other)


def first_core():
    return lax.axis_index("core") == 0


def own_half(array, dim, other=False):
    core = lax.axis_index("core")
    size = array.shape[dim] // 2
    return lax.dynamic_slice_in_dim(array, ((1 - core) if other else core) * size, size, dim)


def joined(mine, theirs, dim):
    return jnp.where(
        first_core(), jnp.concatenate([mine, theirs], dim), jnp.concatenate([theirs, mine], dim)
    )


def halves_of(array):
    half = array.shape[1] // 2
    first = first_core()
    return (
        jnp.where(first, array[:, :half], array[:, half:]),
        jnp.where(first, array[:, half:], array[:, :half]),
    )


def scattered(array):
    return lax.psum_scatter(array, "seq", scatter_dimension=0, tiled=True)


def direct(count):
    return count in (2, 4)


def spread(array):
    count, me = lax.axis_size("seq"), lax.axis_index("seq")
    if not direct(count):
        return lax.all_gather(array, "seq", tiled=True)
    rows = array.shape[0]
    whole = jnp.zeros((count * rows, array.shape[1]), array.dtype)
    whole = lax.dynamic_update_slice_in_dim(whole, array, me * rows, 0)
    for distance in range(1, count):
        came = lax.ppermute(array, "seq", [(i, i ^ distance) for i in range(count)])
        whole = lax.dynamic_update_slice_in_dim(whole, came, (me ^ distance) * rows, 0)
    return whole


def gathered_sum(array, late):
    count, me = lax.axis_size("seq"), lax.axis_index("seq")
    if not direct(count):
        return scattered(array)
    rows = array.shape[0] // count
    total = lax.dynamic_slice_in_dim(array, me * rows, rows, 0).astype(jnp.float32)
    for distance in range(1, count):
        piece = lax.dynamic_slice_in_dim(array, (me ^ distance) * rows, rows, 0)
        came = lax.ppermute(piece, "seq", [(i, i ^ distance) for i in range(count)])
        total = total + after(came, late).astype(jnp.float32)
    return low(total)


def line_sum(array, parts, earlier=None):
    count, me = lax.axis_size("z"), lax.axis_index("z")
    if count % 2:
        return (lax.psum(array, "z"),) * 2
    middle = count // 2
    rows = array.shape[0] // parts
    totals = [array[i * rows : (i + 1) * rows] for i in range(parts)]

    def send(pairs):
        return [lax.ppermute(total, "z", pairs) for total in totals]

    def add(came):
        return [
            low(total.astype(jnp.float32) + other.astype(jnp.float32)) for total, other in zip(totals, came)
        ]

    for step in range(middle - 1):
        totals = add(send([(step, step + 1), (count - 1 - step, count - 2 - step)]))
    if earlier is not None:
        totals[0] = after(totals[0], earlier)
    totals = add(send([(middle - 1, middle), (middle, middle - 1)]))
    at_middle = totals[-1]
    for step in reversed(range(middle - 1)):
        came = send([(step + 1, step), (count - 2 - step, count - 1 - step)])
        end = (me == step) | (me == count - 1 - step)
        totals = [jnp.where(end, other, total) for total, other in zip(totals, came)]
    return jnp.concatenate(totals, 0), at_middle


def local(
    tokens,
    mixer_gain,
    query_weight,
    key_weight,
    value_weight,
    decay_down,
    decay_up,
    decay_bias,
    outgate_weight,
    head_gain,
    output_weight,
    channel_gain,
    gate_weight,
    up_weight,
    down_weight,
    cotangent,
):
    seqs_here, seg_len, width = tokens.shape
    rows_here = seqs_here * seg_len
    count = lax.axis_size("seq")
    ff = gate_weight.shape[1]

    shard_rows = query_weight.shape[0]
    smalls = [mixer_gain, decay_down, decay_up, decay_bias, head_gain, channel_gain]
    flat = jnp.concatenate([small.reshape(-1) for small in smalls])
    flat_size = flat.size
    extra = -(-flat_size // (shard_rows * 128)) * 128
    flat = jnp.pad(flat, (0, shard_rows * extra - flat_size)).reshape(shard_rows, extra)
    mixer_packed = jnp.concatenate(
        [
            own_half(weight, 1)
            for weight in (query_weight, key_weight, value_weight, outgate_weight)
        ]
        + [flat],
        axis=1,
    )
    ffn_packed = jnp.concatenate([own_half(gate_weight, 1), own_half(up_weight, 1)], axis=1)
    mixer_mine = lax.all_gather(mixer_packed, "seq", tiled=True)
    ffn_mine = lax.all_gather(ffn_packed, "seq", tiled=True)
    output_mine = spread(own_half(output_weight, 1))
    mixer_mine = after(after(mixer_mine, output_mine), ffn_packed)
    down_mine = spread(after(own_half(down_weight, 1), mixer_mine))
    mixer_theirs, output_theirs = swapped(mixer_mine), swapped(output_mine)
    mixer_theirs = after(mixer_theirs, output_theirs)
    projection_mine, projection_theirs = mixer_mine[:, :PACKED], mixer_theirs[:, :PACKED]
    small_all = mixer_mine[:, PACKED:].reshape(count, -1)
    pieces, begin = [], 0
    for small in smalls:
        pieces.append(small_all[:, begin : begin + small.size].reshape((count,) + small.shape))
        begin += small.size
    gain_one = pieces[0].reshape(-1).astype(jnp.float32)
    decay_down_all = pieces[1].reshape(width, -1)
    decay_up_f = pieces[2].transpose(1, 0, 2).reshape(decay_up.shape[0], -1).astype(jnp.float32)
    decay_bias_f = pieces[3].reshape(1, -1).astype(jnp.float32)
    head_gain_f = pieces[4].reshape(-1).astype(jnp.float32)
    gain_two = pieces[5].reshape(-1).astype(jnp.float32)
    decay_up_f = jnp.concatenate(halves_of(decay_up_f), 1)
    decay_bias_f = jnp.concatenate(halves_of(decay_bias_f), 1)

    inputs = tokens.reshape(rows_here, width).astype(jnp.float32)

    def first_norm(inputs_in, gain_in):
        return normalize(inputs_in) * gain_in

    normed_one = first_norm(inputs, gain_one).astype(jnp.bfloat16)
    low_rank = product(normed_one, decay_down_all)

    def gate_fn(rank_in, up_in, bias_in):
        return (
            jax.nn.log_sigmoid(jnp.dot(rank_in, up_in, precision=highest_precision) + bias_in)
            / normalizer
        )

    gates = gate_fn(low_rank, decay_up_f, decay_bias_f)
    mine = product(normed_one, projection_mine)
    theirs = product(normed_one, projection_theirs)
    chunk = min(CHUNK, seg_len)
    local_out, forget, scores, states, starts, summary = scan_forward(mine, theirs, gates, seqs_here, chunk)
    incoming_state = after(from_neighbours(low(summary), 1), down_mine)
    attended, mixed = mix_forward(
        local_out, forget, incoming_state, mine, theirs, head_gain_f[None, :], seqs_here, chunk
    )
    mixed = jnp.concatenate(halves_of(mixed), 1)
    resid = inputs + joined(product(mixed, output_mine), product(mixed, output_theirs), 1)
    normed_two = first_norm(resid, gain_two).astype(jnp.bfloat16)
    ffn_mine = after(ffn_mine, normed_two)
    ffn_theirs = swapped(ffn_mine)

    def swiglu(both):
        gate_pre, up_pre = both[:, : ff // 2], both[:, ff // 2 :]
        return low(gate_pre * jax.nn.sigmoid(gate_pre) * up_pre)

    both_mine, both_theirs = product(normed_two, ffn_mine), product(normed_two, ffn_theirs)
    hidden = joined(swiglu(both_mine), swiglu(both_theirs), 1)
    down_theirs = swapped(after(down_mine, mixed))
    result = resid + joined(product(hidden, down_mine), product(hidden, down_theirs), 1)
    block_out = result.astype(jnp.bfloat16).reshape(tokens.shape)

    grad_low = cotangent.reshape(rows_here, width)
    grad_out = grad_low.astype(jnp.float32)
    low_mine, low_theirs = halves_of(grad_low)
    hidden_grad = product_right(low_mine, down_mine) + product_right(low_theirs, down_theirs)

    def swiglu_back(both, grad):
        gate_pre, up_pre = both[:, : ff // 2], both[:, ff // 2 :]
        sigma = jax.nn.sigmoid(gate_pre)
        return jnp.concatenate(
            [
                low(grad * up_pre * (sigma + gate_pre * sigma * (1.0 - sigma))),
                low(grad * (gate_pre * sigma)),
            ],
            axis=1,
        )

    grad_mine, grad_theirs = halves_of(hidden_grad)
    back_mine, back_theirs = swiglu_back(both_mine, grad_mine), swiglu_back(both_theirs, grad_theirs)

    ffn_came = swapped(low(product_left(normed_two, back_theirs)))
    normed_two_grad = product_right(back_mine, ffn_mine) + product_right(back_theirs, ffn_theirs)
    norm_pulled = jax.vjp(first_norm, resid, gain_two)[1](normed_two_grad)
    resid_grad = grad_out + norm_pulled[0]
    channel_gain_grad = norm_pulled[1]
    branch_grad = resid_grad.astype(jnp.bfloat16)
    branch_mine, branch_theirs = halves_of(branch_grad)
    mixed_grad = product_right(branch_mine, output_mine) + product_right(branch_theirs, output_theirs)
    mixed_grad = jnp.concatenate(halves_of(mixed_grad), 1)
    ffn_pair = low(product_left(normed_two, back_mine) + ffn_came.astype(jnp.float32))
    ffn_share = scattered(ffn_pair)
    mixed_grad = after(mixed_grad, ffn_pair)
    attended_grad, *outgate_grads, state_grad, head_gain_grad = mix_backward(
        mixed_grad, attended, mine, theirs, head_gain_f[None, :], forget, seqs_here, chunk
    )
    head_gain_grad = head_gain_grad.sum((0, 1))
    later_grad = from_neighbours(
        jnp.concatenate([state_grad, summary[:, :, DV:]], axis=2).astype(jnp.bfloat16), -1
    )
    down_came = swapped(low(product_left(hidden, after(low_theirs, attended_grad))))
    down_pair = low(product_left(hidden, after(low_mine, attended_grad)) + down_came.astype(jnp.float32))
    packed_mine, packed_theirs, gates_grad = scan_backward(
        mine, theirs, gates, scores, states, starts, incoming_state,
        attended_grad, later_grad, outgate_grads, seqs_here, chunk,
    )
    packed_came = swapped(low(product_left(normed_one, packed_theirs)))
    mixer_pair = low(product_left(normed_one, packed_mine) + packed_came.astype(jnp.float32))
    mixer_share = gathered_sum(mixer_pair, mixer_pair)
    down_share = gathered_sum(after(down_pair, mixer_pair), mixer_share)
    output_came = swapped(low(product_left(mixed, after(branch_theirs, mixer_pair))))
    output_pair = product_left(mixed, after(branch_mine, mixer_pair)) + output_came.astype(jnp.float32)
    gate_pulled = jax.vjp(gate_fn, low_rank, decay_up_f, decay_bias_f)[1](gates_grad)
    low_rank_grad = gate_pulled[0].astype(jnp.bfloat16)
    decay_up_grad = jnp.concatenate(halves_of(gate_pulled[1]), 1)
    decay_bias_grad = jnp.concatenate(halves_of(gate_pulled[2]), 1)[0]
    decay_down_grad = product_left(normed_one, low_rank_grad)
    normed_one_grad = (
        product_right(after(packed_mine, mixer_pair), projection_mine)
        + product_right(after(packed_theirs, mixer_pair), projection_theirs)
        + product_right(low_rank_grad, decay_down_all)
    )
    first_pulled = jax.vjp(first_norm, inputs, gain_one)[1](normed_one_grad)
    tokens_grad = (resid_grad + first_pulled[0]).reshape(tokens.shape)

    def by_shard(grad, dim=0):
        shape = grad.shape[:dim] + (count, grad.shape[dim] // count) + grad.shape[dim + 1 :]
        return jnp.moveaxis(grad.reshape(shape), dim, 0).reshape(count, -1)

    small_grads = jnp.concatenate(
        [
            by_shard(first_pulled[1]),
            by_shard(decay_down_grad),
            by_shard(decay_up_grad, 1),
            by_shard(decay_bias_grad),
            by_shard(head_gain_grad),
            by_shard(channel_gain_grad),
        ],
        axis=1,
    )
    small_rows = -(-flat_size // (width // 2 * 16)) * 16
    small_grads = jnp.pad(low(small_grads), ((0, 0), (0, small_rows * width // 2 - flat_size)))
    rest_pair = jnp.concatenate(
        [
            low(output_pair).reshape(count, shard_rows, width // 2),
            small_grads.reshape(count, small_rows, width // 2),
        ],
        axis=1,
    ).reshape(-1, width // 2)
    rest_share = gathered_sum(rest_pair, mixer_pair)

    ffn_total, ffn_middle = line_sum(after(ffn_share, mixer_pair), 2)
    ffn_other = swapped(ffn_total)
    mixer_total, mixer_middle = line_sum(after(mixer_share, ffn_middle), 2, ffn_total)
    mixer_other = swapped(mixer_total)
    down_total, down_middle = line_sum(after(down_share, mixer_middle), 1, mixer_total)
    down_other = swapped(down_total)
    rest_total, _ = line_sum(after(rest_share, down_middle), 1, down_total)
    rest_other = swapped(rest_total)

    def both_cores(total, other, begin, end):
        return joined(total[:, begin:end], other[:, begin:end], 1).astype(jnp.float32)

    summed = rest_total[shard_rows:].astype(jnp.float32) + rest_other[shard_rows:].astype(jnp.float32)
    summed, shares, begin = summed.reshape(-1), [], 0
    for small in smalls:
        shares.append(summed[begin : begin + small.size].reshape(small.shape))
        begin += small.size

    columns = (0, KEYS // 2, KEYS, KEYS + VALUES // 2, PACKED)
    query_g, key_g, value_g, outgate_g = (
        both_cores(mixer_total, mixer_other, a, b) for a, b in zip(columns[:-1], columns[1:])
    )
    return (
        block_out,
        tokens_grad,
        shares[0],
        query_g,
        key_g,
        value_g,
        shares[1],
        shares[2],
        shares[3],
        outgate_g,
        shares[4],
        joined(rest_total[:shard_rows], rest_other[:shard_rows], 1).astype(jnp.float32),
        shares[5],
        both_cores(ffn_total, ffn_other, 0, ff // 2),
        both_cores(ffn_total, ffn_other, ff // 2, ff),
        joined(down_total, down_other, 1).astype(jnp.float32),
    )


def solution(mesh):
    rep, seq = mesh.shape["rep"], mesh.shape["seq"]
    cores = Mesh(mesh.devices.reshape(rep // 2, 2, seq), EVERYWHERE)
    sequences, weights = P(("z", "core"), "seq", None), P("seq", None)
    in_specs = (
        sequences,
        P("seq"),
        weights,
        weights,
        weights,
        weights,
        P(None, "seq"),
        P("seq"),
        weights,
        P("seq"),
        weights,
        P("seq"),
        weights,
        weights,
        weights,
        sequences,
    )
    out_specs = (sequences, *in_specs[:15])
    return jax.shard_map(local, mesh=cores, in_specs=in_specs, out_specs=out_specs, check_vma=False)
```

```python
import functools

import jax
import jax.numpy as jnp
from jax import lax
from jax.experimental import pallas as pl
from jax.experimental.pallas import tpu as pltpu
from jax.sharding import Mesh, PartitionSpec as P

HEADS = 4
DK = 128
DV = 256
PAIR = HEADS // 2
CHUNK = 128
SAFE = 60.0


epsilon = 1e-06
normalizer = 16.0
highest_precision = lax.Precision.HIGHEST


def normalize(values_in):
    return values_in * lax.rsqrt(jnp.mean(values_in * values_in, axis=-1, keepdims=True) + epsilon)


def dot_nn(left, right):
    return lax.dot_general(left, right, (((1,), (0,)), ((), ())), preferred_element_type=jnp.float32)


def dot_nt(left, right):
    return lax.dot_general(left, right, (((1,), (1,)), ((), ())), preferred_element_type=jnp.float32)


def dot_tn(left, right):
    return lax.dot_general(left, right, (((0,), (0,)), ((), ())), preferred_element_type=jnp.float32)


def low(array):
    return array.astype(jnp.bfloat16)


def exact_sum(selector, array):
    high = low(array)
    rest = low(array - high.astype(jnp.float32))
    return dot_nn(selector, high) + dot_nn(selector, rest)


def halves(array):
    high = low(array)
    return high, low(array - high.astype(jnp.float32))


def close_dot(dot, left, right):
    (left_high, left_rest), (right_high, right_rest) = halves(left), halves(right)
    return dot(left_high, right_high) + (dot(left_high, right_rest) + dot(left_rest, right_high))


def at_head(refs, head, size):
    place = head % PAIR
    return refs[head // PAIR][:, place * size : (place + 1) * size]


def positions(chunk):
    row = lax.broadcasted_iota(jnp.int32, (chunk, chunk), 0)
    column = lax.broadcasted_iota(jnp.int32, (chunk, chunk), 1)
    return row, column


def as_selector(mask):
    return low(jnp.where(mask, 1.0, 0.0))


def halvings(chunk):
    sizes, half = [], chunk // 2
    while half >= 1:
        sizes.append(half)
        half //= 2
    return sizes


def halving_parts(chunk, half):
    row, column = positions(chunk)
    row_late = (row & half) != 0
    pairs = ((row & -(2 * half)) == (column & -(2 * half))) & row_late & ((column & half) == 0)
    middle = (row & -(2 * half)) + (half - 1)
    late = row_late & (column > middle) & (column <= row)
    early = jnp.logical_not(row_late) & (column > row) & (column <= middle)
    return pairs, as_selector(late | early)


def scan_forward_kernel(chunk, q0, k0, v0, q1, k1, v1, g_ref, o_ref, qf_ref, a_ref, st_ref, cs_ref, sum_ref, state, start, table):
    step, steps = pl.program_id(1), pl.num_programs(1)
    q_refs, k_refs, v_refs = (q0, q1), (k0, k1), (v0, v1)

    @pl.when(step == 0)
    def _():
        state[...] = jnp.zeros_like(state)
        start[...] = jnp.zeros_like(start)

    row, column = positions(chunk)
    gates = g_ref[...]
    cumul = exact_sum(as_selector(row >= column), gates)
    left = exact_sum(as_selector(row < column), gates)
    finish = cumul[chunk - 1 : chunk, :]
    mild = jnp.min(finish) > -SAFE
    begin = start[...]
    cs_ref[0] = begin
    grown = jnp.exp(cumul)
    faded = jnp.exp(left)
    begun = jnp.exp(begin)
    kept = jnp.exp(finish)
    scale = DK ** (-0.5)

    @pl.when(mild)
    def _():
        for h in range(HEADS):
            ks = slice(h * DK, (h + 1) * DK)
            far = at_head(q_refs, h, DK) * scale * grown[:, ks]
            near = at_head(k_refs, h, DK) * jnp.exp(-cumul[:, ks])
            table[h] = jnp.where(row >= column, close_dot(dot_nt, far, near), 0.0)

    @pl.when(jnp.logical_not(mild))
    def _():
        for h in range(HEADS):
            ks = slice(h * DK, (h + 1) * DK)
            queries, keys, decay = at_head(q_refs, h, DK) * scale, at_head(k_refs, h, DK), g_ref[:, ks]
            total = jnp.where(row == column, close_dot(dot_nt, queries, keys), 0.0)
            for half in halvings(chunk):
                pairs, selector = halving_parts(chunk, half)
                factor = jnp.exp(exact_sum(selector, decay))
                total = jnp.where(pairs, close_dot(dot_nt, queries * factor, keys * factor), total)
            table[h] = total

    for h in range(HEADS):
        ks, vs = slice(h * DK, (h + 1) * DK), slice(h * DV, (h + 1) * DV)
        queries = at_head(q_refs, h, DK) * scale * grown[:, ks]
        own_values = at_head(v_refs, h, DV)
        values = low(own_values)
        held = state[h]
        st_ref[0, h] = held
        scores = table[h]
        a_ref[0, h] = low(scores)
        o_ref[:, vs] = close_dot(dot_nn, scores, own_values) + dot_nt(low(queries), low(held))
        qf_ref[:, ks] = low(queries * begun[:, ks])
        state[h] = held * kept[:, ks] + dot_tn(values, low(at_head(k_refs, h, DK) * faded[:, ks]))
    start[...] = begin + finish

    @pl.when(step == steps - 1)
    def _():
        for h in range(HEADS):
            ks = slice(h * DK, (h + 1) * DK)
            sum_ref[0, h, :DV] = state[h]
            sum_ref[0, h, DV:] = jnp.broadcast_to(jnp.exp(begin[:, ks] + finish[:, ks]), (8, DK))


def scan_backward_kernel(
    chunk, q0, k0, v0, q1, k1, v1, g_ref, a_ref, st_ref, cs_ref, in_ref, do_ref, later_ref, dog0, dog1,
    out0, out1, dg_ref, later, dqi, dki, dci,
):
    q_refs, k_refs, v_refs = (q0, q1), (k0, k1), (v0, v1)

    @pl.when(pl.program_id(1) == 0)
    def _():
        later[...] = later_ref[0]

    row, column = positions(chunk)
    lower = row >= column
    gates = g_ref[...]
    cumul = exact_sum(as_selector(lower), gates)
    left = exact_sum(as_selector(row < column), gates)
    finish = cumul[chunk - 1 : chunk, :]
    mild = jnp.min(finish) > -SAFE
    grown = jnp.exp(cumul)
    faded = jnp.exp(left)
    kept = jnp.exp(finish)
    begun = jnp.exp(cs_ref[0])
    scale = DK ** (-0.5)

    def overlap(h, vs):
        return close_dot(dot_nt, do_ref[:, vs], at_head(v_refs, h, DV))

    @pl.when(mild)
    def _():
        for h in range(HEADS):
            ks, vs = slice(h * DK, (h + 1) * DK), slice(h * DV, (h + 1) * DV)
            shrunk = jnp.exp(-cumul[:, ks])
            far = low(at_head(q_refs, h, DK) * scale * grown[:, ks])
            near = low(at_head(k_refs, h, DK) * shrunk)
            pairs = low(jnp.where(lower, overlap(h, vs), 0.0))
            for_q, for_k = dot_nn(pairs, near), dot_tn(pairs, far)
            dqi[:, ks] = grown[:, ks] * for_q
            dki[:, ks] = shrunk * for_k
            dci[:, ks] = far.astype(jnp.float32) * for_q - near.astype(jnp.float32) * for_k

    @pl.when(jnp.logical_not(mild))
    def _():
        for h in range(HEADS):
            ks, vs = slice(h * DK, (h + 1) * DK), slice(h * DV, (h + 1) * DV)
            queries, keys, decay = at_head(q_refs, h, DK) * scale, at_head(k_refs, h, DK), g_ref[:, ks]
            both = overlap(h, vs)
            pairs = low(jnp.where(row == column, both, 0.0))
            grad_q, grad_k = dot_nn(pairs, low(keys)), dot_tn(pairs, low(queries))
            grad_c = jnp.zeros_like(grad_q)
            for half in halvings(chunk):
                here, selector = halving_parts(chunk, half)
                factor = jnp.exp(exact_sum(selector, decay))
                far, near = low(queries * factor), low(keys * factor)
                pairs = low(jnp.where(here, both, 0.0))
                for_q, for_k = dot_nn(pairs, near), dot_tn(pairs, far)
                grad_q += factor * for_q
                grad_k += factor * for_k
                grad_c += far.astype(jnp.float32) * for_q - near.astype(jnp.float32) * for_k
            dqi[:, ks] = grad_q
            dki[:, ks] = grad_k
            dci[:, ks] = grad_c

    before = as_selector(row > column)
    after = as_selector(row <= column)
    for h in range(HEADS):
        ks, vs = slice(h * DK, (h + 1) * DK), slice(h * DV, (h + 1) * DV)
        values, grad_out = low(at_head(v_refs, h, DV)), low(do_ref[:, vs])
        held = st_ref[0, h] + in_ref[0, h] * begun[:, ks]
        ahead = later[h]
        ahead_low = low(ahead)
        queries = at_head(q_refs, h, DK) * scale * grown[:, ks]
        keys = at_head(k_refs, h, DK) * faded[:, ks]
        out_ref, place = (out0, out1)[h // PAIR], h % PAIR
        from_state = dot_nn(grad_out, low(held))
        from_later = dot_nn(values, ahead_low)
        out_ref[:, place * DK : (place + 1) * DK] = low((dqi[:, ks] + grown[:, ks] * from_state) * scale)
        out_ref[:, KEYS // 2 + place * DK : KEYS // 2 + (place + 1) * DK] = low(dki[:, ks] + faded[:, ks] * from_later)
        out_ref[:, KEYS + place * DV : KEYS + (place + 1) * DV] = low(
            dot_tn(a_ref[0, h], grad_out) + dot_nt(low(keys), ahead_low)
        )
        through = kept[:, ks] * jnp.sum(held * ahead, axis=0, keepdims=True)
        dg_ref[:, ks] = (
            exact_sum(after, dci[:, ks] + queries * from_state)
            + exact_sum(before, keys * from_later)
            + through
        )
        later[h] = ahead * kept[:, ks] + dot_tn(grad_out, low(queries))
    out0[:, KEYS + VALUES // 2 :] = dog0[...]
    out1[:, KEYS + VALUES // 2 :] = dog1[...]


def mix_forward_kernel(o_ref, qf_ref, in_ref, og0, og1, gain_ref, att_ref, mixed_ref):
    gain = gain_ref[...]
    for h in range(HEADS):
        ks, vs = slice(h * DK, (h + 1) * DK), slice(h * DV, (h + 1) * DV)
        attended = o_ref[:, vs] + dot_nt(qf_ref[:, ks], low(in_ref[0, h]))
        att_ref[:, vs] = attended
        outgate = at_head((og0, og1), h, DV)
        mixed_ref[:, vs] = low(normalize(attended) * gain * (outgate * jax.nn.sigmoid(outgate)))


def mix_backward_kernel(dm_ref, att_ref, og0, og1, gain_ref, qf_ref, do_ref, dog0, dog1, grad_ref, dgain_ref):
    @pl.when(pl.program_id(1) == 0)
    def _():
        grad_ref[...] = jnp.zeros_like(grad_ref)
        dgain_ref[...] = jnp.zeros_like(dgain_ref)

    gain = gain_ref[...]
    for h in range(HEADS):
        ks, vs = slice(h * DK, (h + 1) * DK), slice(h * DV, (h + 1) * DV)
        attended, outgate, grad = att_ref[:, vs], at_head((og0, og1), h, DV), dm_ref[:, vs]
        dog_ref, place = (dog0, dog1)[h // PAIR], h % PAIR
        inverse = lax.rsqrt(jnp.mean(attended * attended, axis=-1, keepdims=True) + epsilon)
        normed = attended * inverse
        sigma = jax.nn.sigmoid(outgate)
        gated = grad * (outgate * sigma)
        dog_ref[:, place * DV : (place + 1) * DV] = low(grad * normed * gain * (sigma + outgate * sigma * (1.0 - sigma)))
        dgain_ref[0] += jnp.sum(gated * normed, axis=0, keepdims=True)
        inner = gated * gain
        result = inverse * (inner - normed * jnp.mean(inner * normed, axis=-1, keepdims=True))
        do_ref[:, vs] = result
        grad_ref[0, h] += dot_tn(low(result), qf_ref[:, ks])


def rows_spec(chunk, chunks, width, backward=False):
    if backward:
        return pl.BlockSpec((chunk, width), lambda s, c: (s * chunks + chunks - 1 - c, 0))
    return pl.BlockSpec((chunk, width), lambda s, c: (s * chunks + c, 0))


def item_spec(shape):
    return pl.BlockSpec((1,) + shape, lambda s, c: (s,) + (0,) * len(shape))


def chunk_spec(chunks, shape, backward=False):
    if backward:
        return pl.BlockSpec((1,) + shape, lambda s, c: (s * chunks + chunks - 1 - c,) + (0,) * len(shape))
    return pl.BlockSpec((1,) + shape, lambda s, c: (s * chunks + c,) + (0,) * len(shape))


def shaped(shape, kind=jnp.float32):
    return jax.ShapeDtypeStruct(shape, kind)


def packed_specs(chunk, chunks, backward=False):
    def at(width, place):
        whole = rows_spec(chunk, chunks, width, backward)
        return pl.BlockSpec(whole.block_shape, lambda s, c: (whole.index_map(s, c)[0], place))

    return [at(KEYS // 2, 0), at(KEYS // 2, 1), at(VALUES // 2, 1), at(VALUES // 2, 2)]


KEYS, VALUES = HEADS * DK, HEADS * DV
PACKED = KEYS + VALUES
ROOM = pltpu.CompilerParams(vmem_limit_bytes=40 * 1024 * 1024)


def scan_forward(mine, theirs, gates, seqs, chunk):
    rows = gates.shape[0]
    chunks = rows // seqs // chunk
    keyed, valued = rows_spec(chunk, chunks, KEYS), rows_spec(chunk, chunks, VALUES)
    return pl.pallas_call(
        functools.partial(scan_forward_kernel, chunk),
        grid=(seqs, chunks),
        in_specs=packed_specs(chunk, chunks)[:3] * 2 + [keyed],
        out_specs=[
            valued,
            keyed,
            chunk_spec(chunks, (HEADS, chunk, chunk)),
            chunk_spec(chunks, (HEADS, DV, DK)),
            chunk_spec(chunks, (1, KEYS)),
            item_spec((HEADS, DV + 8, DK)),
        ],
        out_shape=[
            shaped((rows, VALUES)),
            shaped((rows, KEYS), jnp.bfloat16),
            shaped((seqs * chunks, HEADS, chunk, chunk), jnp.bfloat16),
            shaped((seqs * chunks, HEADS, DV, DK)),
            shaped((seqs * chunks, 1, KEYS)),
            shaped((seqs, HEADS, DV + 8, DK)),
        ],
        scratch_shapes=[
            pltpu.VMEM((HEADS, DV, DK), jnp.float32),
            pltpu.VMEM((1, KEYS), jnp.float32),
            pltpu.VMEM((HEADS, chunk, chunk), jnp.float32),
        ],
        compiler_params=ROOM,
        name="scan_forward",
    )(mine, mine, mine, theirs, theirs, theirs, gates)


def scan_backward(
    mine, theirs, gates, scores, states, starts, incoming, grad_out, later, outgate_grads, seqs, chunk
):
    rows = gates.shape[0]
    chunks = rows // seqs // chunk
    keyed, valued = rows_spec(chunk, chunks, KEYS, True), rows_spec(chunk, chunks, VALUES, True)
    return pl.pallas_call(
        functools.partial(scan_backward_kernel, chunk),
        grid=(seqs, chunks),
        in_specs=[
            *packed_specs(chunk, chunks, True)[:3] * 2,
            keyed,
            chunk_spec(chunks, (HEADS, chunk, chunk), True),
            chunk_spec(chunks, (HEADS, DV, DK), True),
            chunk_spec(chunks, (1, KEYS), True),
            item_spec((HEADS, DV, DK)),
            valued,
            item_spec((HEADS, DV, DK)),
            *[rows_spec(chunk, chunks, VALUES // 2, True)] * 2,
        ],
        out_specs=[*[rows_spec(chunk, chunks, PACKED, True)] * 2, keyed],
        out_shape=[*[shaped((rows, PACKED), jnp.bfloat16)] * 2, shaped((rows, KEYS))],
        scratch_shapes=[pltpu.VMEM((HEADS, DV, DK), jnp.float32)] + [pltpu.VMEM((chunk, KEYS), jnp.float32)] * 3,
        compiler_params=ROOM,
        name="scan_backward",
    )(
        mine, mine, mine, theirs, theirs, theirs,
        gates, scores, states, starts, incoming, grad_out, later, *outgate_grads,
    )


def mix_forward(local_out, forget, incoming, mine, theirs, gain, seqs, chunk):
    rows = local_out.shape[0]
    chunks = rows // seqs // chunk
    keyed, valued = rows_spec(chunk, chunks, KEYS), rows_spec(chunk, chunks, VALUES)
    whole_gain = pl.BlockSpec((1, DV), lambda s, c: (0, 0))
    return pl.pallas_call(
        mix_forward_kernel,
        grid=(seqs, chunks),
        in_specs=[valued, keyed, item_spec((HEADS, DV, DK)), *packed_specs(chunk, chunks)[3:] * 2, whole_gain],
        out_specs=[valued, valued],
        out_shape=[shaped((rows, VALUES)), shaped((rows, VALUES), jnp.bfloat16)],
        compiler_params=ROOM,
        name="mix_forward",
    )(local_out, forget, incoming, mine, theirs, gain)


def mix_backward(mixed_grad, attended, mine, theirs, gain, forget, seqs, chunk):
    rows = attended.shape[0]
    chunks = rows // seqs // chunk
    keyed, valued = rows_spec(chunk, chunks, KEYS), rows_spec(chunk, chunks, VALUES)
    whole_gain = pl.BlockSpec((1, DV), lambda s, c: (0, 0))
    return pl.pallas_call(
        mix_backward_kernel,
        grid=(seqs, chunks),
        in_specs=[valued, valued, *packed_specs(chunk, chunks)[3:] * 2, whole_gain, keyed],
        out_specs=[
            valued,
            *[rows_spec(chunk, chunks, VALUES // 2)] * 2,
            item_spec((HEADS, DV, DK)),
            item_spec((1, DV)),
        ],
        out_shape=[
            shaped((rows, VALUES)),
            *[shaped((rows, VALUES // 2), jnp.bfloat16)] * 2,
            shaped((seqs, HEADS, DV, DK)),
            shaped((seqs, 1, DV)),
        ],
        compiler_params=ROOM,
        name="mix_backward",
    )(mixed_grad, attended, mine, theirs, gain, forget)


def from_neighbours(summary, step):
    count = lax.axis_size("seq")
    total, factor = None, None
    for distance in range(1, count):
        shift = step * distance
        pairs = [(i, i + shift) for i in range(count) if 0 <= i + shift < count]
        came = lax.ppermute(summary, "seq", pairs)
        state, retain = came[:, :, :DV].astype(jnp.float32), came[:, :, DV : DV + 1].astype(jnp.float32)
        if total is None:
            total, factor = state, retain
        else:
            total, factor = total + factor * state, factor * retain
    return total


def product(left, right):
    return jnp.dot(left, right, preferred_element_type=jnp.float32)


def product_left(left, right):
    return lax.dot_general(
        left, right, (((0,), (0,)), ((), ())), preferred_element_type=jnp.float32
    )


def product_right(left, right):
    return lax.dot_general(
        left, right, (((1,), (1,)), ((), ())), preferred_element_type=jnp.float32
    )


EVERYWHERE = ("z", "core", "seq")


def swapped(array):
    return lax.ppermute(array, "core", [(0, 1), (1, 0)])


def after(array, other):
    def nothing(array_ref, other_ref, out_ref):
        pass

    anywhere = pl.BlockSpec(memory_space=pl.ANY)
    return pl.pallas_call(
        nothing,
        in_specs=[anywhere, anywhere],
        out_specs=anywhere,
        out_shape=shaped(array.shape, array.dtype),
        input_output_aliases={0: 0},
        name="after",
    )(array, other)


def first_core():
    return lax.axis_index("core") == 0


def own_half(array, dim, other=False):
    core = lax.axis_index("core")
    size = array.shape[dim] // 2
    return lax.dynamic_slice_in_dim(array, ((1 - core) if other else core) * size, size, dim)


def joined(mine, theirs, dim):
    return jnp.where(
        first_core(), jnp.concatenate([mine, theirs], dim), jnp.concatenate([theirs, mine], dim)
    )


def halves_of(array):
    half = array.shape[1] // 2
    first = first_core()
    return (
        jnp.where(first, array[:, :half], array[:, half:]),
        jnp.where(first, array[:, half:], array[:, :half]),
    )


def scattered(array):
    return lax.psum_scatter(array, "seq", scatter_dimension=0, tiled=True)


def direct(count):
    return count in (2, 4)


def spread(array):
    count, me = lax.axis_size("seq"), lax.axis_index("seq")
    if not direct(count):
        return lax.all_gather(array, "seq", tiled=True)
    rows = array.shape[0]
    whole = jnp.zeros((count * rows, array.shape[1]), array.dtype)
    whole = lax.dynamic_update_slice_in_dim(whole, array, me * rows, 0)
    for distance in range(1, count):
        came = lax.ppermute(array, "seq", [(i, i ^ distance) for i in range(count)])
        whole = lax.dynamic_update_slice_in_dim(whole, came, (me ^ distance) * rows, 0)
    return whole


def gathered_sum(array, late):
    count, me = lax.axis_size("seq"), lax.axis_index("seq")
    if not direct(count):
        return scattered(array)
    rows = array.shape[0] // count
    total = lax.dynamic_slice_in_dim(array, me * rows, rows, 0).astype(jnp.float32)
    for distance in range(1, count):
        piece = lax.dynamic_slice_in_dim(array, (me ^ distance) * rows, rows, 0)
        came = lax.ppermute(piece, "seq", [(i, i ^ distance) for i in range(count)])
        total = total + after(came, late).astype(jnp.float32)
    return low(total)


def local(
    tokens,
    mixer_gain,
    query_weight,
    key_weight,
    value_weight,
    decay_down,
    decay_up,
    decay_bias,
    outgate_weight,
    head_gain,
    output_weight,
    channel_gain,
    gate_weight,
    up_weight,
    down_weight,
    cotangent,
):
    seqs_here, seg_len, width = tokens.shape
    rows_here = seqs_here * seg_len
    count = lax.axis_size("seq")
    ff = gate_weight.shape[1]

    shard_rows = query_weight.shape[0]
    smalls = [mixer_gain, decay_down, decay_up, decay_bias, head_gain, channel_gain]
    flat = jnp.concatenate([small.reshape(-1) for small in smalls])
    flat_size = flat.size
    extra = -(-flat_size // (shard_rows * 128)) * 128
    flat = jnp.pad(flat, (0, shard_rows * extra - flat_size)).reshape(shard_rows, extra)
    mixer_packed = jnp.concatenate(
        [
            own_half(weight, 1)
            for weight in (query_weight, key_weight, value_weight, outgate_weight)
        ]
        + [flat],
        axis=1,
    )
    ffn_packed = jnp.concatenate([own_half(gate_weight, 1), own_half(up_weight, 1)], axis=1)
    mixer_mine = lax.all_gather(mixer_packed, "seq", tiled=True)
    ffn_mine = lax.all_gather(ffn_packed, "seq", tiled=True)
    output_mine = spread(own_half(output_weight, 1))
    mixer_mine = after(after(mixer_mine, output_mine), ffn_packed)
    down_mine = spread(after(own_half(down_weight, 1), mixer_mine))
    mixer_theirs, output_theirs = swapped(mixer_mine), swapped(output_mine)
    mixer_theirs = after(mixer_theirs, output_theirs)
    projection_mine, projection_theirs = mixer_mine[:, :PACKED], mixer_theirs[:, :PACKED]
    small_all = mixer_mine[:, PACKED:].reshape(count, -1)
    pieces, begin = [], 0
    for small in smalls:
        pieces.append(small_all[:, begin : begin + small.size].reshape((count,) + small.shape))
        begin += small.size
    gain_one = pieces[0].reshape(-1).astype(jnp.float32)
    decay_down_all = pieces[1].reshape(width, -1)
    decay_up_f = pieces[2].transpose(1, 0, 2).reshape(decay_up.shape[0], -1).astype(jnp.float32)
    decay_bias_f = pieces[3].reshape(1, -1).astype(jnp.float32)
    head_gain_f = pieces[4].reshape(-1).astype(jnp.float32)
    gain_two = pieces[5].reshape(-1).astype(jnp.float32)
    decay_up_f = jnp.concatenate(halves_of(decay_up_f), 1)
    decay_bias_f = jnp.concatenate(halves_of(decay_bias_f), 1)

    inputs = tokens.reshape(rows_here, width).astype(jnp.float32)

    def first_norm(inputs_in, gain_in):
        return normalize(inputs_in) * gain_in

    normed_one = first_norm(inputs, gain_one).astype(jnp.bfloat16)
    low_rank = product(normed_one, decay_down_all)

    def gate_fn(rank_in, up_in, bias_in):
        return (
            jax.nn.log_sigmoid(jnp.dot(rank_in, up_in, precision=highest_precision) + bias_in)
            / normalizer
        )

    gates = gate_fn(low_rank, decay_up_f, decay_bias_f)
    mine = product(normed_one, projection_mine)
    theirs = product(normed_one, projection_theirs)
    chunk = min(CHUNK, seg_len)
    local_out, forget, scores, states, starts, summary = scan_forward(mine, theirs, gates, seqs_here, chunk)
    incoming_state = after(from_neighbours(low(summary), 1), down_mine)
    attended, mixed = mix_forward(
        local_out, forget, incoming_state, mine, theirs, head_gain_f[None, :], seqs_here, chunk
    )
    mixed = jnp.concatenate(halves_of(mixed), 1)
    resid = inputs + joined(product(mixed, output_mine), product(mixed, output_theirs), 1)
    normed_two = first_norm(resid, gain_two).astype(jnp.bfloat16)
    ffn_mine = after(ffn_mine, normed_two)
    ffn_theirs = swapped(ffn_mine)

    def swiglu(both):
        gate_pre, up_pre = both[:, : ff // 2], both[:, ff // 2 :]
        return low(gate_pre * jax.nn.sigmoid(gate_pre) * up_pre)

    both_mine, both_theirs = product(normed_two, ffn_mine), product(normed_two, ffn_theirs)
    hidden = joined(swiglu(both_mine), swiglu(both_theirs), 1)
    down_theirs = swapped(down_mine)
    result = resid + joined(product(hidden, down_mine), product(hidden, down_theirs), 1)
    block_out = result.astype(jnp.bfloat16).reshape(tokens.shape)

    grad_low = cotangent.reshape(rows_here, width)
    grad_out = grad_low.astype(jnp.float32)
    low_mine, low_theirs = halves_of(grad_low)
    hidden_grad = product_right(low_mine, down_mine) + product_right(low_theirs, down_theirs)

    def swiglu_back(both, grad):
        gate_pre, up_pre = both[:, : ff // 2], both[:, ff // 2 :]
        sigma = jax.nn.sigmoid(gate_pre)
        return jnp.concatenate(
            [
                low(grad * up_pre * (sigma + gate_pre * sigma * (1.0 - sigma))),
                low(grad * (gate_pre * sigma)),
            ],
            axis=1,
        )

    grad_mine, grad_theirs = halves_of(hidden_grad)
    back_mine, back_theirs = swiglu_back(both_mine, grad_mine), swiglu_back(both_theirs, grad_theirs)

    ffn_came = swapped(low(product_left(normed_two, back_theirs)))
    normed_two_grad = product_right(back_mine, ffn_mine) + product_right(back_theirs, ffn_theirs)
    norm_pulled = jax.vjp(first_norm, resid, gain_two)[1](normed_two_grad)
    resid_grad = grad_out + norm_pulled[0]
    channel_gain_grad = norm_pulled[1]
    branch_grad = resid_grad.astype(jnp.bfloat16)
    branch_mine, branch_theirs = halves_of(branch_grad)
    mixed_grad = product_right(branch_mine, output_mine) + product_right(branch_theirs, output_theirs)
    mixed_grad = jnp.concatenate(halves_of(mixed_grad), 1)
    ffn_pair = low(product_left(normed_two, back_mine) + ffn_came.astype(jnp.float32))
    ffn_share = scattered(ffn_pair)
    mixed_grad = after(mixed_grad, ffn_pair)
    attended_grad, *outgate_grads, state_grad, head_gain_grad = mix_backward(
        mixed_grad, attended, mine, theirs, head_gain_f[None, :], forget, seqs_here, chunk
    )
    head_gain_grad = head_gain_grad.sum((0, 1))
    later_grad = from_neighbours(
        jnp.concatenate([state_grad, summary[:, :, DV:]], axis=2).astype(jnp.bfloat16), -1
    )
    down_came = swapped(low(product_left(hidden, after(low_theirs, attended_grad))))
    down_pair = low(product_left(hidden, after(low_mine, attended_grad)) + down_came.astype(jnp.float32))
    packed_mine, packed_theirs, gates_grad = scan_backward(
        mine, theirs, gates, scores, states, starts, incoming_state,
        attended_grad, later_grad, outgate_grads, seqs_here, chunk,
    )
    packed_came = swapped(low(product_left(normed_one, packed_theirs)))
    mixer_pair = low(product_left(normed_one, packed_mine) + packed_came.astype(jnp.float32))
    mixer_share = gathered_sum(mixer_pair, mixer_pair)
    down_share = gathered_sum(after(down_pair, later_grad), mixer_pair)
    output_came = swapped(low(product_left(mixed, after(branch_theirs, mixer_pair))))
    output_pair = product_left(mixed, after(branch_mine, mixer_pair)) + output_came.astype(jnp.float32)
    gate_pulled = jax.vjp(gate_fn, low_rank, decay_up_f, decay_bias_f)[1](gates_grad)
    low_rank_grad = gate_pulled[0].astype(jnp.bfloat16)
    decay_up_grad = jnp.concatenate(halves_of(gate_pulled[1]), 1)
    decay_bias_grad = jnp.concatenate(halves_of(gate_pulled[2]), 1)[0]
    decay_down_grad = product_left(normed_one, low_rank_grad)
    normed_one_grad = (
        product_right(after(packed_mine, mixer_pair), projection_mine)
        + product_right(after(packed_theirs, mixer_pair), projection_theirs)
        + product_right(low_rank_grad, decay_down_all)
    )
    first_pulled = jax.vjp(first_norm, inputs, gain_one)[1](normed_one_grad)
    tokens_grad = (resid_grad + first_pulled[0]).reshape(tokens.shape)

    def by_shard(grad, dim=0):
        shape = grad.shape[:dim] + (count, grad.shape[dim] // count) + grad.shape[dim + 1 :]
        return jnp.moveaxis(grad.reshape(shape), dim, 0).reshape(count, -1)

    small_grads = jnp.concatenate(
        [
            by_shard(first_pulled[1]),
            by_shard(decay_down_grad),
            by_shard(decay_up_grad, 1),
            by_shard(decay_bias_grad),
            by_shard(head_gain_grad),
            by_shard(channel_gain_grad),
        ],
        axis=1,
    )
    small_rows = -(-flat_size // (width // 2 * 16)) * 16
    small_grads = jnp.pad(low(small_grads), ((0, 0), (0, small_rows * width // 2 - flat_size)))
    rest_pair = jnp.concatenate(
        [
            low(output_pair).reshape(count, shard_rows, width // 2),
            small_grads.reshape(count, small_rows, width // 2),
        ],
        axis=1,
    ).reshape(-1, width // 2)
    rest_share = gathered_sum(rest_pair, mixer_pair)

    ffn_total = lax.psum(ffn_share, "z")
    ffn_other = swapped(ffn_total)
    mixer_total, down_total, rest_total = lax.psum(
        tuple(after(share, ffn_total) for share in (mixer_share, down_share, rest_share)), "z"
    )
    mixer_other, down_other, rest_other = (
        swapped(total) for total in (mixer_total, down_total, rest_total)
    )

    def both_cores(total, other, begin, end):
        return joined(total[:, begin:end], other[:, begin:end], 1).astype(jnp.float32)

    summed = rest_total[shard_rows:].astype(jnp.float32) + rest_other[shard_rows:].astype(jnp.float32)
    summed, shares, begin = summed.reshape(-1), [], 0
    for small in smalls:
        shares.append(summed[begin : begin + small.size].reshape(small.shape))
        begin += small.size

    columns = (0, KEYS // 2, KEYS, KEYS + VALUES // 2, PACKED)
    query_g, key_g, value_g, outgate_g = (
        both_cores(mixer_total, mixer_other, a, b) for a, b in zip(columns[:-1], columns[1:])
    )
    return (
        block_out,
        tokens_grad,
        shares[0],
        query_g,
        key_g,
        value_g,
        shares[1],
        shares[2],
        shares[3],
        outgate_g,
        shares[4],
        joined(rest_total[:shard_rows], rest_other[:shard_rows], 1).astype(jnp.float32),
        shares[5],
        both_cores(ffn_total, ffn_other, 0, ff // 2),
        both_cores(ffn_total, ffn_other, ff // 2, ff),
        joined(down_total, down_other, 1).astype(jnp.float32),
    )


def solution(mesh):
    rep, seq = mesh.shape["rep"], mesh.shape["seq"]
    cores = Mesh(mesh.devices.reshape(rep // 2, 2, seq), EVERYWHERE)
    sequences, weights = P(("z", "core"), "seq", None), P("seq", None)
    in_specs = (
        sequences,
        P("seq"),
        weights,
        weights,
        weights,
        weights,
        P(None, "seq"),
        P("seq"),
        weights,
        P("seq"),
        weights,
        P("seq"),
        weights,
        weights,
        weights,
        sequences,
    )
    out_specs = (sequences, *in_specs[:15])
    return jax.shard_map(local, mesh=cores, in_specs=in_specs, out_specs=out_specs, check_vma=False)
```

```python
import functools

import jax
import jax.numpy as jnp
from jax import lax
from jax.experimental import pallas as pl
from jax.experimental.pallas import tpu as pltpu
from jax.sharding import Mesh, PartitionSpec as P

HEADS = 4
DK = 128
DV = 256
PAIR = HEADS // 2
CHUNK = 128
SAFE = 60.0


epsilon = 1e-06
normalizer = 16.0
highest_precision = lax.Precision.HIGHEST


def normalize(values_in):
    return values_in * lax.rsqrt(jnp.mean(values_in * values_in, axis=-1, keepdims=True) + epsilon)


def dot_nn(left, right):
    return lax.dot_general(left, right, (((1,), (0,)), ((), ())), preferred_element_type=jnp.float32)


def dot_nt(left, right):
    return lax.dot_general(left, right, (((1,), (1,)), ((), ())), preferred_element_type=jnp.float32)


def dot_tn(left, right):
    return lax.dot_general(left, right, (((0,), (0,)), ((), ())), preferred_element_type=jnp.float32)


def low(array):
    return array.astype(jnp.bfloat16)


def exact_sum(selector, array):
    high = low(array)
    rest = low(array - high.astype(jnp.float32))
    return dot_nn(selector, high) + dot_nn(selector, rest)


def halves(array):
    high = low(array)
    return high, low(array - high.astype(jnp.float32))


def close_dot(dot, left, right):
    (left_high, left_rest), (right_high, right_rest) = halves(left), halves(right)
    return dot(left_high, right_high) + (dot(left_high, right_rest) + dot(left_rest, right_high))


def at_head(refs, head, size):
    place = head % PAIR
    return refs[head // PAIR][:, place * size : (place + 1) * size]


def positions(chunk):
    row = lax.broadcasted_iota(jnp.int32, (chunk, chunk), 0)
    column = lax.broadcasted_iota(jnp.int32, (chunk, chunk), 1)
    return row, column


def as_selector(mask):
    return low(jnp.where(mask, 1.0, 0.0))


def halvings(chunk):
    sizes, half = [], chunk // 2
    while half >= 1:
        sizes.append(half)
        half //= 2
    return sizes


def halving_parts(chunk, half):
    row, column = positions(chunk)
    row_late = (row & half) != 0
    pairs = ((row & -(2 * half)) == (column & -(2 * half))) & row_late & ((column & half) == 0)
    middle = (row & -(2 * half)) + (half - 1)
    late = row_late & (column > middle) & (column <= row)
    early = jnp.logical_not(row_late) & (column > row) & (column <= middle)
    return pairs, as_selector(late | early)


def scan_forward_kernel(chunk, q0, k0, v0, q1, k1, v1, g_ref, o_ref, qf_ref, a_ref, st_ref, cs_ref, sum_ref, state, start, table):
    step, steps = pl.program_id(1), pl.num_programs(1)
    q_refs, k_refs, v_refs = (q0, q1), (k0, k1), (v0, v1)

    @pl.when(step == 0)
    def _():
        state[...] = jnp.zeros_like(state)
        start[...] = jnp.zeros_like(start)

    row, column = positions(chunk)
    gates = g_ref[...]
    cumul = exact_sum(as_selector(row >= column), gates)
    left = exact_sum(as_selector(row < column), gates)
    finish = cumul[chunk - 1 : chunk, :]
    mild = jnp.min(finish) > -SAFE
    begin = start[...]
    cs_ref[0] = begin
    grown = jnp.exp(cumul)
    faded = jnp.exp(left)
    begun = jnp.exp(begin)
    kept = jnp.exp(finish)
    scale = DK ** (-0.5)

    @pl.when(mild)
    def _():
        for h in range(HEADS):
            ks = slice(h * DK, (h + 1) * DK)
            far = at_head(q_refs, h, DK) * scale * grown[:, ks]
            near = at_head(k_refs, h, DK) * jnp.exp(-cumul[:, ks])
            table[h] = jnp.where(row >= column, close_dot(dot_nt, far, near), 0.0)

    @pl.when(jnp.logical_not(mild))
    def _():
        for h in range(HEADS):
            ks = slice(h * DK, (h + 1) * DK)
            queries, keys, decay = at_head(q_refs, h, DK) * scale, at_head(k_refs, h, DK), g_ref[:, ks]
            total = jnp.where(row == column, close_dot(dot_nt, queries, keys), 0.0)
            for half in halvings(chunk):
                pairs, selector = halving_parts(chunk, half)
                factor = jnp.exp(exact_sum(selector, decay))
                total = jnp.where(pairs, close_dot(dot_nt, queries * factor, keys * factor), total)
            table[h] = total

    for h in range(HEADS):
        ks, vs = slice(h * DK, (h + 1) * DK), slice(h * DV, (h + 1) * DV)
        queries = at_head(q_refs, h, DK) * scale * grown[:, ks]
        own_values = at_head(v_refs, h, DV)
        values = low(own_values)
        held = state[h]
        st_ref[0, h] = held
        scores = table[h]
        a_ref[0, h] = low(scores)
        o_ref[:, vs] = close_dot(dot_nn, scores, own_values) + dot_nt(low(queries), low(held))
        qf_ref[:, ks] = low(queries * begun[:, ks])
        state[h] = held * kept[:, ks] + dot_tn(values, low(at_head(k_refs, h, DK) * faded[:, ks]))
    start[...] = begin + finish

    @pl.when(step == steps - 1)
    def _():
        for h in range(HEADS):
            ks = slice(h * DK, (h + 1) * DK)
            sum_ref[0, h, :DV] = state[h]
            sum_ref[0, h, DV:] = jnp.broadcast_to(jnp.exp(begin[:, ks] + finish[:, ks]), (8, DK))


def scan_backward_kernel(
    chunk, q0, k0, v0, q1, k1, v1, g_ref, a_ref, st_ref, cs_ref, in_ref, do_ref, later_ref, dog0, dog1,
    out0, out1, dg_ref, later, dqi, dki, dci,
):
    q_refs, k_refs, v_refs = (q0, q1), (k0, k1), (v0, v1)

    @pl.when(pl.program_id(1) == 0)
    def _():
        later[...] = later_ref[0]

    row, column = positions(chunk)
    lower = row >= column
    gates = g_ref[...]
    cumul = exact_sum(as_selector(lower), gates)
    left = exact_sum(as_selector(row < column), gates)
    finish = cumul[chunk - 1 : chunk, :]
    mild = jnp.min(finish) > -SAFE
    grown = jnp.exp(cumul)
    faded = jnp.exp(left)
    kept = jnp.exp(finish)
    begun = jnp.exp(cs_ref[0])
    scale = DK ** (-0.5)

    def overlap(h, vs):
        return close_dot(dot_nt, do_ref[:, vs], at_head(v_refs, h, DV))

    @pl.when(mild)
    def _():
        for h in range(HEADS):
            ks, vs = slice(h * DK, (h + 1) * DK), slice(h * DV, (h + 1) * DV)
            shrunk = jnp.exp(-cumul[:, ks])
            far = low(at_head(q_refs, h, DK) * scale * grown[:, ks])
            near = low(at_head(k_refs, h, DK) * shrunk)
            pairs = low(jnp.where(lower, overlap(h, vs), 0.0))
            for_q, for_k = dot_nn(pairs, near), dot_tn(pairs, far)
            dqi[:, ks] = grown[:, ks] * for_q
            dki[:, ks] = shrunk * for_k
            dci[:, ks] = far.astype(jnp.float32) * for_q - near.astype(jnp.float32) * for_k

    @pl.when(jnp.logical_not(mild))
    def _():
        for h in range(HEADS):
            ks, vs = slice(h * DK, (h + 1) * DK), slice(h * DV, (h + 1) * DV)
            queries, keys, decay = at_head(q_refs, h, DK) * scale, at_head(k_refs, h, DK), g_ref[:, ks]
            both = overlap(h, vs)
            pairs = low(jnp.where(row == column, both, 0.0))
            grad_q, grad_k = dot_nn(pairs, low(keys)), dot_tn(pairs, low(queries))
            grad_c = jnp.zeros_like(grad_q)
            for half in halvings(chunk):
                here, selector = halving_parts(chunk, half)
                factor = jnp.exp(exact_sum(selector, decay))
                far, near = low(queries * factor), low(keys * factor)
                pairs = low(jnp.where(here, both, 0.0))
                for_q, for_k = dot_nn(pairs, near), dot_tn(pairs, far)
                grad_q += factor * for_q
                grad_k += factor * for_k
                grad_c += far.astype(jnp.float32) * for_q - near.astype(jnp.float32) * for_k
            dqi[:, ks] = grad_q
            dki[:, ks] = grad_k
            dci[:, ks] = grad_c

    before = as_selector(row > column)
    after = as_selector(row <= column)
    for h in range(HEADS):
        ks, vs = slice(h * DK, (h + 1) * DK), slice(h * DV, (h + 1) * DV)
        values, grad_out = low(at_head(v_refs, h, DV)), low(do_ref[:, vs])
        held = st_ref[0, h] + in_ref[0, h] * begun[:, ks]
        ahead = later[h]
        ahead_low = low(ahead)
        queries = at_head(q_refs, h, DK) * scale * grown[:, ks]
        keys = at_head(k_refs, h, DK) * faded[:, ks]
        out_ref, place = (out0, out1)[h // PAIR], h % PAIR
        from_state = dot_nn(grad_out, low(held))
        from_later = dot_nn(values, ahead_low)
        out_ref[:, place * DK : (place + 1) * DK] = low((dqi[:, ks] + grown[:, ks] * from_state) * scale)
        out_ref[:, KEYS // 2 + place * DK : KEYS // 2 + (place + 1) * DK] = low(dki[:, ks] + faded[:, ks] * from_later)
        out_ref[:, KEYS + place * DV : KEYS + (place + 1) * DV] = low(
            dot_tn(a_ref[0, h], grad_out) + dot_nt(low(keys), ahead_low)
        )
        through = kept[:, ks] * jnp.sum(held * ahead, axis=0, keepdims=True)
        dg_ref[:, ks] = (
            exact_sum(after, dci[:, ks] + queries * from_state)
            + exact_sum(before, keys * from_later)
            + through
        )
        later[h] = ahead * kept[:, ks] + dot_tn(grad_out, low(queries))
    out0[:, KEYS + VALUES // 2 :] = dog0[...]
    out1[:, KEYS + VALUES // 2 :] = dog1[...]


def mix_forward_kernel(o_ref, qf_ref, in_ref, og0, og1, gain_ref, att_ref, mixed_ref):
    gain = gain_ref[...]
    for h in range(HEADS):
        ks, vs = slice(h * DK, (h + 1) * DK), slice(h * DV, (h + 1) * DV)
        attended = o_ref[:, vs] + dot_nt(qf_ref[:, ks], low(in_ref[0, h]))
        att_ref[:, vs] = attended
        outgate = at_head((og0, og1), h, DV)
        mixed_ref[:, vs] = low(normalize(attended) * gain * (outgate * jax.nn.sigmoid(outgate)))


def mix_backward_kernel(dm_ref, att_ref, og0, og1, gain_ref, qf_ref, do_ref, dog0, dog1, grad_ref, dgain_ref):
    @pl.when(pl.program_id(1) == 0)
    def _():
        grad_ref[...] = jnp.zeros_like(grad_ref)
        dgain_ref[...] = jnp.zeros_like(dgain_ref)

    gain = gain_ref[...]
    for h in range(HEADS):
        ks, vs = slice(h * DK, (h + 1) * DK), slice(h * DV, (h + 1) * DV)
        attended, outgate, grad = att_ref[:, vs], at_head((og0, og1), h, DV), dm_ref[:, vs]
        dog_ref, place = (dog0, dog1)[h // PAIR], h % PAIR
        inverse = lax.rsqrt(jnp.mean(attended * attended, axis=-1, keepdims=True) + epsilon)
        normed = attended * inverse
        sigma = jax.nn.sigmoid(outgate)
        gated = grad * (outgate * sigma)
        dog_ref[:, place * DV : (place + 1) * DV] = low(grad * normed * gain * (sigma + outgate * sigma * (1.0 - sigma)))
        dgain_ref[0] += jnp.sum(gated * normed, axis=0, keepdims=True)
        inner = gated * gain
        result = inverse * (inner - normed * jnp.mean(inner * normed, axis=-1, keepdims=True))
        do_ref[:, vs] = result
        grad_ref[0, h] += dot_tn(low(result), qf_ref[:, ks])


def rows_spec(chunk, chunks, width, backward=False):
    if backward:
        return pl.BlockSpec((chunk, width), lambda s, c: (s * chunks + chunks - 1 - c, 0))
    return pl.BlockSpec((chunk, width), lambda s, c: (s * chunks + c, 0))


def item_spec(shape):
    return pl.BlockSpec((1,) + shape, lambda s, c: (s,) + (0,) * len(shape))


def chunk_spec(chunks, shape, backward=False):
    if backward:
        return pl.BlockSpec((1,) + shape, lambda s, c: (s * chunks + chunks - 1 - c,) + (0,) * len(shape))
    return pl.BlockSpec((1,) + shape, lambda s, c: (s * chunks + c,) + (0,) * len(shape))


def shaped(shape, kind=jnp.float32):
    return jax.ShapeDtypeStruct(shape, kind)


def packed_specs(chunk, chunks, backward=False):
    def at(width, place):
        whole = rows_spec(chunk, chunks, width, backward)
        return pl.BlockSpec(whole.block_shape, lambda s, c: (whole.index_map(s, c)[0], place))

    return [at(KEYS // 2, 0), at(KEYS // 2, 1), at(VALUES // 2, 1), at(VALUES // 2, 2)]


KEYS, VALUES = HEADS * DK, HEADS * DV
PACKED = KEYS + VALUES
ROOM = pltpu.CompilerParams(vmem_limit_bytes=40 * 1024 * 1024)


def scan_forward(mine, theirs, gates, seqs, chunk):
    rows = gates.shape[0]
    chunks = rows // seqs // chunk
    keyed, valued = rows_spec(chunk, chunks, KEYS), rows_spec(chunk, chunks, VALUES)
    return pl.pallas_call(
        functools.partial(scan_forward_kernel, chunk),
        grid=(seqs, chunks),
        in_specs=packed_specs(chunk, chunks)[:3] * 2 + [keyed],
        out_specs=[
            valued,
            keyed,
            chunk_spec(chunks, (HEADS, chunk, chunk)),
            chunk_spec(chunks, (HEADS, DV, DK)),
            chunk_spec(chunks, (1, KEYS)),
            item_spec((HEADS, DV + 8, DK)),
        ],
        out_shape=[
            shaped((rows, VALUES)),
            shaped((rows, KEYS), jnp.bfloat16),
            shaped((seqs * chunks, HEADS, chunk, chunk), jnp.bfloat16),
            shaped((seqs * chunks, HEADS, DV, DK)),
            shaped((seqs * chunks, 1, KEYS)),
            shaped((seqs, HEADS, DV + 8, DK)),
        ],
        scratch_shapes=[
            pltpu.VMEM((HEADS, DV, DK), jnp.float32),
            pltpu.VMEM((1, KEYS), jnp.float32),
            pltpu.VMEM((HEADS, chunk, chunk), jnp.float32),
        ],
        compiler_params=ROOM,
        name="scan_forward",
    )(mine, mine, mine, theirs, theirs, theirs, gates)


def scan_backward(
    mine, theirs, gates, scores, states, starts, incoming, grad_out, later, outgate_grads, seqs, chunk
):
    rows = gates.shape[0]
    chunks = rows // seqs // chunk
    keyed, valued = rows_spec(chunk, chunks, KEYS, True), rows_spec(chunk, chunks, VALUES, True)
    return pl.pallas_call(
        functools.partial(scan_backward_kernel, chunk),
        grid=(seqs, chunks),
        in_specs=[
            *packed_specs(chunk, chunks, True)[:3] * 2,
            keyed,
            chunk_spec(chunks, (HEADS, chunk, chunk), True),
            chunk_spec(chunks, (HEADS, DV, DK), True),
            chunk_spec(chunks, (1, KEYS), True),
            item_spec((HEADS, DV, DK)),
            valued,
            item_spec((HEADS, DV, DK)),
            *[rows_spec(chunk, chunks, VALUES // 2, True)] * 2,
        ],
        out_specs=[*[rows_spec(chunk, chunks, PACKED, True)] * 2, keyed],
        out_shape=[*[shaped((rows, PACKED), jnp.bfloat16)] * 2, shaped((rows, KEYS))],
        scratch_shapes=[pltpu.VMEM((HEADS, DV, DK), jnp.float32)] + [pltpu.VMEM((chunk, KEYS), jnp.float32)] * 3,
        compiler_params=ROOM,
        name="scan_backward",
    )(
        mine, mine, mine, theirs, theirs, theirs,
        gates, scores, states, starts, incoming, grad_out, later, *outgate_grads,
    )


def mix_forward(local_out, forget, incoming, mine, theirs, gain, seqs, chunk):
    rows = local_out.shape[0]
    chunks = rows // seqs // chunk
    keyed, valued = rows_spec(chunk, chunks, KEYS), rows_spec(chunk, chunks, VALUES)
    whole_gain = pl.BlockSpec((1, DV), lambda s, c: (0, 0))
    return pl.pallas_call(
        mix_forward_kernel,
        grid=(seqs, chunks),
        in_specs=[valued, keyed, item_spec((HEADS, DV, DK)), *packed_specs(chunk, chunks)[3:] * 2, whole_gain],
        out_specs=[valued, valued],
        out_shape=[shaped((rows, VALUES)), shaped((rows, VALUES), jnp.bfloat16)],
        compiler_params=ROOM,
        name="mix_forward",
    )(local_out, forget, incoming, mine, theirs, gain)


def mix_backward(mixed_grad, attended, mine, theirs, gain, forget, seqs, chunk):
    rows = attended.shape[0]
    chunks = rows // seqs // chunk
    keyed, valued = rows_spec(chunk, chunks, KEYS), rows_spec(chunk, chunks, VALUES)
    whole_gain = pl.BlockSpec((1, DV), lambda s, c: (0, 0))
    return pl.pallas_call(
        mix_backward_kernel,
        grid=(seqs, chunks),
        in_specs=[valued, valued, *packed_specs(chunk, chunks)[3:] * 2, whole_gain, keyed],
        out_specs=[
            valued,
            *[rows_spec(chunk, chunks, VALUES // 2)] * 2,
            item_spec((HEADS, DV, DK)),
            item_spec((1, DV)),
        ],
        out_shape=[
            shaped((rows, VALUES)),
            *[shaped((rows, VALUES // 2), jnp.bfloat16)] * 2,
            shaped((seqs, HEADS, DV, DK)),
            shaped((seqs, 1, DV)),
        ],
        compiler_params=ROOM,
        name="mix_backward",
    )(mixed_grad, attended, mine, theirs, gain, forget)


def from_neighbours(summary, step):
    count = lax.axis_size("seq")
    total, factor = None, None
    for distance in range(1, count):
        shift = step * distance
        pairs = [(i, i + shift) for i in range(count) if 0 <= i + shift < count]
        came = lax.ppermute(summary, "seq", pairs)
        state, retain = came[:, :, :DV].astype(jnp.float32), came[:, :, DV : DV + 1].astype(jnp.float32)
        if total is None:
            total, factor = state, retain
        else:
            total, factor = total + factor * state, factor * retain
    return total


def product(left, right):
    return jnp.dot(left, right, preferred_element_type=jnp.float32)


def product_left(left, right):
    return lax.dot_general(
        left, right, (((0,), (0,)), ((), ())), preferred_element_type=jnp.float32
    )


def product_right(left, right):
    return lax.dot_general(
        left, right, (((1,), (1,)), ((), ())), preferred_element_type=jnp.float32
    )


EVERYWHERE = ("z", "core", "seq")


def swapped(array):
    return lax.ppermute(array, "core", [(0, 1), (1, 0)])


def after(array, other):
    def nothing(array_ref, other_ref, out_ref):
        pass

    anywhere = pl.BlockSpec(memory_space=pl.ANY)
    return pl.pallas_call(
        nothing,
        in_specs=[anywhere, anywhere],
        out_specs=anywhere,
        out_shape=shaped(array.shape, array.dtype),
        input_output_aliases={0: 0},
        name="after",
    )(array, other)


def first_core():
    return lax.axis_index("core") == 0


def own_half(array, dim, other=False):
    core = lax.axis_index("core")
    size = array.shape[dim] // 2
    return lax.dynamic_slice_in_dim(array, ((1 - core) if other else core) * size, size, dim)


def joined(mine, theirs, dim):
    return jnp.where(
        first_core(), jnp.concatenate([mine, theirs], dim), jnp.concatenate([theirs, mine], dim)
    )


def halves_of(array):
    half = array.shape[1] // 2
    first = first_core()
    return (
        jnp.where(first, array[:, :half], array[:, half:]),
        jnp.where(first, array[:, half:], array[:, :half]),
    )


def scattered(array):
    return lax.psum_scatter(array, "seq", scatter_dimension=0, tiled=True)


def direct(count):
    return count in (2, 4)


def spread(array):
    count, me = lax.axis_size("seq"), lax.axis_index("seq")
    if not direct(count):
        return lax.all_gather(array, "seq", tiled=True)
    rows = array.shape[0]
    whole = jnp.zeros((count * rows, array.shape[1]), array.dtype)
    whole = lax.dynamic_update_slice_in_dim(whole, array, me * rows, 0)
    for distance in range(1, count):
        came = lax.ppermute(array, "seq", [(i, i ^ distance) for i in range(count)])
        whole = lax.dynamic_update_slice_in_dim(whole, came, (me ^ distance) * rows, 0)
    return whole


def gathered_sum(array, late):
    count, me = lax.axis_size("seq"), lax.axis_index("seq")
    if not direct(count):
        return scattered(array), late
    rows = array.shape[0] // count
    pieces = []
    total = lax.dynamic_slice_in_dim(array, me * rows, rows, 0).astype(jnp.float32)
    for distance in range(1, count):
        piece = lax.dynamic_slice_in_dim(array, (me ^ distance) * rows, rows, 0)
        came = lax.ppermute(piece, "seq", [(i, i ^ distance) for i in range(count)])
        pieces.append(after(came, late))
        total = total + pieces[-1].astype(jnp.float32)
    return low(total), pieces[0]


def local(
    tokens,
    mixer_gain,
    query_weight,
    key_weight,
    value_weight,
    decay_down,
    decay_up,
    decay_bias,
    outgate_weight,
    head_gain,
    output_weight,
    channel_gain,
    gate_weight,
    up_weight,
    down_weight,
    cotangent,
):
    seqs_here, seg_len, width = tokens.shape
    rows_here = seqs_here * seg_len
    count = lax.axis_size("seq")
    ff = gate_weight.shape[1]

    shard_rows = query_weight.shape[0]
    smalls = [mixer_gain, decay_down, decay_up, decay_bias, head_gain, channel_gain]
    flat = jnp.concatenate([small.reshape(-1) for small in smalls])
    flat_size = flat.size
    extra = -(-flat_size // (shard_rows * 128)) * 128
    flat = jnp.pad(flat, (0, shard_rows * extra - flat_size)).reshape(shard_rows, extra)
    mixer_packed = jnp.concatenate(
        [
            own_half(weight, 1)
            for weight in (query_weight, key_weight, value_weight, outgate_weight)
        ]
        + [flat],
        axis=1,
    )
    ffn_packed = jnp.concatenate([own_half(gate_weight, 1), own_half(up_weight, 1)], axis=1)
    mixer_mine = lax.all_gather(mixer_packed, "seq", tiled=True)
    ffn_mine = lax.all_gather(ffn_packed, "seq", tiled=True)
    output_mine = spread(own_half(output_weight, 1))
    mixer_mine = after(after(mixer_mine, output_mine), ffn_packed)
    down_mine = spread(after(own_half(down_weight, 1), mixer_mine))
    mixer_theirs, output_theirs = swapped(mixer_mine), swapped(output_mine)
    mixer_theirs = after(mixer_theirs, output_theirs)
    projection_mine, projection_theirs = mixer_mine[:, :PACKED], mixer_theirs[:, :PACKED]
    small_all = mixer_mine[:, PACKED:].reshape(count, -1)
    pieces, begin = [], 0
    for small in smalls:
        pieces.append(small_all[:, begin : begin + small.size].reshape((count,) + small.shape))
        begin += small.size
    gain_one = pieces[0].reshape(-1).astype(jnp.float32)
    decay_down_all = pieces[1].reshape(width, -1)
    decay_up_f = pieces[2].transpose(1, 0, 2).reshape(decay_up.shape[0], -1).astype(jnp.float32)
    decay_bias_f = pieces[3].reshape(1, -1).astype(jnp.float32)
    head_gain_f = pieces[4].reshape(-1).astype(jnp.float32)
    gain_two = pieces[5].reshape(-1).astype(jnp.float32)
    decay_up_f = jnp.concatenate(halves_of(decay_up_f), 1)
    decay_bias_f = jnp.concatenate(halves_of(decay_bias_f), 1)

    inputs = tokens.reshape(rows_here, width).astype(jnp.float32)

    def first_norm(inputs_in, gain_in):
        return normalize(inputs_in) * gain_in

    normed_one = first_norm(inputs, gain_one).astype(jnp.bfloat16)
    low_rank = product(normed_one, decay_down_all)

    def gate_fn(rank_in, up_in, bias_in):
        return (
            jax.nn.log_sigmoid(jnp.dot(rank_in, up_in, precision=highest_precision) + bias_in)
            / normalizer
        )

    gates = gate_fn(low_rank, decay_up_f, decay_bias_f)
    mine = product(normed_one, projection_mine)
    theirs = product(normed_one, projection_theirs)
    chunk = min(CHUNK, seg_len)
    local_out, forget, scores, states, starts, summary = scan_forward(mine, theirs, gates, seqs_here, chunk)
    incoming_state = after(from_neighbours(low(summary), 1), down_mine)
    attended, mixed = mix_forward(
        local_out, forget, incoming_state, mine, theirs, head_gain_f[None, :], seqs_here, chunk
    )
    down_theirs = swapped(down_mine)
    mixed = jnp.concatenate(halves_of(after(mixed, down_theirs)), 1)
    resid = inputs + joined(product(mixed, output_mine), product(mixed, output_theirs), 1)
    normed_two = first_norm(resid, gain_two).astype(jnp.bfloat16)
    ffn_mine = after(ffn_mine, normed_two)
    ffn_theirs = swapped(ffn_mine)

    def swiglu(both):
        gate_pre, up_pre = both[:, : ff // 2], both[:, ff // 2 :]
        return low(gate_pre * jax.nn.sigmoid(gate_pre) * up_pre)

    both_mine, both_theirs = product(normed_two, ffn_mine), product(normed_two, ffn_theirs)
    hidden = joined(swiglu(both_mine), swiglu(both_theirs), 1)
    result = resid + joined(product(hidden, down_mine), product(hidden, down_theirs), 1)
    block_out = result.astype(jnp.bfloat16).reshape(tokens.shape)

    grad_low = cotangent.reshape(rows_here, width)
    grad_out = grad_low.astype(jnp.float32)
    low_mine, low_theirs = halves_of(grad_low)
    hidden_grad = product_right(low_mine, down_mine) + product_right(low_theirs, down_theirs)

    def swiglu_back(both, grad):
        gate_pre, up_pre = both[:, : ff // 2], both[:, ff // 2 :]
        sigma = jax.nn.sigmoid(gate_pre)
        return jnp.concatenate(
            [
                low(grad * up_pre * (sigma + gate_pre * sigma * (1.0 - sigma))),
                low(grad * (gate_pre * sigma)),
            ],
            axis=1,
        )

    grad_mine, grad_theirs = halves_of(hidden_grad)
    back_mine, back_theirs = swiglu_back(both_mine, grad_mine), swiglu_back(both_theirs, grad_theirs)

    down_came = swapped(low(product_left(hidden, low_theirs)))
    ffn_came = swapped(low(product_left(normed_two, back_theirs)))
    down_pair = low(product_left(hidden, low_mine) + down_came.astype(jnp.float32))
    back_mine = after(back_mine, down_pair)
    normed_two_grad = product_right(back_mine, ffn_mine) + product_right(back_theirs, ffn_theirs)
    norm_pulled = jax.vjp(first_norm, resid, gain_two)[1](normed_two_grad)
    resid_grad = grad_out + norm_pulled[0]
    channel_gain_grad = norm_pulled[1]
    branch_grad = resid_grad.astype(jnp.bfloat16)
    branch_mine, branch_theirs = halves_of(branch_grad)
    mixed_grad = product_right(branch_mine, output_mine) + product_right(branch_theirs, output_theirs)
    mixed_grad = jnp.concatenate(halves_of(mixed_grad), 1)
    ffn_pair = low(product_left(normed_two, back_mine) + ffn_came.astype(jnp.float32))
    ffn_share = scattered(ffn_pair)
    mixed_grad = after(mixed_grad, ffn_pair)
    attended_grad, *outgate_grads, state_grad, head_gain_grad = mix_backward(
        mixed_grad, attended, mine, theirs, head_gain_f[None, :], forget, seqs_here, chunk
    )
    head_gain_grad = head_gain_grad.sum((0, 1))
    later_grad = from_neighbours(
        jnp.concatenate([state_grad, summary[:, :, DV:]], axis=2).astype(jnp.bfloat16), -1
    )
    output_came = swapped(low(product_left(mixed, after(branch_theirs, attended_grad))))
    output_pair = product_left(mixed, after(branch_mine, attended_grad)) + output_came.astype(jnp.float32)
    output_pair = low(output_pair)
    down_share, _ = gathered_sum(down_pair, attended_grad)
    attended_grad = after(after(attended_grad, output_pair), down_share)
    packed_mine, packed_theirs, gates_grad = scan_backward(
        mine, theirs, gates, scores, states, starts, incoming_state,
        attended_grad, later_grad, outgate_grads, seqs_here, chunk,
    )
    packed_theirs = after(packed_theirs, ffn_share)
    packed_came = swapped(low(product_left(normed_one, packed_theirs)))
    mixer_pair = low(product_left(normed_one, packed_mine) + packed_came.astype(jnp.float32))
    mixer_share, mixer_first = gathered_sum(mixer_pair, mixer_pair)
    gates_grad = after(gates_grad, mixer_first)
    gate_pulled = jax.vjp(gate_fn, low_rank, decay_up_f, decay_bias_f)[1](gates_grad)
    low_rank_grad = gate_pulled[0].astype(jnp.bfloat16)
    decay_up_grad = jnp.concatenate(halves_of(gate_pulled[1]), 1)
    decay_bias_grad = jnp.concatenate(halves_of(gate_pulled[2]), 1)[0]
    decay_down_grad = product_left(normed_one, low_rank_grad)
    normed_one_grad = (
        product_right(after(packed_mine, mixer_first), projection_mine)
        + product_right(after(packed_theirs, mixer_first), projection_theirs)
        + product_right(low_rank_grad, decay_down_all)
    )
    first_pulled = jax.vjp(first_norm, inputs, gain_one)[1](normed_one_grad)
    tokens_grad = (resid_grad + first_pulled[0]).reshape(tokens.shape)

    def by_shard(grad, dim=0):
        shape = grad.shape[:dim] + (count, grad.shape[dim] // count) + grad.shape[dim + 1 :]
        return jnp.moveaxis(grad.reshape(shape), dim, 0).reshape(count, -1)

    small_grads = jnp.concatenate(
        [
            by_shard(first_pulled[1]),
            by_shard(decay_down_grad),
            by_shard(decay_up_grad, 1),
            by_shard(decay_bias_grad),
            by_shard(head_gain_grad),
            by_shard(channel_gain_grad),
        ],
        axis=1,
    )
    small_rows = -(-flat_size // (width // 2 * 16)) * 16
    small_grads = jnp.pad(low(small_grads), ((0, 0), (0, small_rows * width // 2 - flat_size)))
    rest_pair = jnp.concatenate(
        [
            output_pair.reshape(count, shard_rows, width // 2),
            small_grads.reshape(count, small_rows, width // 2),
        ],
        axis=1,
    ).reshape(-1, width // 2)
    rest_share, _ = gathered_sum(rest_pair, mixer_pair)

    ffn_total = after(lax.psum(ffn_share, "z"), rest_share)
    ffn_other = swapped(ffn_total)
    mixer_total, down_total, rest_total = lax.psum(
        tuple(after(share, ffn_total) for share in (mixer_share, down_share, rest_share)), "z"
    )
    mixer_other, down_other, rest_other = (
        swapped(total) for total in (mixer_total, down_total, rest_total)
    )

    def both_cores(total, other, begin, end):
        return joined(total[:, begin:end], other[:, begin:end], 1).astype(jnp.float32)

    summed = rest_total[shard_rows:].astype(jnp.float32) + rest_other[shard_rows:].astype(jnp.float32)
    summed, shares, begin = summed.reshape(-1), [], 0
    for small in smalls:
        shares.append(summed[begin : begin + small.size].reshape(small.shape))
        begin += small.size

    columns = (0, KEYS // 2, KEYS, KEYS + VALUES // 2, PACKED)
    query_g, key_g, value_g, outgate_g = (
        both_cores(mixer_total, mixer_other, a, b) for a, b in zip(columns[:-1], columns[1:])
    )
    return (
        block_out,
        tokens_grad,
        shares[0],
        query_g,
        key_g,
        value_g,
        shares[1],
        shares[2],
        shares[3],
        outgate_g,
        shares[4],
        joined(rest_total[:shard_rows], rest_other[:shard_rows], 1).astype(jnp.float32),
        shares[5],
        both_cores(ffn_total, ffn_other, 0, ff // 2),
        both_cores(ffn_total, ffn_other, ff // 2, ff),
        joined(down_total, down_other, 1).astype(jnp.float32),
    )


def solution(mesh):
    rep, seq = mesh.shape["rep"], mesh.shape["seq"]
    cores = Mesh(mesh.devices.reshape(rep // 2, 2, seq), EVERYWHERE)
    sequences, weights = P(("z", "core"), "seq", None), P("seq", None)
    in_specs = (
        sequences,
        P("seq"),
        weights,
        weights,
        weights,
        weights,
        P(None, "seq"),
        P("seq"),
        weights,
        P("seq"),
        weights,
        P("seq"),
        weights,
        weights,
        weights,
        sequences,
    )
    out_specs = (sequences, *in_specs[:15])
    return jax.shard_map(local, mesh=cores, in_specs=in_specs, out_specs=out_specs, check_vma=False)
```

```python
import functools

import jax
import jax.numpy as jnp
from jax import lax
from jax.experimental import pallas as pl
from jax.experimental.pallas import tpu as pltpu
from jax.sharding import Mesh, PartitionSpec as P

HEADS = 4
DK = 128
DV = 256
PAIR = HEADS // 2
CHUNK = 128
SAFE = 60.0


epsilon = 1e-06
normalizer = 16.0
highest_precision = lax.Precision.HIGHEST


def normalize(values_in):
    return values_in * lax.rsqrt(jnp.mean(values_in * values_in, axis=-1, keepdims=True) + epsilon)


def dot_nn(left, right):
    return lax.dot_general(left, right, (((1,), (0,)), ((), ())), preferred_element_type=jnp.float32)


def dot_nt(left, right):
    return lax.dot_general(left, right, (((1,), (1,)), ((), ())), preferred_element_type=jnp.float32)


def dot_tn(left, right):
    return lax.dot_general(left, right, (((0,), (0,)), ((), ())), preferred_element_type=jnp.float32)


def low(array):
    return array.astype(jnp.bfloat16)


def exact_sum(selector, array):
    high = low(array)
    rest = low(array - high.astype(jnp.float32))
    return dot_nn(selector, high) + dot_nn(selector, rest)


def halves(array):
    high = low(array)
    return high, low(array - high.astype(jnp.float32))


def close_dot(dot, left, right):
    (left_high, left_rest), (right_high, right_rest) = halves(left), halves(right)
    return dot(left_high, right_high) + (dot(left_high, right_rest) + dot(left_rest, right_high))


def at_head(refs, head, size):
    place = head % PAIR
    return refs[head // PAIR][:, place * size : (place + 1) * size]


def positions(chunk):
    row = lax.broadcasted_iota(jnp.int32, (chunk, chunk), 0)
    column = lax.broadcasted_iota(jnp.int32, (chunk, chunk), 1)
    return row, column


def as_selector(mask):
    return low(jnp.where(mask, 1.0, 0.0))


def halvings(chunk):
    sizes, half = [], chunk // 2
    while half >= 1:
        sizes.append(half)
        half //= 2
    return sizes


def halving_parts(chunk, half):
    row, column = positions(chunk)
    row_late = (row & half) != 0
    pairs = ((row & -(2 * half)) == (column & -(2 * half))) & row_late & ((column & half) == 0)
    middle = (row & -(2 * half)) + (half - 1)
    late = row_late & (column > middle) & (column <= row)
    early = jnp.logical_not(row_late) & (column > row) & (column <= middle)
    return pairs, as_selector(late | early)


def scan_forward_kernel(chunk, q0, k0, v0, q1, k1, v1, g_ref, o_ref, qf_ref, a_ref, st_ref, cs_ref, sum_ref, state, start, table):
    step, steps = pl.program_id(1), pl.num_programs(1)
    q_refs, k_refs, v_refs = (q0, q1), (k0, k1), (v0, v1)

    @pl.when(step == 0)
    def _():
        state[...] = jnp.zeros_like(state)
        start[...] = jnp.zeros_like(start)

    row, column = positions(chunk)
    gates = g_ref[...]
    cumul = exact_sum(as_selector(row >= column), gates)
    left = exact_sum(as_selector(row < column), gates)
    finish = cumul[chunk - 1 : chunk, :]
    mild = jnp.min(finish) > -SAFE
    begin = start[...]
    cs_ref[0] = begin
    grown = jnp.exp(cumul)
    faded = jnp.exp(left)
    begun = jnp.exp(begin)
    kept = jnp.exp(finish)
    scale = DK ** (-0.5)

    @pl.when(mild)
    def _():
        for h in range(HEADS):
            ks = slice(h * DK, (h + 1) * DK)
            far = at_head(q_refs, h, DK) * scale * grown[:, ks]
            near = at_head(k_refs, h, DK) * jnp.exp(-cumul[:, ks])
            table[h] = jnp.where(row >= column, close_dot(dot_nt, far, near), 0.0)

    @pl.when(jnp.logical_not(mild))
    def _():
        for h in range(HEADS):
            ks = slice(h * DK, (h + 1) * DK)
            queries, keys, decay = at_head(q_refs, h, DK) * scale, at_head(k_refs, h, DK), g_ref[:, ks]
            total = jnp.where(row == column, close_dot(dot_nt, queries, keys), 0.0)
            for half in halvings(chunk):
                pairs, selector = halving_parts(chunk, half)
                factor = jnp.exp(exact_sum(selector, decay))
                total = jnp.where(pairs, close_dot(dot_nt, queries * factor, keys * factor), total)
            table[h] = total

    for h in range(HEADS):
        ks, vs = slice(h * DK, (h + 1) * DK), slice(h * DV, (h + 1) * DV)
        queries = at_head(q_refs, h, DK) * scale * grown[:, ks]
        own_values = at_head(v_refs, h, DV)
        values = low(own_values)
        held = state[h]
        st_ref[0, h] = held
        scores = table[h]
        a_ref[0, h] = low(scores)
        o_ref[:, vs] = close_dot(dot_nn, scores, own_values) + dot_nt(low(queries), low(held))
        qf_ref[:, ks] = low(queries * begun[:, ks])
        state[h] = held * kept[:, ks] + dot_tn(values, low(at_head(k_refs, h, DK) * faded[:, ks]))
    start[...] = begin + finish

    @pl.when(step == steps - 1)
    def _():
        for h in range(HEADS):
            ks = slice(h * DK, (h + 1) * DK)
            sum_ref[0, h, :DV] = state[h]
            sum_ref[0, h, DV:] = jnp.broadcast_to(jnp.exp(begin[:, ks] + finish[:, ks]), (8, DK))


def scan_backward_kernel(
    chunk, q0, k0, v0, q1, k1, v1, g_ref, a_ref, st_ref, cs_ref, in_ref, do_ref, later_ref, dog0, dog1,
    out0, out1, dg_ref, later, dqi, dki, dci,
):
    q_refs, k_refs, v_refs = (q0, q1), (k0, k1), (v0, v1)

    @pl.when(pl.program_id(1) == 0)
    def _():
        later[...] = later_ref[0]

    row, column = positions(chunk)
    lower = row >= column
    gates = g_ref[...]
    cumul = exact_sum(as_selector(lower), gates)
    left = exact_sum(as_selector(row < column), gates)
    finish = cumul[chunk - 1 : chunk, :]
    mild = jnp.min(finish) > -SAFE
    grown = jnp.exp(cumul)
    faded = jnp.exp(left)
    kept = jnp.exp(finish)
    begun = jnp.exp(cs_ref[0])
    scale = DK ** (-0.5)

    def overlap(h, vs):
        return close_dot(dot_nt, do_ref[:, vs], at_head(v_refs, h, DV))

    @pl.when(mild)
    def _():
        for h in range(HEADS):
            ks, vs = slice(h * DK, (h + 1) * DK), slice(h * DV, (h + 1) * DV)
            shrunk = jnp.exp(-cumul[:, ks])
            far = low(at_head(q_refs, h, DK) * scale * grown[:, ks])
            near = low(at_head(k_refs, h, DK) * shrunk)
            pairs = low(jnp.where(lower, overlap(h, vs), 0.0))
            for_q, for_k = dot_nn(pairs, near), dot_tn(pairs, far)
            dqi[:, ks] = grown[:, ks] * for_q
            dki[:, ks] = shrunk * for_k
            dci[:, ks] = far.astype(jnp.float32) * for_q - near.astype(jnp.float32) * for_k

    @pl.when(jnp.logical_not(mild))
    def _():
        for h in range(HEADS):
            ks, vs = slice(h * DK, (h + 1) * DK), slice(h * DV, (h + 1) * DV)
            queries, keys, decay = at_head(q_refs, h, DK) * scale, at_head(k_refs, h, DK), g_ref[:, ks]
            both = overlap(h, vs)
            pairs = low(jnp.where(row == column, both, 0.0))
            grad_q, grad_k = dot_nn(pairs, low(keys)), dot_tn(pairs, low(queries))
            grad_c = jnp.zeros_like(grad_q)
            for half in halvings(chunk):
                here, selector = halving_parts(chunk, half)
                factor = jnp.exp(exact_sum(selector, decay))
                far, near = low(queries * factor), low(keys * factor)
                pairs = low(jnp.where(here, both, 0.0))
                for_q, for_k = dot_nn(pairs, near), dot_tn(pairs, far)
                grad_q += factor * for_q
                grad_k += factor * for_k
                grad_c += far.astype(jnp.float32) * for_q - near.astype(jnp.float32) * for_k
            dqi[:, ks] = grad_q
            dki[:, ks] = grad_k
            dci[:, ks] = grad_c

    before = as_selector(row > column)
    after = as_selector(row <= column)
    for h in range(HEADS):
        ks, vs = slice(h * DK, (h + 1) * DK), slice(h * DV, (h + 1) * DV)
        values, grad_out = low(at_head(v_refs, h, DV)), low(do_ref[:, vs])
        held = st_ref[0, h] + in_ref[0, h] * begun[:, ks]
        ahead = later[h]
        ahead_low = low(ahead)
        queries = at_head(q_refs, h, DK) * scale * grown[:, ks]
        keys = at_head(k_refs, h, DK) * faded[:, ks]
        out_ref, place = (out0, out1)[h // PAIR], h % PAIR
        from_state = dot_nn(grad_out, low(held))
        from_later = dot_nn(values, ahead_low)
        out_ref[:, place * DK : (place + 1) * DK] = low((dqi[:, ks] + grown[:, ks] * from_state) * scale)
        out_ref[:, KEYS // 2 + place * DK : KEYS // 2 + (place + 1) * DK] = low(dki[:, ks] + faded[:, ks] * from_later)
        out_ref[:, KEYS + place * DV : KEYS + (place + 1) * DV] = low(
            dot_tn(a_ref[0, h], grad_out) + dot_nt(low(keys), ahead_low)
        )
        through = kept[:, ks] * jnp.sum(held * ahead, axis=0, keepdims=True)
        dg_ref[:, ks] = (
            exact_sum(after, dci[:, ks] + queries * from_state)
            + exact_sum(before, keys * from_later)
            + through
        )
        later[h] = ahead * kept[:, ks] + dot_tn(grad_out, low(queries))
    out0[:, KEYS + VALUES // 2 :] = dog0[...]
    out1[:, KEYS + VALUES // 2 :] = dog1[...]


def mix_forward_kernel(o_ref, qf_ref, in_ref, og0, og1, gain_ref, att_ref, mixed_ref):
    gain = gain_ref[...]
    for h in range(HEADS):
        ks, vs = slice(h * DK, (h + 1) * DK), slice(h * DV, (h + 1) * DV)
        attended = o_ref[:, vs] + dot_nt(qf_ref[:, ks], low(in_ref[0, h]))
        att_ref[:, vs] = attended
        outgate = at_head((og0, og1), h, DV)
        mixed_ref[:, vs] = low(normalize(attended) * gain * (outgate * jax.nn.sigmoid(outgate)))


def mix_backward_kernel(dm_ref, att_ref, og0, og1, gain_ref, qf_ref, do_ref, dog0, dog1, grad_ref, dgain_ref):
    @pl.when(pl.program_id(1) == 0)
    def _():
        grad_ref[...] = jnp.zeros_like(grad_ref)
        dgain_ref[...] = jnp.zeros_like(dgain_ref)

    gain = gain_ref[...]
    for h in range(HEADS):
        ks, vs = slice(h * DK, (h + 1) * DK), slice(h * DV, (h + 1) * DV)
        attended, outgate, grad = att_ref[:, vs], at_head((og0, og1), h, DV), dm_ref[:, vs]
        dog_ref, place = (dog0, dog1)[h // PAIR], h % PAIR
        inverse = lax.rsqrt(jnp.mean(attended * attended, axis=-1, keepdims=True) + epsilon)
        normed = attended * inverse
        sigma = jax.nn.sigmoid(outgate)
        gated = grad * (outgate * sigma)
        dog_ref[:, place * DV : (place + 1) * DV] = low(grad * normed * gain * (sigma + outgate * sigma * (1.0 - sigma)))
        dgain_ref[0] += jnp.sum(gated * normed, axis=0, keepdims=True)
        inner = gated * gain
        result = inverse * (inner - normed * jnp.mean(inner * normed, axis=-1, keepdims=True))
        do_ref[:, vs] = result
        grad_ref[0, h] += dot_tn(low(result), qf_ref[:, ks])


def rows_spec(chunk, chunks, width, backward=False):
    if backward:
        return pl.BlockSpec((chunk, width), lambda s, c: (s * chunks + chunks - 1 - c, 0))
    return pl.BlockSpec((chunk, width), lambda s, c: (s * chunks + c, 0))


def item_spec(shape):
    return pl.BlockSpec((1,) + shape, lambda s, c: (s,) + (0,) * len(shape))


def chunk_spec(chunks, shape, backward=False):
    if backward:
        return pl.BlockSpec((1,) + shape, lambda s, c: (s * chunks + chunks - 1 - c,) + (0,) * len(shape))
    return pl.BlockSpec((1,) + shape, lambda s, c: (s * chunks + c,) + (0,) * len(shape))


def shaped(shape, kind=jnp.float32):
    return jax.ShapeDtypeStruct(shape, kind)


def packed_specs(chunk, chunks, backward=False):
    def at(width, place):
        whole = rows_spec(chunk, chunks, width, backward)
        return pl.BlockSpec(whole.block_shape, lambda s, c: (whole.index_map(s, c)[0], place))

    return [at(KEYS // 2, 0), at(KEYS // 2, 1), at(VALUES // 2, 1), at(VALUES // 2, 2)]


KEYS, VALUES = HEADS * DK, HEADS * DV
PACKED = KEYS + VALUES
ROOM = pltpu.CompilerParams(vmem_limit_bytes=40 * 1024 * 1024)


def scan_forward(mine, theirs, gates, seqs, chunk):
    rows = gates.shape[0]
    chunks = rows // seqs // chunk
    keyed, valued = rows_spec(chunk, chunks, KEYS), rows_spec(chunk, chunks, VALUES)
    return pl.pallas_call(
        functools.partial(scan_forward_kernel, chunk),
        grid=(seqs, chunks),
        in_specs=packed_specs(chunk, chunks)[:3] * 2 + [keyed],
        out_specs=[
            valued,
            keyed,
            chunk_spec(chunks, (HEADS, chunk, chunk)),
            chunk_spec(chunks, (HEADS, DV, DK)),
            chunk_spec(chunks, (1, KEYS)),
            item_spec((HEADS, DV + 8, DK)),
        ],
        out_shape=[
            shaped((rows, VALUES)),
            shaped((rows, KEYS), jnp.bfloat16),
            shaped((seqs * chunks, HEADS, chunk, chunk), jnp.bfloat16),
            shaped((seqs * chunks, HEADS, DV, DK)),
            shaped((seqs * chunks, 1, KEYS)),
            shaped((seqs, HEADS, DV + 8, DK)),
        ],
        scratch_shapes=[
            pltpu.VMEM((HEADS, DV, DK), jnp.float32),
            pltpu.VMEM((1, KEYS), jnp.float32),
            pltpu.VMEM((HEADS, chunk, chunk), jnp.float32),
        ],
        compiler_params=ROOM,
        name="scan_forward",
    )(mine, mine, mine, theirs, theirs, theirs, gates)


def scan_backward(
    mine, theirs, gates, scores, states, starts, incoming, grad_out, later, outgate_grads, seqs, chunk
):
    rows = gates.shape[0]
    chunks = rows // seqs // chunk
    keyed, valued = rows_spec(chunk, chunks, KEYS, True), rows_spec(chunk, chunks, VALUES, True)
    return pl.pallas_call(
        functools.partial(scan_backward_kernel, chunk),
        grid=(seqs, chunks),
        in_specs=[
            *packed_specs(chunk, chunks, True)[:3] * 2,
            keyed,
            chunk_spec(chunks, (HEADS, chunk, chunk), True),
            chunk_spec(chunks, (HEADS, DV, DK), True),
            chunk_spec(chunks, (1, KEYS), True),
            item_spec((HEADS, DV, DK)),
            valued,
            item_spec((HEADS, DV, DK)),
            *[rows_spec(chunk, chunks, VALUES // 2, True)] * 2,
        ],
        out_specs=[*[rows_spec(chunk, chunks, PACKED, True)] * 2, keyed],
        out_shape=[*[shaped((rows, PACKED), jnp.bfloat16)] * 2, shaped((rows, KEYS))],
        scratch_shapes=[pltpu.VMEM((HEADS, DV, DK), jnp.float32)] + [pltpu.VMEM((chunk, KEYS), jnp.float32)] * 3,
        compiler_params=ROOM,
        name="scan_backward",
    )(
        mine, mine, mine, theirs, theirs, theirs,
        gates, scores, states, starts, incoming, grad_out, later, *outgate_grads,
    )


def mix_forward(local_out, forget, incoming, mine, theirs, gain, seqs, chunk):
    rows = local_out.shape[0]
    chunks = rows // seqs // chunk
    keyed, valued = rows_spec(chunk, chunks, KEYS), rows_spec(chunk, chunks, VALUES)
    whole_gain = pl.BlockSpec((1, DV), lambda s, c: (0, 0))
    return pl.pallas_call(
        mix_forward_kernel,
        grid=(seqs, chunks),
        in_specs=[valued, keyed, item_spec((HEADS, DV, DK)), *packed_specs(chunk, chunks)[3:] * 2, whole_gain],
        out_specs=[valued, valued],
        out_shape=[shaped((rows, VALUES)), shaped((rows, VALUES), jnp.bfloat16)],
        compiler_params=ROOM,
        name="mix_forward",
    )(local_out, forget, incoming, mine, theirs, gain)


def mix_backward(mixed_grad, attended, mine, theirs, gain, forget, seqs, chunk):
    rows = attended.shape[0]
    chunks = rows // seqs // chunk
    keyed, valued = rows_spec(chunk, chunks, KEYS), rows_spec(chunk, chunks, VALUES)
    whole_gain = pl.BlockSpec((1, DV), lambda s, c: (0, 0))
    return pl.pallas_call(
        mix_backward_kernel,
        grid=(seqs, chunks),
        in_specs=[valued, valued, *packed_specs(chunk, chunks)[3:] * 2, whole_gain, keyed],
        out_specs=[
            valued,
            *[rows_spec(chunk, chunks, VALUES // 2)] * 2,
            item_spec((HEADS, DV, DK)),
            item_spec((1, DV)),
        ],
        out_shape=[
            shaped((rows, VALUES)),
            *[shaped((rows, VALUES // 2), jnp.bfloat16)] * 2,
            shaped((seqs, HEADS, DV, DK)),
            shaped((seqs, 1, DV)),
        ],
        compiler_params=ROOM,
        name="mix_backward",
    )(mixed_grad, attended, mine, theirs, gain, forget)


def from_neighbours(summary, step):
    count = lax.axis_size("seq")
    total, factor = None, None
    for distance in range(1, count):
        shift = step * distance
        pairs = [(i, i + shift) for i in range(count) if 0 <= i + shift < count]
        came = lax.ppermute(summary, "seq", pairs)
        state, retain = came[:, :, :DV].astype(jnp.float32), came[:, :, DV : DV + 1].astype(jnp.float32)
        if total is None:
            total, factor = state, retain
        else:
            total, factor = total + factor * state, factor * retain
    return total


def product(left, right):
    return jnp.dot(left, right, preferred_element_type=jnp.float32)


def product_left(left, right):
    return lax.dot_general(
        left, right, (((0,), (0,)), ((), ())), preferred_element_type=jnp.float32
    )


def product_right(left, right):
    return lax.dot_general(
        left, right, (((1,), (1,)), ((), ())), preferred_element_type=jnp.float32
    )


EVERYWHERE = ("z", "core", "seq")


def swapped(array):
    return lax.ppermute(array, "core", [(0, 1), (1, 0)])


def after(array, other):
    def nothing(array_ref, other_ref, out_ref):
        pass

    anywhere = pl.BlockSpec(memory_space=pl.ANY)
    return pl.pallas_call(
        nothing,
        in_specs=[anywhere, anywhere],
        out_specs=anywhere,
        out_shape=shaped(array.shape, array.dtype),
        input_output_aliases={0: 0},
        name="after",
    )(array, other)


def first_core():
    return lax.axis_index("core") == 0


def own_half(array, dim, other=False):
    core = lax.axis_index("core")
    size = array.shape[dim] // 2
    return lax.dynamic_slice_in_dim(array, ((1 - core) if other else core) * size, size, dim)


def joined(mine, theirs, dim):
    return jnp.where(
        first_core(), jnp.concatenate([mine, theirs], dim), jnp.concatenate([theirs, mine], dim)
    )


def halves_of(array):
    half = array.shape[1] // 2
    first = first_core()
    return (
        jnp.where(first, array[:, :half], array[:, half:]),
        jnp.where(first, array[:, half:], array[:, :half]),
    )


def scattered(array):
    return lax.psum_scatter(array, "seq", scatter_dimension=0, tiled=True)


def direct(count):
    return count in (2, 4)


def spread(array):
    count, me = lax.axis_size("seq"), lax.axis_index("seq")
    if not direct(count):
        return lax.all_gather(array, "seq", tiled=True)
    rows = array.shape[0]
    whole = jnp.zeros((count * rows, array.shape[1]), array.dtype)
    whole = lax.dynamic_update_slice_in_dim(whole, array, me * rows, 0)
    for distance in range(1, count):
        came = lax.ppermute(array, "seq", [(i, i ^ distance) for i in range(count)])
        whole = lax.dynamic_update_slice_in_dim(whole, came, (me ^ distance) * rows, 0)
    return whole


def gathered_sum(array, late):
    count, me = lax.axis_size("seq"), lax.axis_index("seq")
    if not direct(count):
        return scattered(array), late
    rows = array.shape[0] // count
    pieces = []
    total = lax.dynamic_slice_in_dim(array, me * rows, rows, 0).astype(jnp.float32)
    for distance in range(1, count):
        piece = lax.dynamic_slice_in_dim(array, (me ^ distance) * rows, rows, 0)
        came = lax.ppermute(piece, "seq", [(i, i ^ distance) for i in range(count)])
        pieces.append(after(came, late))
        total = total + pieces[-1].astype(jnp.float32)
    return low(total), pieces[0]


def local(
    tokens,
    mixer_gain,
    query_weight,
    key_weight,
    value_weight,
    decay_down,
    decay_up,
    decay_bias,
    outgate_weight,
    head_gain,
    output_weight,
    channel_gain,
    gate_weight,
    up_weight,
    down_weight,
    cotangent,
):
    seqs_here, seg_len, width = tokens.shape
    rows_here = seqs_here * seg_len
    count = lax.axis_size("seq")
    ff = gate_weight.shape[1]

    shard_rows = query_weight.shape[0]
    smalls = [mixer_gain, decay_down, decay_up, decay_bias, head_gain, channel_gain]
    flat = jnp.concatenate([small.reshape(-1) for small in smalls])
    flat_size = flat.size
    extra = -(-flat_size // (shard_rows * 128)) * 128
    flat = jnp.pad(flat, (0, shard_rows * extra - flat_size)).reshape(shard_rows, extra)
    mixer_packed = jnp.concatenate(
        [
            own_half(weight, 1)
            for weight in (query_weight, key_weight, value_weight, outgate_weight)
        ]
        + [flat],
        axis=1,
    )
    ffn_packed = jnp.concatenate([own_half(gate_weight, 1), own_half(up_weight, 1)], axis=1)
    mixer_mine = lax.all_gather(mixer_packed, "seq", tiled=True)
    ffn_mine = lax.all_gather(ffn_packed, "seq", tiled=True)
    output_mine = spread(own_half(output_weight, 1))
    mixer_mine = after(after(mixer_mine, output_mine), ffn_packed)
    down_mine = spread(after(own_half(down_weight, 1), mixer_mine))
    mixer_theirs, output_theirs = swapped(mixer_mine), swapped(output_mine)
    mixer_theirs = after(mixer_theirs, output_theirs)
    projection_mine, projection_theirs = mixer_mine[:, :PACKED], mixer_theirs[:, :PACKED]
    small_all = mixer_mine[:, PACKED:].reshape(count, -1)
    pieces, begin = [], 0
    for small in smalls:
        pieces.append(small_all[:, begin : begin + small.size].reshape((count,) + small.shape))
        begin += small.size
    gain_one = pieces[0].reshape(-1).astype(jnp.float32)
    decay_down_all = pieces[1].reshape(width, -1)
    decay_up_f = pieces[2].transpose(1, 0, 2).reshape(decay_up.shape[0], -1).astype(jnp.float32)
    decay_bias_f = pieces[3].reshape(1, -1).astype(jnp.float32)
    head_gain_f = pieces[4].reshape(-1).astype(jnp.float32)
    gain_two = pieces[5].reshape(-1).astype(jnp.float32)
    decay_up_f = jnp.concatenate(halves_of(decay_up_f), 1)
    decay_bias_f = jnp.concatenate(halves_of(decay_bias_f), 1)

    inputs = tokens.reshape(rows_here, width).astype(jnp.float32)

    def first_norm(inputs_in, gain_in):
        return normalize(inputs_in) * gain_in

    normed_one = first_norm(inputs, gain_one).astype(jnp.bfloat16)
    low_rank = product(normed_one, decay_down_all)

    def gate_fn(rank_in, up_in, bias_in):
        return (
            jax.nn.log_sigmoid(jnp.dot(rank_in, up_in, precision=highest_precision) + bias_in)
            / normalizer
        )

    gates = gate_fn(low_rank, decay_up_f, decay_bias_f)
    mine = product(normed_one, projection_mine)
    theirs = product(normed_one, projection_theirs)
    chunk = min(CHUNK, seg_len)
    local_out, forget, scores, states, starts, summary = scan_forward(mine, theirs, gates, seqs_here, chunk)
    incoming_state = after(from_neighbours(low(summary), 1), down_mine)
    attended, mixed = mix_forward(
        local_out, forget, incoming_state, mine, theirs, head_gain_f[None, :], seqs_here, chunk
    )
    mixed = jnp.concatenate(halves_of(mixed), 1)
    resid = inputs + joined(product(mixed, output_mine), product(mixed, output_theirs), 1)
    normed_two = first_norm(resid, gain_two).astype(jnp.bfloat16)
    ffn_mine = after(ffn_mine, normed_two)
    down_theirs = swapped(down_mine)
    ffn_theirs = swapped(ffn_mine)

    def swiglu(both):
        gate_pre, up_pre = both[:, : ff // 2], both[:, ff // 2 :]
        return low(gate_pre * jax.nn.sigmoid(gate_pre) * up_pre)

    both_mine, both_theirs = product(normed_two, ffn_mine), product(normed_two, ffn_theirs)
    hidden = joined(swiglu(both_mine), swiglu(both_theirs), 1)
    result = resid + joined(product(hidden, down_mine), product(hidden, down_theirs), 1)
    block_out = result.astype(jnp.bfloat16).reshape(tokens.shape)

    grad_low = cotangent.reshape(rows_here, width)
    grad_out = grad_low.astype(jnp.float32)
    low_mine, low_theirs = halves_of(grad_low)
    hidden_grad = product_right(low_mine, down_mine) + product_right(low_theirs, down_theirs)

    def swiglu_back(both, grad):
        gate_pre, up_pre = both[:, : ff // 2], both[:, ff // 2 :]
        sigma = jax.nn.sigmoid(gate_pre)
        return jnp.concatenate(
            [
                low(grad * up_pre * (sigma + gate_pre * sigma * (1.0 - sigma))),
                low(grad * (gate_pre * sigma)),
            ],
            axis=1,
        )

    grad_mine, grad_theirs = halves_of(hidden_grad)
    back_mine, back_theirs = swiglu_back(both_mine, grad_mine), swiglu_back(both_theirs, grad_theirs)

    ffn_came = swapped(low(product_left(normed_two, back_theirs)))
    normed_two_grad = product_right(back_mine, ffn_mine) + product_right(back_theirs, ffn_theirs)
    norm_pulled = jax.vjp(first_norm, resid, gain_two)[1](normed_two_grad)
    resid_grad = grad_out + norm_pulled[0]
    channel_gain_grad = norm_pulled[1]
    branch_grad = resid_grad.astype(jnp.bfloat16)
    branch_mine, branch_theirs = halves_of(branch_grad)
    mixed_grad = product_right(branch_mine, output_mine) + product_right(branch_theirs, output_theirs)
    mixed_grad = jnp.concatenate(halves_of(mixed_grad), 1)
    ffn_pair = low(product_left(normed_two, back_mine) + ffn_came.astype(jnp.float32))
    ffn_share = scattered(ffn_pair)
    mixed_grad = after(mixed_grad, ffn_pair)
    attended_grad, *outgate_grads, state_grad, head_gain_grad = mix_backward(
        mixed_grad, attended, mine, theirs, head_gain_f[None, :], forget, seqs_here, chunk
    )
    head_gain_grad = head_gain_grad.sum((0, 1))
    later_grad = from_neighbours(
        jnp.concatenate([state_grad, summary[:, :, DV:]], axis=2).astype(jnp.bfloat16), -1
    )
    output_came = swapped(low(product_left(mixed, after(branch_theirs, attended_grad))))
    output_pair = product_left(mixed, after(branch_mine, attended_grad)) + output_came.astype(jnp.float32)
    output_pair = low(output_pair)
    down_came = swapped(low(product_left(hidden, after(low_theirs, attended_grad))))
    down_pair = low(product_left(hidden, after(low_mine, attended_grad)) + down_came.astype(jnp.float32))
    attended_grad = after(after(attended_grad, output_pair), down_pair)
    packed_mine, packed_theirs, gates_grad = scan_backward(
        mine, theirs, gates, scores, states, starts, incoming_state,
        attended_grad, later_grad, outgate_grads, seqs_here, chunk,
    )
    packed_theirs = after(packed_theirs, ffn_share)
    packed_came = swapped(low(product_left(normed_one, packed_theirs)))
    mixer_pair = low(product_left(normed_one, packed_mine) + packed_came.astype(jnp.float32))
    mixer_share, mixer_first = gathered_sum(mixer_pair, mixer_pair)
    gates_grad = after(gates_grad, mixer_first)
    gate_pulled = jax.vjp(gate_fn, low_rank, decay_up_f, decay_bias_f)[1](gates_grad)
    low_rank_grad = gate_pulled[0].astype(jnp.bfloat16)
    decay_up_grad = jnp.concatenate(halves_of(gate_pulled[1]), 1)
    decay_bias_grad = jnp.concatenate(halves_of(gate_pulled[2]), 1)[0]
    decay_down_grad = product_left(normed_one, low_rank_grad)
    normed_one_grad = (
        product_right(after(packed_mine, mixer_first), projection_mine)
        + product_right(after(packed_theirs, mixer_first), projection_theirs)
        + product_right(low_rank_grad, decay_down_all)
    )
    first_pulled = jax.vjp(first_norm, inputs, gain_one)[1](normed_one_grad)
    tokens_grad = (resid_grad + first_pulled[0]).reshape(tokens.shape)

    def by_shard(grad, dim=0):
        shape = grad.shape[:dim] + (count, grad.shape[dim] // count) + grad.shape[dim + 1 :]
        return jnp.moveaxis(grad.reshape(shape), dim, 0).reshape(count, -1)

    small_grads = jnp.concatenate(
        [
            by_shard(first_pulled[1]),
            by_shard(decay_down_grad),
            by_shard(decay_up_grad, 1),
            by_shard(decay_bias_grad),
            by_shard(head_gain_grad),
            by_shard(channel_gain_grad),
        ],
        axis=1,
    )
    small_rows = -(-flat_size // (width // 2 * 16)) * 16
    small_grads = jnp.pad(low(small_grads), ((0, 0), (0, small_rows * width // 2 - flat_size)))
    rest_pair = jnp.concatenate(
        [
            output_pair.reshape(count, shard_rows, width // 2),
            small_grads.reshape(count, small_rows, width // 2),
        ],
        axis=1,
    ).reshape(-1, width // 2)
    rest_share, _ = gathered_sum(rest_pair, mixer_pair)
    down_share, _ = gathered_sum(after(down_pair, later_grad), tokens_grad)

    ffn_total = after(lax.psum(ffn_share, "z"), rest_share)
    ffn_other = swapped(ffn_total)
    mixer_total, down_total, rest_total = lax.psum(
        tuple(after(share, ffn_total) for share in (mixer_share, down_share, rest_share)), "z"
    )
    mixer_other, down_other, rest_other = (
        swapped(total) for total in (mixer_total, down_total, rest_total)
    )

    def both_cores(total, other, begin, end):
        return joined(total[:, begin:end], other[:, begin:end], 1).astype(jnp.float32)

    summed = rest_total[shard_rows:].astype(jnp.float32) + rest_other[shard_rows:].astype(jnp.float32)
    summed, shares, begin = summed.reshape(-1), [], 0
    for small in smalls:
        shares.append(summed[begin : begin + small.size].reshape(small.shape))
        begin += small.size

    columns = (0, KEYS // 2, KEYS, KEYS + VALUES // 2, PACKED)
    query_g, key_g, value_g, outgate_g = (
        both_cores(mixer_total, mixer_other, a, b) for a, b in zip(columns[:-1], columns[1:])
    )
    return (
        block_out,
        tokens_grad,
        shares[0],
        query_g,
        key_g,
        value_g,
        shares[1],
        shares[2],
        shares[3],
        outgate_g,
        shares[4],
        joined(rest_total[:shard_rows], rest_other[:shard_rows], 1).astype(jnp.float32),
        shares[5],
        both_cores(ffn_total, ffn_other, 0, ff // 2),
        both_cores(ffn_total, ffn_other, ff // 2, ff),
        joined(down_total, down_other, 1).astype(jnp.float32),
    )


def solution(mesh):
    rep, seq = mesh.shape["rep"], mesh.shape["seq"]
    cores = Mesh(mesh.devices.reshape(rep // 2, 2, seq), EVERYWHERE)
    sequences, weights = P(("z", "core"), "seq", None), P("seq", None)
    in_specs = (
        sequences,
        P("seq"),
        weights,
        weights,
        weights,
        weights,
        P(None, "seq"),
        P("seq"),
        weights,
        P("seq"),
        weights,
        P("seq"),
        weights,
        weights,
        weights,
        sequences,
    )
    out_specs = (sequences, *in_specs[:15])
    return jax.shard_map(local, mesh=cores, in_specs=in_specs, out_specs=out_specs, check_vma=False)
```
